128 devices in a mesh: dp: 8 (over y, x_hi), tx: 4 (over z), ty: 4 (over x_lo, core).
Axes of the slice: x: 4 (x_hi: 2, x_lo: 2; x = x_hi * 2 + x_lo), y: 4, z: 4, core: 2. Of those that a mesh axis runs over, the one named last changes fastest.
Arguments:
- tokens: bfloat16 [4096, 8192], P(('dp', 'tx', 'ty')), may hold values from -6 to 6
- mod_shift: bfloat16 [16, 8192], P('dp'), may hold values from -3 to 3
- mod_scale: bfloat16 [16, 8192], P('dp'), may hold values from -2.5 to 2.5
- up_weight: bfloat16 [8192, 16384], P(None, ('tx', 'ty')), may hold values from -0.0625 to 0.0625
- up_bias: bfloat16 [16384], P(('tx', 'ty')), may hold values from -4 to 4
- act_grad: bfloat16 [4096, 16384], P('dp', ('tx', 'ty')), may hold values from -24 to 24
Outputs:
- token_grad: bfloat16 [4096, 8192], P(('dp', 'tx', 'ty'))
- weight_grad: bfloat16 [8192, 16384], P('dp', ('tx', 'ty'))
- bias_grad: float32 [16384], P(('tx', 'ty'))
- shift_grad: float32 [16, 8192], P('dp')
- modulation_scale_gradient: float32 [16, 8192], P('dp')
The draws below stay inside these ranges and needn't reach their ends.
All inputs are finite; a program needn't handle non-finite values.
Results may differ from the reference program's by a relative error of at most 0.029.
Values may be sent and summed in bfloat16 or wider, within the bound.
A program may use at most 256 MiB of HBM per device.

```python
import jax
import jax.numpy as jnp
from jax import lax

MODEL_DIM = 8192
FF = 16384
IMAGE_TOKENS = 256
TOK_DEV = 512
TOKENS = 4096
IMAGE_COUNT = 16
N_DP = 8


def draw_act_grad(key, part):
    key = jax.random.fold_in(key, 7)
    key_noise = jax.random.fold_in(key, 0)
    row_index = jnp.arange(TOKENS) % TOK_DEV
    rising = 1.0 + 2.0 * row_index.astype(jnp.float32) / max(TOK_DEV - 1, 1)
    values = jnp.clip(jax.random.normal(key_noise, (TOKENS, FF), jnp.float32), -5.0, 5.0)
    return jnp.clip(values * rising[:, None], -24.0, 24.0).astype(jnp.bfloat16)


def shard_levels(rng, shape, pieces, low, high):
    def one(dim, parts):
        draws = jax.random.uniform(jax.random.fold_in(jax.random.fold_in(rng, 6), dim), (parts,), jnp.float32, low / len(pieces), high / len(pieces))
        return jnp.repeat(jnp.exp(draws), shape[dim] // parts).reshape((-1,) + (1,) * (len(shape) - dim - 1))

    gain = one(*pieces[0])
    for cut in pieces[1:]:
        gain = gain * one(*cut)
    return gain


def gaussian(stream_key, shape, width, bound, cuts=(), dtype=jnp.bfloat16):
    values = jax.random.normal(stream_key, shape, jnp.float32) * width
    if len(cuts) > 0:
        values = shard_levels(stream_key, shape, cuts, -0.22, 0.18) * values
    return jnp.clip(values, min=-bound, max=bound).astype(dtype)


def setup_inputs(seed: int = 0) -> dict:
    seeds = jax.random.split(jax.random.key(seed), 7)
    return {
        "tokens": gaussian(seeds[0], (TOKENS, MODEL_DIM), 1.0, 6.0, ((0, 128),)),
        "mod_shift": gaussian(seeds[1], (IMAGE_COUNT, MODEL_DIM), 0.5, 3.0, ((0, 8),)),
        "mod_scale": gaussian(seeds[2], (IMAGE_COUNT, MODEL_DIM), 0.4, 2.5, ((0, 8),)),
        "up_weight": gaussian(seeds[3], (MODEL_DIM, FF), MODEL_DIM ** -0.5, 0.0625, ((1, 16),)),
        "up_bias": gaussian(seeds[4], (FF,), 0.7, 4.0, ((0, 16),)),
        "act_grad": draw_act_grad(jax.random.fold_in(seeds[6], 71), 0),
    }


def layer_normalize(tokens):
    values = tokens.astype(jnp.float32)
    average = lax.optimization_barrier(jnp.mean(values, axis=-1, keepdims=True))
    centered = values - average
    spread = lax.optimization_barrier(jnp.mean(centered * centered, axis=-1, keepdims=True))
    inverse_deviation = lax.rsqrt(spread + 1e-06)
    return (centered * inverse_deviation, inverse_deviation)

def activation_grad(preact, act_grad):
    _, pullback = jax.vjp(lambda entries: jax.nn.gelu(entries, approximate=True), preact)
    return pullback(act_grad.astype(jnp.float32))[0]

def reference(tokens, mod_shift, mod_scale, up_weight, up_bias, act_grad):
    standardized_input, inverse_deviation = layer_normalize(tokens)
    scale_per_row = jnp.repeat(mod_scale.astype(jnp.float32), IMAGE_TOKENS, axis=0)
    shift_per_row = jnp.repeat(mod_shift.astype(jnp.float32), IMAGE_TOKENS, axis=0)
    normalized_rows = (standardized_input * (1.0 + scale_per_row) + shift_per_row).astype(jnp.bfloat16)
    preact = jnp.dot(normalized_rows, up_weight, preferred_element_type=jnp.float32) + up_bias.astype(jnp.float32)
    grad_pre = activation_grad(preact, act_grad).astype(jnp.bfloat16)
    weight_total = jnp.zeros((MODEL_DIM, FF), jnp.float32)
    for member in range(N_DP):
        group_rows = normalized_rows[member * TOK_DEV:(member + 1) * TOK_DEV]
        group_grad = grad_pre[member * TOK_DEV:(member + 1) * TOK_DEV]
        partial_term = lax.dot_general(group_rows, group_grad, (((0,), (0,)), ((), ())), preferred_element_type=jnp.float32)
        weight_total = weight_total + lax.optimization_barrier(partial_term.astype(jnp.bfloat16)).astype(jnp.float32)
    bias_grad = lax.optimization_barrier(jnp.sum(grad_pre.astype(jnp.float32), axis=0))
    normalized_gradient = lax.dot_general(grad_pre, up_weight, (((1,), (1,)), ((), ())), preferred_element_type=jnp.float32)
    shift_grad = lax.optimization_barrier(jnp.sum(normalized_gradient.reshape(IMAGE_COUNT, IMAGE_TOKENS, MODEL_DIM), axis=1))
    modulation_scale_gradient = lax.optimization_barrier(jnp.sum((normalized_gradient * standardized_input).reshape(IMAGE_COUNT, IMAGE_TOKENS, MODEL_DIM), axis=1))
    gradient_scaled = normalized_gradient * (1.0 + scale_per_row)
    gradient_centered = gradient_scaled - lax.optimization_barrier(jnp.mean(gradient_scaled, axis=-1, keepdims=True)) - standardized_input * lax.optimization_barrier(jnp.mean(gradient_scaled * standardized_input, axis=-1, keepdims=True))
    token_grad = (inverse_deviation * gradient_centered).astype(jnp.bfloat16)
    return (token_grad, weight_total.astype(jnp.bfloat16), bias_grad, shift_grad, modulation_scale_gradient)
```

```python
import functools

import jax
import jax.numpy as jnp
from jax import lax
from jax.experimental import pallas as pl
from jax.experimental.pallas import tpu as pltpu
from jax.sharding import PartitionSpec as P

MESH = pl.DeviceIdType.MESH
MIB = 1 << 20
F32 = jnp.float32
BF16 = jnp.bfloat16
GELU_A = 0.7978845608028654
GELU_B = 0.044715


def place():
    dp, tx, ty = (lax.axis_index(a) for a in ("dp", "tx", "ty"))
    return dp // 2, dp % 2, tx, ty // 2, ty % 2


def peer(dy=0, dh=0, dz=0, dl=0, dc=0):
    y, h, z, l, c = place()
    return (
        lax.rem(y + dy, 4) * 2 + lax.rem(h + dh, 2),
        lax.rem(z + dz, 4),
        lax.rem(l + dl, 2) * 2 + lax.rem(c + dc, 2),
    )


def greet(peers):
    barrier = pltpu.get_barrier_semaphore()
    for p in peers:
        pl.semaphore_signal(barrier, inc=1, device_id=p, device_id_type=MESH)
    pl.semaphore_wait(barrier, len(peers))


def remote(src, dst, send, recv, to):
    return pltpu.make_async_remote_copy(
        src_ref=src, dst_ref=dst, send_sem=send, recv_sem=recv, device_id=to, device_id_type=MESH
    )


def landed(ref, sem):
    pltpu.make_async_copy(ref, ref, sem).wait()


def cols(i, n):
    return pl.ds(pl.multiple_of(i * n, n), n)


def standardize(tok_ref):
    values = tok_ref[...].astype(F32)
    average = jnp.mean(values, axis=-1, keepdims=True)
    centered = values - average
    spread = jnp.mean(centered * centered, axis=-1, keepdims=True)
    inv = lax.rsqrt(spread + 1e-06)
    return centered * inv, inv


def own_image(ref):
    _, _, z, _, _ = place()
    m = ref[...].astype(F32)
    first = (z < 2).astype(F32)
    return jnp.where(first > 0.5, m[0:1], m[1:2])


def slot(c, z, l):
    return c * 8 + z * 2 + l


def rows(c, z, l):
    return pl.ds(slot(c, z, l) * 32, 32)


PIECES = ((0, 0), (0, 1), (3, 0), (1, 0), (3, 1), (1, 1), (2, 0), (2, 1))


def gather_kernel(
    tok, shift, scale, w_hbm, bias, act, g_out, gt_out, cb,
    n, w, w_sem, n_send, n_recv, c_send, c_recv, f_send, f_recv, o_sem,
):
    y, _, z, l, c = place()
    sib = peer(dc=1)
    pair = peer(dl=1)
    ring = {d: peer(dz=d) for d in (1, 2, 3)}
    group = {d: peer(dy=d) for d in (1, 2, 3)}

    load_w = pltpu.make_async_copy(w_hbm, w, w_sem)
    load_w.start()
    greet([sib, pair, *ring.values(), *group.values()])

    xhat, _ = standardize(tok)
    n[rows(0, 0, 0), :] = (xhat * (1.0 + own_image(scale)) + own_image(shift)).astype(BF16)

    pending = []

    def send(src, dst, to):
        s, d = rows(*src), rows(*dst)
        cp = remote(n.at[s], n.at[d], n_send.at[len(pending)], n_recv.at[slot(*dst)], to)
        cp.start()
        pending.append(cp)

    def exchange(zz, ll):
        p = zz * 2 + ll
        for d in (2, 1, 3):
            block = lax.rem(y + d, 4)
            src = n.at[rows(0, zz, ll), cols(block, 2048)]
            cp = remote(
                src, cb.at[4 - d, rows(0, zz, ll)], c_send.at[d - 1, p], c_recv.at[3 - d, p], group[d]
            )
            cp.start()

    def arrived(*s):
        landed(n.at[rows(*s)], n_recv.at[slot(*s)])

    def block(zz):
        for ll in (0, 1):
            arrived(1, zz, ll)
        a, b = zz * 64, 256 + zz * 64
        at = []
        for cc in (0, 1):
            for ll in (0, 1):
                zr = lax.rem(z + zz, 4)
                at.append((zr * 4 + lax.rem(l + ll, 2) * 2 + lax.rem(c + cc, 2)) * 32)

        @pl.loop(0, 4)
        def _(j):
            t = cols(j, 256)
            x = jnp.concatenate([n[a : a + 64, :], n[b : b + 64, :]], axis=0)
            pre = jnp.dot(x, w[:, t], preferred_element_type=F32) + bias[:, t].astype(F32)
            up = jnp.concatenate([act[pl.ds(pl.multiple_of(r, 32), 32), t] for r in at], axis=0).astype(F32)
            sq = pre * pre
            th = jnp.tanh(GELU_A * pre * (1.0 + GELU_B * sq))
            slope = 0.5 * (1.0 + th) + 0.5 * GELU_A * pre * (1.0 - th * th) * (1.0 + 3.0 * GELU_B * sq)
            grad = (up * slope).astype(BF16)
            g_out[a : a + 64, t] = grad[0:64]
            g_out[b : b + 64, t] = grad[64:128]

    own = (0, 0, 0)
    send(own, (0, 0, 1), pair)
    for d in (1, 3, 2):
        send(own, (0, 4 - d, 0), ring[d])
    send(own, (1, 0, 0), sib)
    exchange(0, 0)

    arrived(0, 0, 1)
    for d in (1, 3, 2):
        send((0, 0, 1), (0, 4 - d, 1), ring[d])
    send((0, 0, 1), (1, 0, 1), sib)
    exchange(0, 1)
    load_w.wait()
    block(0)
    for zz, ll in ((3, 0), (1, 0), (3, 1), (1, 1)):
        arrived(0, zz, ll)
        send((0, zz, ll), (1, zz, ll), sib)
        exchange(zz, ll)
    block(3)
    block(1)
    for ll in (0, 1):
        arrived(0, 2, ll)
        send((0, 2, ll), (1, 2, ll), sib)
        exchange(2, ll)
    block(2)

    keep = pltpu.make_async_copy(n.at[:, cols(y, 2048)], cb.at[0], o_sem)
    keep.start()

    @pl.loop(0, 4)
    def _(j):
        gt_out[cols(j, 256), :] = g_out[:, cols(j, 256)].T

    moved = []
    for zz, ll in PIECES:
        p = zz * 2 + ll
        for s in (1, 2, 3):
            src = cb.at[s, rows(0, zz, ll)]
            landed(src, c_recv.at[s - 1, p])
            cp = remote(src, cb.at[s, rows(1, zz, ll)], f_send.at[s - 1, p], f_recv.at[s - 1, p], sib)
            cp.start()
            moved.append(cp)
    for cp in moved:
        cp.wait()
    for cp in pending:
        cp.wait_send()
    for zz, ll in PIECES:
        for s in (0, 1, 2):
            src = n.at[rows(0, zz, ll), pl.ds(0, 2048)]
            landed(src, c_send.at[s, zz * 2 + ll])
    keep.wait()


NF = 8
ND = 8


def grad_kernel(
    tok, scale, g, gt, cb_hbm, w_hbm, token_grad, weight_grad, bias_grad, shift_grad, scale_grad,
    w, cb, gb, sb, rb, zs, zr, xs, xr, keep, xhat, inv, part, pws, xw, bsum, brec, term, trec,
    w_sem, cb_sem, y_send, y_recv, s_send, s_recv, z_send, z_recv, l_send, l_recv, x_send, x_recv,
    b_send, b_recv, t_send, t_recv,
):
    _, h, z, _, _ = place()
    sib = peer(dc=1)
    pair = peer(dl=1)
    ring = {d: peer(dz=d) for d in (1, 2, 3)}
    group = {d: peer(dy=d) for d in (1, 2, 3)}
    cross = peer(dh=1)
    fc, dc = 1024 // NF, 8192 // ND

    load_w = pltpu.make_async_copy(w_hbm, w, w_sem)
    load_w.start()
    load_cb = pltpu.make_async_copy(cb_hbm, cb, cb_sem)
    load_cb.start()
    greet([sib, pair, *ring.values(), *group.values(), cross])

    def y_copy(d, q):
        return remote(
            gt.at[cols(q, fc)], gb.at[3 - d, cols(q, fc)], y_send.at[d - 1, q], y_recv.at[3 - d, q], group[d]
        )

    @pl.loop(0, NF)
    def _(q):
        for d in (2, 1, 3):
            y_copy(d, q).start()

    xh, iv = standardize(tok)
    xhat[...] = xh
    inv[...] = jnp.broadcast_to(iv, inv.shape)
    load_w.wait()

    def s_copy(j):
        k = lax.rem(j, 2)
        return remote(sb.at[k], rb.at[:, cols(j, dc)], s_send.at[k], s_recv.at[j], sib)

    def z_copy(d, j):
        return remote(
            zs.at[pl.ds(d * 64, 64), cols(j, dc)],
            zr.at[3 - d, :, cols(j, dc)],
            z_send.at[d - 1, j],
            z_recv.at[3 - d, j],
            ring[d],
        )

    def core_sum(j):
        t = cols(j, dc)
        landed(rb.at[:, t], s_recv.at[j])
        zs[:, t] = (zs[:, t].astype(F32) + rb[:, t].astype(F32)).astype(BF16)
        for d in (2, 1, 3):
            z_copy(d, j).start()

    @pl.loop(0, ND)
    def _(j):
        k = lax.rem(j, 2)

        @pl.when(j >= 2)
        def _():
            s_copy(j).wait_send()

        @pl.loop(0, dc // 512)
        def _(i):
            t = pl.ds(pl.multiple_of(j * dc + i * 512, 512), 512)
            p = lax.dot_general(g[...], w[t, :], (((1,), (1,)), ((), ())), preferred_element_type=F32)
            p = p.astype(BF16)
            zs[:, t] = p[0:256]
            sb[k, :, cols(i, 512)] = p[256:512]

        s_copy(j).start()

        @pl.when(j >= 1)
        def _():
            core_sum(j - 1)

    core_sum(ND - 1)
    s_copy(0).wait_send()
    s_copy(1).wait_send()
    load_cb.wait()

    def x_copy(q):
        return remote(pws.at[cols(q, fc)], xw.at[cols(q, fc)], x_send.at[q], x_recv.at[q], cross)

    def l_copy(j):
        return remote(xs.at[:, cols(j, dc)], xr.at[:, cols(j, dc)], l_send.at[j], l_recv.at[j], pair)

    def weight_part(q):
        r = cols(q, fc)
        for s in range(3):
            landed(gb.at[s, r], y_recv.at[s, q])

        def tile(column):
            t = pl.ds(pl.multiple_of(column, 512), 512)
            acc = jnp.dot(gt[r, :], cb[0, :, t], preferred_element_type=F32)
            for s in range(3):
                acc += jnp.dot(gb[s, r, :], cb[s + 1, :, t], preferred_element_type=F32)
            return acc

        @pl.loop(0, 2)
        def _(i):
            pws[r, cols(i, 512)] = tile((1 - h) * 1024 + i * 512).astype(BF16)

        x_copy(q).start()

        @pl.loop(0, 2)
        def _(i):
            part[r, cols(i, 512)] = tile(h * 1024 + i * 512)

        ones = jnp.ones((8, 512), BF16)
        nt = (((1,), (1,)), ((), ()))
        total = lax.dot_general(ones, gt[r, :], nt, preferred_element_type=F32)
        for s in range(3):
            total += lax.dot_general(ones, gb[s, r, :], nt, preferred_element_type=F32)
        bsum[:, r] = total

    def weight_sum(q):
        r = cols(q, fc)
        landed(xw.at[r], x_recv.at[q])
        weight_grad[:, r] = (part[r, :] + xw[r, :].astype(F32)).T.astype(BF16)

    def z_sum(j):
        t = cols(j, dc)
        for s in range(3):
            landed(zr.at[s, :, t], z_recv.at[s, j])
        total = zs[0:64, t].astype(F32)
        for s in range(3):
            total += zr[s, :, t].astype(F32)
        keep[:, t] = total[0:32]
        xs[:, t] = total[32:64].astype(BF16)
        l_copy(j).start()

    def row_sum(j):
        t = cols(j, dc)
        landed(xr.at[:, t], l_recv.at[j])
        own = keep[:, t] + xr[:, t].astype(F32)
        keep[:, t] = own
        term[0, 0:1, t] = jnp.sum(own, axis=0, keepdims=True)
        term[0, 1:2, t] = jnp.sum(own * xhat[:, t], axis=0, keepdims=True)

    @pl.loop(0, NF)
    def _(q):
        weight_part(q)
        z_sum(q)

        @pl.when(q >= 1)
        def _():
            row_sum(q - 1)

        @pl.when(q >= 4)
        def _():
            weight_sum(q - 4)

    b_copy = remote(bsum, brec, b_send.at[0], b_recv.at[0], cross)
    b_copy.start()
    row_sum(ND - 1)

    flip = lax.rem(z, 2)
    near = (peer()[0], z + 1 - 2 * flip, peer()[2])

    def t_copy(k, to):
        return remote(term.at[k], trec.at[k], t_send.at[k], t_recv.at[k], to)

    partners = (sib, pair, near, ring[2])
    hops = [t_copy(k, to) for k, to in enumerate(partners)]
    hops[0].start()

    grown = 1.0 + own_image(scale)
    scaled = keep[...] * grown
    mean_one = jnp.mean(scaled, axis=-1, keepdims=True)
    mean_two = jnp.mean(scaled * xhat[...], axis=-1, keepdims=True)
    token_grad[...] = (inv[:, 0:1] * (scaled - mean_one - xhat[...] * mean_two)).astype(BF16)

    for k in range(3):
        hops[k].wait_recv()
        term[k + 1] = term[k] + trec[k]
        hops[k + 1].start()
        weight_sum(NF - 4 + k)
    b_copy.wait()
    bias_grad[...] = bsum[...] + brec[...]
    hops[3].wait_recv()
    first = (z < 2).astype(F32) > 0.5
    mine, other = term[3], trec[3]
    shift_grad[0:1, :] = jnp.where(first, mine[0:1], other[0:1])
    shift_grad[1:2, :] = jnp.where(first, other[0:1], mine[0:1])
    scale_grad[0:1, :] = jnp.where(first, mine[1:2], other[1:2])
    scale_grad[1:2, :] = jnp.where(first, other[1:2], mine[1:2])
    weight_sum(NF - 1)

    for k in range(4):
        hops[k].wait_send()

    @pl.loop(0, NF)
    def _(q):
        for d in (1, 2, 3):
            y_copy(d, q).wait_send()
            z_copy(d, q).wait_send()
        l_copy(q).wait_send()
        x_copy(q).wait_send()


def local(tokens, mod_shift, mod_scale, up_weight, up_bias, act_grad):
    vmem = pl.BlockSpec(memory_space=pltpu.VMEM)
    hbm = pl.BlockSpec(memory_space=pltpu.HBM)
    dma = pltpu.SemaphoreType.DMA
    g, gt, cb = pl.pallas_call(
        gather_kernel,
        out_shape=(
            jax.ShapeDtypeStruct((512, 1024), BF16),
            jax.ShapeDtypeStruct((1024, 512), BF16),
            jax.ShapeDtypeStruct((4, 512, 2048), BF16),
        ),
        in_specs=[vmem, vmem, vmem, hbm, vmem, vmem],
        out_specs=(vmem, vmem, hbm),
        scratch_shapes=[
            pltpu.VMEM((512, 8192), BF16),
            pltpu.VMEM((8192, 1024), BF16),
            dma(()),
            dma((15,)),
            dma((16,)),
            dma((3, 8)),
            dma((3, 8)),
            dma((3, 8)),
            dma((3, 8)),
            dma(()),
        ],
        compiler_params=pltpu.CompilerParams(
            collective_id=0, has_side_effects=True, vmem_limit_bytes=48 * MIB
        ),
        name="gather_up",
    )(tokens, mod_shift, mod_scale, up_weight, up_bias[None, :], act_grad)
    token_grad, weight_grad, bias_grad, shift_grad, scale_grad = pl.pallas_call(
        grad_kernel,
        out_shape=(
            jax.ShapeDtypeStruct((32, 8192), BF16),
            jax.ShapeDtypeStruct((1024, 1024), BF16),
            jax.ShapeDtypeStruct((8, 1024), F32),
            jax.ShapeDtypeStruct((2, 8192), F32),
            jax.ShapeDtypeStruct((2, 8192), F32),
        ),
        in_specs=[vmem, vmem, vmem, vmem, hbm, hbm],
        out_specs=(vmem,) * 5,
        scratch_shapes=[
            pltpu.VMEM((8192, 1024), BF16),
            pltpu.VMEM((4, 512, 2048), BF16),
            pltpu.VMEM((3, 1024, 512), BF16),
            pltpu.VMEM((2, 256, 8192 // ND), BF16),
            pltpu.VMEM((256, 8192), BF16),
            pltpu.VMEM((256, 8192), BF16),
            pltpu.VMEM((3, 64, 8192), BF16),
            pltpu.VMEM((32, 8192), BF16),
            pltpu.VMEM((32, 8192), BF16),
            pltpu.VMEM((32, 8192), F32),
            pltpu.VMEM((32, 8192), F32),
            pltpu.VMEM((32, 128), F32),
            pltpu.VMEM((1024, 1024), F32),
            pltpu.VMEM((1024, 1024), BF16),
            pltpu.VMEM((1024, 1024), BF16),
            pltpu.VMEM((8, 1024), F32),
            pltpu.VMEM((8, 1024), F32),
            pltpu.VMEM((4, 2, 8192), F32),
            pltpu.VMEM((4, 2, 8192), F32),
            dma(()),
            dma(()),
            dma((3, NF)),
            dma((3, NF)),
            dma((2,)),
            dma((ND,)),
            dma((3, ND)),
            dma((3, ND)),
            dma((ND,)),
            dma((ND,)),
            dma((NF,)),
            dma((NF,)),
            dma((1,)),
            dma((1,)),
            dma((4,)),
            dma((4,)),
        ],
        compiler_params=pltpu.CompilerParams(
            collective_id=1, has_side_effects=True, vmem_limit_bytes=60 * MIB
        ),
        name="grads",
    )(tokens, mod_scale, g, gt, cb, up_weight)
    return token_grad, weight_grad, bias_grad[0], shift_grad, scale_grad


def solution(mesh):
    return jax.shard_map(
        local,
        mesh=mesh,
        in_specs=(
            P(("dp", "tx", "ty"), None),
            P("dp", None),
            P("dp", None),
            P(None, ("tx", "ty")),
            P(("tx", "ty")),
            P("dp", ("tx", "ty")),
        ),
        out_specs=(
            P(("dp", "tx", "ty"), None),
            P("dp", ("tx", "ty")),
            P(("tx", "ty")),
            P("dp", None),
            P("dp", None),
        ),
        check_vma=False,
    )
```

```python
import jax
import jax.numpy as jnp
from jax import lax
from jax.experimental import pallas as pl
from jax.experimental.pallas import tpu as pltpu
from jax.sharding import PartitionSpec as P

MESH = pl.DeviceIdType.MESH
MIB = 1 << 20
F32 = jnp.float32
BF16 = jnp.bfloat16
GELU_A = 0.7978845608028654
GELU_B = 0.044715


def place():
    dp, tx, ty = (lax.axis_index(a) for a in ("dp", "tx", "ty"))
    return dp // 2, dp % 2, tx, ty // 2, ty % 2


def peer(dy=0, dh=0, dz=0, dl=0, dc=0):
    y, h, z, l, c = place()
    return (
        lax.rem(y + dy, 4) * 2 + lax.rem(h + dh, 2),
        lax.rem(z + dz, 4),
        lax.rem(l + dl, 2) * 2 + lax.rem(c + dc, 2),
    )


def remote(src, dst, send, recv, to):
    return pltpu.make_async_remote_copy(
        src_ref=src, dst_ref=dst, send_sem=send, recv_sem=recv, device_id=to, device_id_type=MESH
    )


def landed(ref, sem):
    pltpu.make_async_copy(ref, ref, sem).wait()


def cols(i, n):
    return pl.ds(pl.multiple_of(i * n, n), n)


def standardize(tok_ref):
    values = tok_ref[...].astype(F32)
    average = jnp.mean(values, axis=-1, keepdims=True)
    centered = values - average
    spread = jnp.mean(centered * centered, axis=-1, keepdims=True)
    inv = lax.rsqrt(spread + 1e-06)
    return centered * inv, inv


def own_image(ref):
    _, _, z, _, _ = place()
    m = ref[...].astype(F32)
    first = (z < 2).astype(F32)
    return jnp.where(first > 0.5, m[0:1], m[1:2])


def slot(c, z, l):
    return c * 8 + z * 2 + l


def rows(c, z, l):
    return pl.ds(slot(c, z, l) * 32, 32)


PIECES = ((0, 0), (0, 1), (3, 0), (1, 0), (3, 1), (1, 1), (2, 0), (2, 1))
NF = 8
ND = 8
EARLY = 6


def block_kernel(
    tok_hbm, shift_hbm, scale_hbm, w_hbm, bias_hbm, act_hbm,
    token_grad, weight_grad, bias_grad, shift_grad, scale_grad,
    tok, shift, scale, bias, act, n, cb, w, g, gt, gb, sb, share, zs, zr, xs, xr, keep, xhat, inv,
    xw, bsum, brec, term, trec,
    in_sem, n_send, n_recv, c_send, c_recv, f_send, f_recv,
    y_send, y_recv, s_send, s_recv, z_send, z_recv, l_send, l_recv, x_send, x_recv,
    b_send, b_recv, t_send, t_recv,
):
    y, h, z, l, c = place()
    sib = peer(dc=1)
    pair = peer(dl=1)
    ring = {d: peer(dz=d) for d in (1, 2, 3)}
    group = {d: peer(dy=d) for d in (1, 2, 3)}
    cross = peer(dh=1)
    fc, dc = 1024 // NF, 8192 // ND

    loads = [
        pltpu.make_async_copy(src, dst, in_sem.at[k])
        for k, (src, dst) in enumerate(
            ((tok_hbm, tok), (shift_hbm, shift), (scale_hbm, scale), (bias_hbm, bias), (act_hbm, act), (w_hbm, w))
        )
    ]
    for cp in loads:
        cp.start()
    peers = [sib, pair, *ring.values(), *group.values(), cross]
    barrier = pltpu.get_barrier_semaphore()
    for p in peers:
        pl.semaphore_signal(barrier, inc=1, device_id=p, device_id_type=MESH)
    for cp in loads[:3]:
        cp.wait()
    xh, iv = standardize(tok)
    xhat[...] = xh
    inv[...] = jnp.broadcast_to(iv, inv.shape)
    n[rows(0, 0, 0), :] = (xh * (1.0 + own_image(scale)) + own_image(shift)).astype(BF16)
    pl.semaphore_wait(barrier, len(peers))

    pending = []

    def send(src, dst, to, half=None):
        s, d, sem = rows(*src), rows(*dst), slot(*dst)
        if half is not None:
            s = pl.ds(slot(*src) * 32 + half * 16, 16)
            d = pl.ds(slot(*dst) * 32 + half * 16, 16)
            sem = sem if half == 0 else 16 + dst[2]
        cp = remote(n.at[s], n.at[d], n_send.at[len(pending)], n_recv.at[sem], to)
        cp.start()
        pending.append(cp)

    def exchange(zz, ll):
        p = zz * 2 + ll
        for d in (2, 1, 3):
            block = lax.rem(y + d, 4)
            src = n.at[rows(0, zz, ll), cols(block, 2048)]
            cp = remote(
                src, cb.at[3 - d, rows(0, zz, ll)], c_send.at[d - 1, p], c_recv.at[3 - d, p], group[d]
            )
            cp.start()

    def arrived(*s):
        landed(n.at[rows(*s)], n_recv.at[slot(*s)])

    def block(zz):
        for ll in (0, 1):
            arrived(1, zz, ll)
        a, b = zz * 64, 256 + zz * 64
        at = []
        for cc in (0, 1):
            for ll in (0, 1):
                zr_ = lax.rem(z + zz, 4)
                at.append((zr_ * 4 + lax.rem(l + ll, 2) * 2 + lax.rem(c + cc, 2)) * 32)

        @pl.loop(0, 4)
        def _(j):
            t = cols(j, 256)
            x = jnp.concatenate([n[a : a + 64, :], n[b : b + 64, :]], axis=0)
            pre = jnp.dot(x, w[:, t], preferred_element_type=F32) + bias[:, t].astype(F32)
            up = jnp.concatenate([act[pl.ds(pl.multiple_of(r, 32), 32), t] for r in at], axis=0).astype(F32)
            sq = pre * pre
            th = jnp.tanh(GELU_A * pre * (1.0 + GELU_B * sq))
            slope = 0.5 * (1.0 + th) + 0.5 * GELU_A * pre * (1.0 - th * th) * (1.0 + 3.0 * GELU_B * sq)
            grad = (up * slope).astype(BF16)
            g[a : a + 64, t] = grad[0:64]
            g[b : b + 64, t] = grad[64:128]

    own = (0, 0, 0)
    send(own, (0, 0, 1), pair)
    send(own, (0, 3, 0), ring[1])
    send(own, (0, 1, 0), ring[3])
    send(own, (1, 0, 0), sib)
    exchange(0, 0)

    arrived(0, 0, 1)
    send((0, 0, 1), (0, 3, 1), ring[1])
    send((0, 0, 1), (0, 1, 1), ring[3])
    send((0, 0, 1), (1, 0, 1), sib)
    exchange(0, 1)
    for cp in loads[3:]:
        cp.wait()
    block(0)
    for ll in (0, 1):
        arrived(0, 3, ll)
        send((0, 3, ll), (0, 2, ll), ring[1], half=0)
        arrived(0, 1, ll)
        send((0, 1, ll), (0, 2, ll), ring[3], half=1)
        for zz in (3, 1):
            send((0, zz, ll), (1, zz, ll), sib)
            exchange(zz, ll)
    block(3)
    block(1)
    for ll in (0, 1):
        for half, sem in ((0, slot(0, 2, ll)), (1, 16 + ll)):
            landed(n.at[pl.ds(slot(0, 2, ll) * 32 + half * 16, 16)], n_recv.at[sem])
        send((0, 2, ll), (1, 2, ll), sib)
        exchange(2, ll)
    block(2)

    @pl.loop(0, 4)
    def _(j):
        gt[cols(j, 256), :] = g[:, cols(j, 256)].T

    def y_copy(d, q):
        return remote(
            gt.at[cols(q, fc)], gb.at[3 - d, cols(q, fc)], y_send.at[d - 1, q], y_recv.at[3 - d, q], group[d]
        )

    def y_start(q):
        for d in (2, 1, 3):
            y_copy(d, q).start()

    y_start(0)
    y_start(1)

    moved = []

    def pass_on(pieces):
        for zz, ll in pieces:
            p = zz * 2 + ll
            for s in range(3):
                src = cb.at[s, rows(0, zz, ll)]
                landed(src, c_recv.at[s, p])
                cp = remote(src, cb.at[s, rows(1, zz, ll)], f_send.at[s, p], f_recv.at[s, p], sib)
                cp.start()
                moved.append(cp)

    pass_on(PIECES[:6])

    def s_copy(j):
        k = lax.rem(j, 2)
        return remote(sb.at[k], share.at[pl.ds(2 * j, 2)], s_send.at[k], s_recv.at[j], sib)

    def z_copy(d, j):
        return remote(
            zs.at[pl.ds(d * 64, 64), cols(j, dc)],
            zr.at[3 - d, :, cols(j, dc)],
            z_send.at[d - 1, j],
            z_recv.at[3 - d, j],
            ring[d],
        )

    def core_sum(j):
        t = cols(j, dc)
        landed(share.at[pl.ds(2 * j, 2)], s_recv.at[j])
        theirs = share[pl.ds(2 * j, 2)].reshape(256, dc).astype(F32)
        zs[:, t] = (zs[:, t].astype(F32) + theirs).astype(BF16)
        for d in (2, 1, 3):
            z_copy(d, j).start()

    def normed_part(j):
        k = lax.rem(j, 2)

        @pl.when(j >= 2)
        def _():
            s_copy(j).wait_send()

        @pl.loop(0, dc // 512)
        def _(i):
            t = pl.ds(pl.multiple_of(j * dc + i * 512, 512), 512)
            p = lax.dot_general(g[...], w[t, :], (((1,), (1,)), ((), ())), preferred_element_type=F32)
            p = p.astype(BF16)
            zs[:, t] = p[0:256]
            sb[k, 0, :, cols(i, 512)] = p[256:384]
            sb[k, 1, :, cols(i, 512)] = p[384:512]

        s_copy(j).start()

        @pl.when(j >= 1)
        def _():
            core_sum(j - 1)

    pl.loop(0, EARLY)(normed_part)

    pass_on(PIECES[6:])
    pl.loop(2, NF)(y_start)

    pl.loop(EARLY, ND)(normed_part)
    core_sum(ND - 1)
    s_copy(0).wait_send()
    s_copy(1).wait_send()
    for cp in moved:
        cp.wait()

    def x_copy(q):
        return remote(share.at[q], xw.at[q], x_send.at[q], x_recv.at[q], cross)

    def l_copy(j):
        return remote(xs.at[:, cols(j, dc)], xr.at[:, cols(j, dc)], l_send.at[j], l_recv.at[j], pair)

    def weight_part(q):
        r = cols(q, fc)
        for s in range(3):
            landed(gb.at[s, r], y_recv.at[s, q])

        def tile(column):
            t = pl.ds(pl.multiple_of(column, 512), 512)
            own_t = pl.ds(pl.multiple_of(y * 2048 + column, 512), 512)
            acc = jnp.dot(gt[r, :], n[:, own_t], preferred_element_type=F32)
            for s in range(3):
                acc += jnp.dot(gb[s, r, :], cb[s, :, t], preferred_element_type=F32)
            return acc.astype(BF16)

        @pl.loop(0, 2)
        def _(i):
            share[q, :, cols(i, 512)] = tile((1 - h) * 1024 + i * 512)

        x_copy(q).start()

        @pl.loop(0, 2)
        def _(i):
            share[NF + q, :, cols(i, 512)] = tile(h * 1024 + i * 512)

        ones = jnp.ones((8, 512), BF16)
        nt = (((1,), (1,)), ((), ()))
        total = lax.dot_general(ones, gt[r, :], nt, preferred_element_type=F32)
        for s in range(3):
            total += lax.dot_general(ones, gb[s, r, :], nt, preferred_element_type=F32)
        bsum[:, r] = total

    def weight_sum(q):
        r = cols(q, fc)
        landed(xw.at[q], x_recv.at[q])
        weight_grad[:, r] = (share[NF + q].astype(F32) + xw[q].astype(F32)).T.astype(BF16)

    def z_sum(j):
        t = cols(j, dc)
        for s in range(3):
            landed(zr.at[s, :, t], z_recv.at[s, j])
        total = zs[0:64, t].astype(F32)
        for s in range(3):
            total += zr[s, :, t].astype(F32)
        keep[:, t] = total[0:32]
        xs[:, t] = total[32:64].astype(BF16)
        l_copy(j).start()

    def row_sum(j):
        t = cols(j, dc)
        landed(xr.at[:, t], l_recv.at[j])
        mine = keep[:, t] + xr[:, t].astype(F32)
        keep[:, t] = mine
        term[0, 0:1, t] = jnp.sum(mine, axis=0, keepdims=True)
        term[0, 1:2, t] = jnp.sum(mine * xhat[:, t], axis=0, keepdims=True)

    @pl.loop(0, NF)
    def _(q):
        weight_part(q)
        z_sum(q)

        @pl.when(q >= 1)
        def _():
            row_sum(q - 1)

        @pl.when(q >= 4)
        def _():
            weight_sum(q - 4)

    b_copy = remote(bsum, brec, b_send.at[0], b_recv.at[0], cross)
    b_copy.start()
    row_sum(ND - 1)

    near = (peer()[0], z + 1 - 2 * lax.rem(z, 2), peer()[2])
    hops = [
        remote(term.at[k], trec.at[k], t_send.at[k], t_recv.at[k], to)
        for k, to in enumerate((sib, pair, near, ring[2]))
    ]
    hops[0].start()

    scaled = keep[...] * (1.0 + own_image(scale))
    mean_one = jnp.mean(scaled, axis=-1, keepdims=True)
    mean_two = jnp.mean(scaled * xhat[...], axis=-1, keepdims=True)
    token_grad[...] = (inv[:, 0:1] * (scaled - mean_one - xhat[...] * mean_two)).astype(BF16)

    for k in range(3):
        hops[k].wait_recv()
        term[k + 1] = term[k] + trec[k]
        hops[k + 1].start()
        weight_sum(NF - 4 + k)
    b_copy.wait()
    bias_grad[...] = bsum[...] + brec[...]
    hops[3].wait_recv()
    first = (z < 2).astype(F32) > 0.5
    mine, other = term[3], trec[3]
    shift_grad[0:1, :] = jnp.where(first, mine[0:1], other[0:1])
    shift_grad[1:2, :] = jnp.where(first, other[0:1], mine[0:1])
    scale_grad[0:1, :] = jnp.where(first, mine[1:2], other[1:2])
    scale_grad[1:2, :] = jnp.where(first, other[1:2], mine[1:2])
    weight_sum(NF - 1)

    for k in range(4):
        hops[k].wait_send()
    for cp in pending:
        cp.wait_send()
    for zz, ll in PIECES:
        for s in range(3):
            landed(n.at[rows(0, zz, ll), pl.ds(0, 2048)], c_send.at[s, zz * 2 + ll])

    @pl.loop(0, NF)
    def _(q):
        for d in (1, 2, 3):
            y_copy(d, q).wait_send()
            z_copy(d, q).wait_send()
        l_copy(q).wait_send()
        x_copy(q).wait_send()


def result_kernel(a, b, c, d, e, ao, bo, co, do, eo, av, bv, cv, dv, ev, sem):
    held = (av, bv, cv, dv, ev)
    takes = [pltpu.make_async_copy(src, v, sem.at[k]) for k, (src, v) in enumerate(zip((a, b, c, d, e), held))]
    gives = [
        pltpu.make_async_copy(v, dst, sem.at[5 + k])
        for k, (v, dst) in enumerate(zip((av, bv, cv.at[0:1], dv, ev), (ao, bo, co, do, eo)))
    ]
    for cp in takes:
        cp.start()
    for cp, give in zip(takes, gives):
        cp.wait()
        give.start()
    for give in gives:
        give.wait()


def local(tokens, mod_shift, mod_scale, up_weight, up_bias, act_grad):
    vmem = pl.BlockSpec(memory_space=pltpu.VMEM)
    hbm = pl.BlockSpec(memory_space=pltpu.HBM)
    dma = pltpu.SemaphoreType.DMA
    results = (
        jax.ShapeDtypeStruct((32, 8192), BF16),
        jax.ShapeDtypeStruct((1024, 1024), BF16),
        jax.ShapeDtypeStruct((8, 1024), F32),
        jax.ShapeDtypeStruct((2, 8192), F32),
        jax.ShapeDtypeStruct((2, 8192), F32),
    )
    parts = pl.pallas_call(
        block_kernel,
        out_shape=results,
        in_specs=[hbm] * 6,
        out_specs=(vmem,) * 5,
        scratch_shapes=[
            pltpu.VMEM((32, 8192), BF16),
            pltpu.VMEM((2, 8192), BF16),
            pltpu.VMEM((2, 8192), BF16),
            pltpu.VMEM((1, 1024), BF16),
            pltpu.VMEM((512, 1024), BF16),
            pltpu.VMEM((512, 8192), BF16),
            pltpu.VMEM((3, 512, 2048), BF16),
            pltpu.VMEM((8192, 1024), BF16),
            pltpu.VMEM((512, 1024), BF16),
            pltpu.VMEM((1024, 512), BF16),
            pltpu.VMEM((3, 1024, 512), BF16),
            pltpu.VMEM((2, 2, 128, 1024), BF16),
            pltpu.VMEM((16, 128, 1024), BF16),
            pltpu.VMEM((256, 8192), BF16),
            pltpu.VMEM((3, 64, 8192), BF16),
            pltpu.VMEM((32, 8192), BF16),
            pltpu.VMEM((32, 8192), BF16),
            pltpu.VMEM((32, 8192), F32),
            pltpu.VMEM((32, 8192), F32),
            pltpu.VMEM((32, 128), F32),
            pltpu.VMEM((NF, 128, 1024), BF16),
            pltpu.VMEM((8, 1024), F32),
            pltpu.VMEM((8, 1024), F32),
            pltpu.VMEM((4, 2, 8192), F32),
            pltpu.VMEM((4, 2, 8192), F32),
            dma((6,)),
            dma((17,)),
            dma((18,)),
            dma((3, 8)),
            dma((3, 8)),
            dma((3, 8)),
            dma((3, 8)),
            dma((3, NF)),
            dma((3, NF)),
            dma((2,)),
            dma((ND,)),
            dma((3, ND)),
            dma((3, ND)),
            dma((ND,)),
            dma((ND,)),
            dma((NF,)),
            dma((NF,)),
            dma((1,)),
            dma((1,)),
            dma((4,)),
            dma((4,)),
        ],
        compiler_params=pltpu.CompilerParams(
            collective_id=0, has_side_effects=True, vmem_limit_bytes=61 * MIB
        ),
        name="block",
    )(tokens, mod_shift, mod_scale, up_weight, up_bias[None, :], act_grad)
    final = list(results)
    final[2] = jax.ShapeDtypeStruct((1, 1024), F32)
    token_grad, weight_grad, bias_grad, shift_grad, scale_grad = pl.pallas_call(
        result_kernel,
        out_shape=tuple(final),
        in_specs=[hbm] * 5,
        out_specs=(hbm,) * 5,
        scratch_shapes=[pltpu.VMEM(r.shape, r.dtype) for r in results] + [dma((10,))],
        compiler_params=pltpu.CompilerParams(vmem_limit_bytes=61 * MIB),
        name="results",
    )(*parts)
    return token_grad, weight_grad, bias_grad.reshape(1024), shift_grad, scale_grad


def solution(mesh):
    return jax.shard_map(
        local,
        mesh=mesh,
        in_specs=(
            P(("dp", "tx", "ty"), None),
            P("dp", None),
            P("dp", None),
            P(None, ("tx", "ty")),
            P(("tx", "ty")),
            P("dp", ("tx", "ty")),
        ),
        out_specs=(
            P(("dp", "tx", "ty"), None),
            P("dp", ("tx", "ty")),
            P(("tx", "ty")),
            P("dp", None),
            P("dp", None),
        ),
        check_vma=False,
    )
```

```python
import jax
import jax.numpy as jnp
from jax import lax
from jax.experimental import pallas as pl
from jax.experimental.pallas import tpu as pltpu
from jax.sharding import PartitionSpec as P

MESH = pl.DeviceIdType.MESH
MIB = 1 << 20
F32 = jnp.float32
BF16 = jnp.bfloat16
GELU_A = 0.7978845608028654
GELU_B = 0.044715


def place():
    dp, tx, ty = (lax.axis_index(a) for a in ("dp", "tx", "ty"))
    return dp // 2, dp % 2, tx, ty // 2, ty % 2


def peer(dy=0, dh=0, dz=0, dl=0, dc=0):
    y, h, z, l, c = place()
    return (
        lax.rem(y + dy, 4) * 2 + lax.rem(h + dh, 2),
        lax.rem(z + dz, 4),
        lax.rem(l + dl, 2) * 2 + lax.rem(c + dc, 2),
    )


def remote(src, dst, send, recv, to):
    return pltpu.make_async_remote_copy(
        src_ref=src, dst_ref=dst, send_sem=send, recv_sem=recv, device_id=to, device_id_type=MESH
    )


def landed(ref, sem):
    pltpu.make_async_copy(ref, ref, sem).wait()


def cols(i, n):
    return pl.ds(pl.multiple_of(i * n, n), n)


def wide(x):
    return jnp.broadcast_to(x, (32, 128))


def slot(c, z, l):
    return c * 8 + z * 2 + l


def rows(c, z, l):
    return pl.ds(slot(c, z, l) * 32, 32)


SOON = ((0, 0), (0, 1), (3, 0), (1, 0))
LATE = ((3, 1), (1, 1), (2, 0), (2, 1))
NF = 8
ND = 8
AHEAD = 3


def block_kernel(
    tok_hbm, shift_hbm, scale_hbm, w_hbm, bias_hbm, act_hbm,
    token_hbm, weight_hbm, sums_hbm, shift_out, scale_out,
    tok, shift, scale, bias, n, cb, w, g, gt, sb, share, pw, zs, zr, xs, xr, keep, stats,
    xw, bsum, brec, term, trec, token_grad, weight_grad, shift_grad, scale_grad,
    in_sem, out_sem, wo_sem, own_sem, n_send, n_recv, c_send, c_recv, f_send, f_recv,
    y_send, y_recv, s_send, s_recv, z_send, z_recv, l_send, l_recv, x_send, x_recv,
    b_send, b_recv, t_send, t_recv,
):
    y, h, z, l, c = place()
    sib = peer(dc=1)
    pair = peer(dl=1)
    ring = {d: peer(dz=d) for d in (1, 2, 3)}
    group = {d: peer(dy=d) for d in (1, 2, 3)}
    cross = peer(dh=1)
    fc, dc = 1024 // NF, 8192 // ND

    loads = [
        pltpu.make_async_copy(src, dst, in_sem.at[k])
        for k, (src, dst) in enumerate(
            ((tok_hbm, tok), (shift_hbm, shift), (scale_hbm, scale), (bias_hbm, bias), (w_hbm, w))
        )
    ]
    for cc in (0, 1):
        for zz in range(4):
            for ll in (0, 1):
                r = (lax.rem(z + zz, 4) * 4 + lax.rem(l + ll, 2) * 2 + lax.rem(c + cc, 2)) * 32
                src = act_hbm.at[pl.ds(pl.multiple_of(r, 32), 32)]
                loads.append(pltpu.make_async_copy(src, g.at[rows(cc, zz, ll)], in_sem.at[len(loads)]))
    for cp in loads:
        cp.start()
    peers = [sib, pair, *ring.values(), *group.values(), cross]
    barrier = pltpu.get_barrier_semaphore()
    for p in peers:
        pl.semaphore_signal(barrier, inc=1, device_id=p, device_id_type=MESH)
    for cp in loads[:3]:
        cp.wait()

    def of_image(ref, t):
        m = ref[:, t].astype(F32)
        return jnp.where((z < 2).astype(F32) > 0.5, m[0:1], m[1:2])

    def row_total(f):
        def body(j, acc):
            return acc + jnp.sum(f(tok[:, cols(j, dc)].astype(F32)), axis=-1, keepdims=True)

        return lax.fori_loop(0, ND, body, jnp.zeros((32, 1), F32)) * (1.0 / 8192)

    average = row_total(lambda v: v)
    inverse = lax.rsqrt(row_total(lambda v: (v - average) * (v - average)) + 1e-06)
    stats[0] = wide(average)
    stats[1] = wide(inverse)
    stats[2] = jnp.zeros((32, 128), F32)
    stats[3] = jnp.zeros((32, 128), F32)

    def xhat(t):
        return (tok[:, t].astype(F32) - stats[0, :, 0:1]) * stats[1, :, 0:1]

    @pl.loop(0, ND)
    def _(j):
        t = cols(j, dc)
        n[rows(0, 0, 0), t] = (xhat(t) * (1.0 + of_image(scale, t)) + of_image(shift, t)).astype(BF16)

    pl.semaphore_wait(barrier, len(peers))

    pending = []

    def send(src, dst, to, half=None):
        s, d, sem = rows(*src), rows(*dst), slot(*dst)
        if half is not None:
            s = pl.ds(slot(*src) * 32 + half * 16, 16)
            d = pl.ds(slot(*dst) * 32 + half * 16, 16)
            sem = sem if half == 0 else 16 + dst[2]
        cp = remote(n.at[s], n.at[d], n_send.at[len(pending)], n_recv.at[sem], to)
        cp.start()
        pending.append(cp)

    def span(piece, part):
        k = piece[0] * 2 + piece[1]
        if part == "whole":
            return 0, 2048, k
        if part == "first":
            return (1 - h) * 1024, 1024, k
        return h * 1024, 1024, 8 + LATE.index(piece)

    def place_of(s, cc, piece, part):
        start, width, _ = span(piece, part)
        r = pl.ds(s * 512 + slot(cc, *piece) * 32, 32)
        return cb.at[r, pl.ds(pl.multiple_of(start, 1024), width)]

    def columns_copy(d, piece, part):
        start, width, k = span(piece, part)
        start = lax.rem(y + d, 4) * 2048 + start
        src = n.at[rows(0, *piece), pl.ds(pl.multiple_of(start, 1024), width)]
        dst = place_of(4 - d, 0, piece, part)
        return remote(src, dst, c_send.at[d - 1, k], c_recv.at[3 - d, k], group[d])

    sent = []

    def exchange(piece, part):
        for d in (2, 1, 3):
            cp = columns_copy(d, piece, part)
            cp.start()
            sent.append(cp)

    moved = []

    def pass_on(pieces, part):
        now = []
        for piece in pieces:
            k = span(piece, part)[2]
            for s in (1, 2, 3):
                src = place_of(s, 0, piece, part)
                landed(src, c_recv.at[s - 1, k])
                cp = remote(
                    src, place_of(s, 1, piece, part), f_send.at[s - 1, k], f_recv.at[s - 1, k], sib
                )
                cp.start()
                now.append(cp)
        moved.extend(now)
        return now

    def y_copy(d, q):
        return remote(
            gt.at[cols(q, fc), pl.ds(0, 512)],
            gt.at[cols(q, fc), pl.ds((4 - d) * 512, 512)],
            y_send.at[d - 1, q],
            y_recv.at[3 - d, q],
            group[d],
        )

    def y_start(q):
        for d in (2, 1, 3):
            y_copy(d, q).start()

    def arrived(*s):
        landed(n.at[rows(*s)], n_recv.at[slot(*s)])

    def block(zz, last=False):
        for ll in (0, 1):
            arrived(1, zz, ll)
        a, b = zz * 64, 256 + zz * 64

        @pl.loop(0, 4)
        def _(j):
            t = cols(j, 256)
            x = jnp.concatenate([n[a : a + 64, :], n[b : b + 64, :]], axis=0)
            pre = jnp.dot(x, w[:, t], preferred_element_type=F32) + bias[:, t].astype(F32)
            up = jnp.concatenate([g[a : a + 64, t], g[b : b + 64, t]], axis=0).astype(F32)
            sq = pre * pre
            th = jnp.tanh(GELU_A * pre * (1.0 + GELU_B * sq))
            slope = 0.5 * (1.0 + th) + 0.5 * GELU_A * pre * (1.0 - th * th) * (1.0 + 3.0 * GELU_B * sq)
            grad = (up * slope).astype(BF16)
            g[a : a + 64, t] = grad[0:64]
            g[b : b + 64, t] = grad[64:128]
            if last:
                gt[t, 0:512] = g[:, t].T

                @pl.when(j == 0)
                def _():
                    y_start(0)
                    y_start(1)

    own = (0, 0, 0)
    send(own, (0, 0, 1), pair)
    send(own, (0, 3, 0), ring[1])
    send(own, (0, 1, 0), ring[3])
    send(own, (1, 0, 0), sib)
    exchange((0, 0), "whole")

    arrived(0, 0, 1)
    send((0, 0, 1), (0, 3, 1), ring[1])
    send((0, 0, 1), (0, 1, 1), ring[3])
    send((0, 0, 1), (1, 0, 1), sib)
    exchange((0, 1), "whole")
    for cp in loads[3:]:
        cp.wait()
    block(0)
    for ll in (0, 1):
        arrived(0, 3, ll)
        send((0, 3, ll), (0, 2, ll), ring[1], half=0)
        arrived(0, 1, ll)
        send((0, 1, ll), (0, 2, ll), ring[3], half=1)
        for zz in (3, 1):
            send((0, zz, ll), (1, zz, ll), sib)
            exchange((zz, ll), "first" if ll else "whole")
    block(3)
    block(1)
    pass_on(SOON, "whole")
    for ll in (0, 1):
        for half, sem in ((0, slot(0, 2, ll)), (1, 16 + ll)):
            landed(n.at[pl.ds(slot(0, 2, ll) * 32 + half * 16, 16)], n_recv.at[sem])
        send((0, 2, ll), (1, 2, ll), sib)
        exchange((2, ll), "first")
    block(2, last=True)
    own_columns = pltpu.make_async_copy(n.at[:, cols(y, 2048)], cb.at[pl.ds(0, 512)], own_sem)
    own_columns.start()

    def s_copy(j):
        k = lax.rem(j, 2)
        return remote(sb.at[k], share.at[pl.ds(2 * j, 2)], s_send.at[k], s_recv.at[j], sib)

    def z_copy(d, j):
        return remote(
            zs.at[pl.ds(d * 64, 64), cols(j, dc)],
            zr.at[3 - d, :, cols(j, dc)],
            z_send.at[d - 1, j],
            z_recv.at[3 - d, j],
            ring[d],
        )

    def core_sum(j):
        t = cols(j, dc)
        landed(share.at[pl.ds(2 * j, 2)], s_recv.at[j])
        theirs = share[pl.ds(2 * j, 2)].reshape(256, dc).astype(F32)
        zs[:, t] = (zs[:, t].astype(F32) + theirs).astype(BF16)
        for d in (2, 1, 3):
            z_copy(d, j).start()

    def normed_part(j):
        k = lax.rem(j, 2)

        @pl.when(j >= 2)
        def _():
            s_copy(j).wait_send()

        @pl.loop(0, dc // 512)
        def _(i):
            t = pl.ds(pl.multiple_of(j * dc + i * 512, 512), 512)
            p = lax.dot_general(g[...], w[t, :], (((1,), (1,)), ((), ())), preferred_element_type=F32)
            p = p.astype(BF16)
            zs[:, t] = p[0:256]
            sb[k, 0, :, cols(i, 512)] = p[256:384]
            sb[k, 1, :, cols(i, 512)] = p[384:512]

        s_copy(j).start()

        @pl.when(j >= 1)
        def _():
            core_sum(j - 1)

    def x_copy(q):
        return remote(pw.at[q], xw.at[q], x_send.at[q], x_recv.at[q], cross)

    def l_copy(j):
        return remote(xs.at[:, cols(j, dc)], xr.at[:, cols(j, dc)], l_send.at[j], l_recv.at[j], pair)

    def weight_tile(q, column):
        t = pl.ds(pl.multiple_of(column, 512), 512)
        return jnp.dot(gt[cols(q, fc), :], cb[:, t], preferred_element_type=F32).astype(BF16)

    def weight_first(q):
        for s in (1, 2, 3):
            landed(gt.at[cols(q, fc), pl.ds(s * 512, 512)], y_recv.at[s - 1, q])

        @pl.loop(0, 2)
        def _(i):
            pw[q, :, cols(i, 512)] = weight_tile(q, (1 - h) * 1024 + i * 512)

        x_copy(q).start()

    def weight_second(q):
        @pl.loop(0, 2)
        def _(i):
            share[q, :, cols(i, 512)] = weight_tile(q, h * 1024 + i * 512)

        nt = (((1,), (1,)), ((), ()))
        bsum[:, cols(q, fc)] = lax.dot_general(
            jnp.ones((8, 2048), BF16), gt[cols(q, fc), :], nt, preferred_element_type=F32
        )

    def out_copy(q):
        k = lax.rem(q, 2)
        return pltpu.make_async_copy(weight_grad.at[k], weight_hbm.at[:, cols(q, fc)], wo_sem.at[k])

    def weight_sum(q):
        landed(xw.at[q], x_recv.at[q])

        @pl.when(q >= 2)
        def _():
            out_copy(q - 2).wait()

        weight_grad[lax.rem(q, 2)] = (share[q].astype(F32) + xw[q].astype(F32)).T.astype(BF16)
        out_copy(q).start()

    def z_sum(j):
        t = cols(j, dc)
        for s in range(3):
            landed(zr.at[s, :, t], z_recv.at[s, j])
        total = zs[0:64, t].astype(F32)
        for s in range(3):
            total += zr[s, :, t].astype(F32)
        keep[:, t] = total[0:32]
        xs[:, t] = total[32:64].astype(BF16)
        l_copy(j).start()

    def row_sum(j):
        t = cols(j, dc)
        landed(xr.at[:, t], l_recv.at[j])
        total = keep[:, t] + xr[:, t].astype(F32)
        keep[:, t] = total
        term[0, 0:1, t] = jnp.sum(total, axis=0, keepdims=True)
        hat = xhat(t)
        term[0, 1:2, t] = jnp.sum(total * hat, axis=0, keepdims=True)
        scaled = total * (1.0 + of_image(scale, t))
        stats[2] += wide(jnp.sum(scaled, axis=-1, keepdims=True))
        stats[3] += wide(jnp.sum(scaled * hat, axis=-1, keepdims=True))

    normed_part(0)
    pass_on(LATE, "first")
    pl.loop(1, AHEAD)(normed_part)
    own_columns.wait()
    for cp in moved:
        cp.wait()

    def step(q):
        weight_first(q)

        @pl.when(q + 2 < NF)
        def _():
            y_start(q + 2)

        @pl.when(q + AHEAD < ND)
        def _():
            normed_part(q + AHEAD)

        @pl.when(q + AHEAD == ND)
        def _():
            core_sum(ND - 1)

    step(0)
    for piece in LATE:
        exchange(piece, "second")
    step(1)
    for cp in pass_on(LATE, "second"):
        cp.wait()
    z_sum(0)

    @pl.loop(2, NF)
    def _(q):
        step(q)
        weight_second(q - 2)
        z_sum(q - 1)
        row_sum(q - 2)

        @pl.when(q >= 4)
        def _():
            weight_sum(q - 4)

    z_sum(ND - 1)
    weight_second(NF - 2)
    weight_second(NF - 1)
    b_copy = remote(bsum, brec, b_send.at[0], b_recv.at[0], cross)
    b_copy.start()
    row_sum(ND - 2)
    row_sum(ND - 1)

    near = (peer()[0], z + 1 - 2 * lax.rem(z, 2), peer()[2])
    hops = [
        remote(term.at[k], trec.at[k], t_send.at[k], t_recv.at[k], to)
        for k, to in enumerate((sib, pair, near, ring[2]))
    ]
    hops[0].start()

    @pl.loop(0, ND)
    def _(j):
        t = cols(j, dc)
        mean_one, mean_two = stats[2, :, 0:1] * (1.0 / 8192), stats[3, :, 0:1] * (1.0 / 8192)
        scaled = keep[:, t] * (1.0 + of_image(scale, t))
        token_grad[:, t] = (stats[1, :, 0:1] * (scaled - mean_one - xhat(t) * mean_two)).astype(BF16)

    outs = [
        pltpu.make_async_copy(src, dst, out_sem.at[k])
        for k, (src, dst) in enumerate(
            ((token_grad, token_hbm), (brec, sums_hbm), (shift_grad, shift_out), (scale_grad, scale_out))
        )
    ]
    outs[0].start()

    for k in range(3):
        hops[k].wait_recv()
        term[k + 1] = term[k] + trec[k]
        hops[k + 1].start()
        weight_sum(NF - 4 + k)
    b_copy.wait()
    brec[...] = bsum[...] + brec[...]
    outs[1].start()
    hops[3].wait_recv()
    first = (z < 2).astype(F32) > 0.5
    near_sum, far_sum = term[3], trec[3]
    shift_grad[0:1, :] = jnp.where(first, near_sum[0:1], far_sum[0:1])
    shift_grad[1:2, :] = jnp.where(first, far_sum[0:1], near_sum[0:1])
    scale_grad[0:1, :] = jnp.where(first, near_sum[1:2], far_sum[1:2])
    scale_grad[1:2, :] = jnp.where(first, far_sum[1:2], near_sum[1:2])
    outs[2].start()
    outs[3].start()
    weight_sum(NF - 1)

    for k in range(4):
        hops[k].wait_send()
    for cp in pending + sent:
        cp.wait_send()
    s_copy(0).wait_send()
    s_copy(1).wait_send()

    @pl.loop(0, NF)
    def _(q):
        for d in (1, 2, 3):
            y_copy(d, q).wait_send()
            z_copy(d, q).wait_send()
        l_copy(q).wait_send()
        x_copy(q).wait_send()

    out_copy(NF - 2).wait()
    out_copy(NF - 1).wait()
    for cp in outs:
        cp.wait()


def result_kernel(a, b, c, d, e, ao, bo, co, do, eo, av, bv, cv, dv, ev, sem):
    held = (av, bv, cv, dv, ev)
    takes = [pltpu.make_async_copy(src, v, sem.at[k]) for k, (src, v) in enumerate(zip((a, b, c, d, e), held))]
    gives = [
        pltpu.make_async_copy(v, dst, sem.at[5 + k])
        for k, (v, dst) in enumerate(zip((av, bv, cv.at[0:1], dv, ev), (ao, bo, co, do, eo)))
    ]
    for cp in takes:
        cp.start()
    for cp, give in zip(takes, gives):
        cp.wait()
        give.start()
    for give in gives:
        give.wait()


def local(tokens, mod_shift, mod_scale, up_weight, up_bias, act_grad):
    vmem = pl.BlockSpec(memory_space=pltpu.VMEM)
    hbm = pl.BlockSpec(memory_space=pltpu.HBM)
    dma = pltpu.SemaphoreType.DMA
    results = (
        jax.ShapeDtypeStruct((32, 8192), BF16),
        jax.ShapeDtypeStruct((1024, 1024), BF16),
        jax.ShapeDtypeStruct((8, 1024), F32),
        jax.ShapeDtypeStruct((2, 8192), F32),
        jax.ShapeDtypeStruct((2, 8192), F32),
    )
    parts = pl.pallas_call(
        block_kernel,
        out_shape=results,
        in_specs=[hbm] * 6,
        out_specs=(hbm,) * 5,
        scratch_shapes=[
            pltpu.VMEM((32, 8192), BF16),
            pltpu.VMEM((2, 8192), BF16),
            pltpu.VMEM((2, 8192), BF16),
            pltpu.VMEM((1, 1024), BF16),
            pltpu.VMEM((512, 8192), BF16),
            pltpu.VMEM((2048, 2048), BF16),
            pltpu.VMEM((8192, 1024), BF16),
            pltpu.VMEM((512, 1024), BF16),
            pltpu.VMEM((1024, 2048), BF16),
            pltpu.VMEM((2, 2, 128, 1024), BF16),
            pltpu.VMEM((16, 128, 1024), BF16),
            pltpu.VMEM((NF, 128, 1024), BF16),
            pltpu.VMEM((256, 8192), BF16),
            pltpu.VMEM((3, 64, 8192), BF16),
            pltpu.VMEM((32, 8192), BF16),
            pltpu.VMEM((32, 8192), BF16),
            pltpu.VMEM((32, 8192), F32),
            pltpu.VMEM((4, 32, 128), F32),
            pltpu.VMEM((NF, 128, 1024), BF16),
            pltpu.VMEM((8, 1024), F32),
            pltpu.VMEM((8, 1024), F32),
            pltpu.VMEM((4, 2, 8192), F32),
            pltpu.VMEM((4, 2, 8192), F32),
            pltpu.VMEM((32, 8192), BF16),
            pltpu.VMEM((2, 1024, 128), BF16),
            pltpu.VMEM((2, 8192), F32),
            pltpu.VMEM((2, 8192), F32),
            dma((21,)),
            dma((4,)),
            dma((2,)),
            dma(()),
            dma((17,)),
            dma((18,)),
            dma((3, 12)),
            dma((3, 12)),
            dma((3, 12)),
            dma((3, 12)),
            dma((3, NF)),
            dma((3, NF)),
            dma((2,)),
            dma((ND,)),
            dma((3, ND)),
            dma((3, ND)),
            dma((ND,)),
            dma((ND,)),
            dma((NF,)),
            dma((NF,)),
            dma((1,)),
            dma((1,)),
            dma((4,)),
            dma((4,)),
        ],
        compiler_params=pltpu.CompilerParams(
            collective_id=0, has_side_effects=True, vmem_limit_bytes=61 * MIB
        ),
        name="block",
    )(tokens, mod_shift, mod_scale, up_weight, up_bias[None, :], act_grad)
    final = list(results)
    final[2] = jax.ShapeDtypeStruct((1, 1024), F32)
    token_grad, weight_grad, bias_grad, shift_grad, scale_grad = pl.pallas_call(
        result_kernel,
        out_shape=tuple(final),
        in_specs=[hbm] * 5,
        out_specs=(hbm,) * 5,
        scratch_shapes=[pltpu.VMEM(r.shape, r.dtype) for r in results] + [dma((10,))],
        compiler_params=pltpu.CompilerParams(vmem_limit_bytes=61 * MIB),
        name="results",
    )(*parts)
    return token_grad, weight_grad, bias_grad.reshape(1024), shift_grad, scale_grad


def solution(mesh):
    return jax.shard_map(
        local,
        mesh=mesh,
        in_specs=(
            P(("dp", "tx", "ty"), None),
            P("dp", None),
            P("dp", None),
            P(None, ("tx", "ty")),
            P(("tx", "ty")),
            P("dp", ("tx", "ty")),
        ),
        out_specs=(
            P(("dp", "tx", "ty"), None),
            P("dp", ("tx", "ty")),
            P(("tx", "ty")),
            P("dp", None),
            P("dp", None),
        ),
        check_vma=False,
    )
```

```python
import jax
import jax.numpy as jnp
from jax import lax
from jax.experimental import pallas as pl
from jax.experimental.pallas import tpu as pltpu
from jax.sharding import PartitionSpec as P

MESH = pl.DeviceIdType.MESH
MIB = 1 << 20
F32 = jnp.float32
BF16 = jnp.bfloat16
GELU_A = 0.7978845608028654
GELU_B = 0.044715


def place():
    dp, tx, ty = (lax.axis_index(a) for a in ("dp", "tx", "ty"))
    return dp // 2, dp % 2, tx, ty // 2, ty % 2


def peer(dy=0, dh=0, dz=0, dl=0, dc=0):
    y, h, z, l, c = place()
    return (
        lax.rem(y + dy, 4) * 2 + lax.rem(h + dh, 2),
        lax.rem(z + dz, 4),
        lax.rem(l + dl, 2) * 2 + lax.rem(c + dc, 2),
    )


def remote(src, dst, send, recv, to):
    return pltpu.make_async_remote_copy(
        src_ref=src, dst_ref=dst, send_sem=send, recv_sem=recv, device_id=to, device_id_type=MESH
    )


def landed(ref, sem):
    pltpu.make_async_copy(ref, ref, sem).wait()


def cols(i, n):
    return pl.ds(pl.multiple_of(i * n, n), n)


def wide(x):
    return jnp.broadcast_to(x, (32, 128))


def slot(c, z, l):
    return c * 8 + z * 2 + l


def rows(c, z, l):
    return pl.ds(slot(c, z, l) * 32, 32)


SOON = ((0, 0), (0, 1), (3, 0), (1, 0))
LATE = ((3, 1), (1, 1), (2, 0), (2, 1))
NF = 8
ND = 8
AHEAD = 3


def block_kernel(
    tok_hbm, shift_hbm, scale_hbm, w_hbm, bias_hbm, act_hbm,
    token_hbm, weight_hbm, sums_hbm, shift_out, scale_out,
    tok, shift, scale, bias, n, cb, w, g, gt, sb, share, pw, zs, zr, xs, xr, keep, stats,
    xw, bsum, brec, term, trec, token_grad, weight_grad, shift_grad, scale_grad,
    in_sem, out_sem, wo_sem, own_sem, n_send, n_recv, c_send, c_recv, f_send, f_recv,
    y_send, y_recv, s_send, s_recv, z_send, z_recv, l_send, l_recv, x_send, x_recv,
    b_send, b_recv, t_send, t_recv,
):
    y, h, z, l, c = place()
    sib = peer(dc=1)
    pair = peer(dl=1)
    ring = {d: peer(dz=d) for d in (1, 2, 3)}
    group = {d: peer(dy=d) for d in (1, 2, 3)}
    cross = peer(dh=1)
    fc, dc = 1024 // NF, 8192 // ND

    loads = [
        pltpu.make_async_copy(src, dst, in_sem.at[k])
        for k, (src, dst) in enumerate(
            ((tok_hbm, tok), (shift_hbm, shift), (scale_hbm, scale), (bias_hbm, bias), (w_hbm, w))
        )
    ]
    for cc in (0, 1):
        for zz in range(4):
            for ll in (0, 1):
                r = (lax.rem(z + zz, 4) * 4 + lax.rem(l + ll, 2) * 2 + lax.rem(c + cc, 2)) * 32
                src = act_hbm.at[pl.ds(pl.multiple_of(r, 32), 32)]
                loads.append(pltpu.make_async_copy(src, g.at[rows(cc, zz, ll)], in_sem.at[len(loads)]))
    for cp in loads:
        cp.start()
    peers = [sib, pair, *ring.values(), *group.values(), cross]
    barrier = pltpu.get_barrier_semaphore()
    for p in peers:
        pl.semaphore_signal(barrier, inc=1, device_id=p, device_id_type=MESH)
    for cp in loads[:3]:
        cp.wait()

    def of_image(ref, t):
        m = ref[:, t].astype(F32)
        return jnp.where((z < 2).astype(F32) > 0.5, m[0:1], m[1:2])

    def row_total(f):
        def body(j, acc):
            return acc + jnp.sum(f(tok[:, cols(j, dc)].astype(F32)), axis=-1, keepdims=True)

        return lax.fori_loop(0, ND, body, jnp.zeros((32, 1), F32)) * (1.0 / 8192)

    average = row_total(lambda v: v)
    inverse = lax.rsqrt(row_total(lambda v: (v - average) * (v - average)) + 1e-06)
    stats[0] = wide(average)
    stats[1] = wide(inverse)
    stats[2] = jnp.zeros((32, 128), F32)
    stats[3] = jnp.zeros((32, 128), F32)

    def xhat(t):
        return (tok[:, t].astype(F32) - stats[0, :, 0:1]) * stats[1, :, 0:1]

    @pl.loop(0, ND)
    def _(j):
        t = cols(j, dc)
        n[rows(0, 0, 0), t] = (xhat(t) * (1.0 + of_image(scale, t)) + of_image(shift, t)).astype(BF16)

    pl.semaphore_wait(barrier, len(peers))

    pending = []

    def half_rows(s, half):
        return n.at[pl.ds(slot(*s) * 32 + half * 16, 16)]

    def send(src, dst, to, halves=(0, 1)):
        for half in halves:
            sem = n_recv.at[slot(*dst) * 2 + half]
            cp = remote(half_rows(src, half), half_rows(dst, half), n_send.at[len(pending)], sem, to)
            cp.start()
            pending.append(cp)

    def span(piece, part):
        k = piece[0] * 2 + piece[1]
        if part == "whole":
            return 0, 2048, k
        if part == "first":
            return (1 - h) * 1024, 1024, k
        return h * 1024, 1024, 8 + LATE.index(piece)

    def place_of(s, cc, piece, part):
        start, width, _ = span(piece, part)
        r = pl.ds(s * 512 + slot(cc, *piece) * 32, 32)
        return cb.at[r, pl.ds(pl.multiple_of(start, 1024), width)]

    def columns_copy(d, piece, part):
        start, width, k = span(piece, part)
        start = lax.rem(y + d, 4) * 2048 + start
        src = n.at[rows(0, *piece), pl.ds(pl.multiple_of(start, 1024), width)]
        dst = place_of(4 - d, 0, piece, part)
        return remote(src, dst, c_send.at[d - 1, k], c_recv.at[3 - d, k], group[d])

    sent = []

    def exchange(piece, part):
        for d in (2, 1, 3):
            cp = columns_copy(d, piece, part)
            cp.start()
            sent.append(cp)

    moved = []

    def pass_on(pieces, part):
        now = []
        for piece in pieces:
            k = span(piece, part)[2]
            for s in (1, 2, 3):
                src = place_of(s, 0, piece, part)
                landed(src, c_recv.at[s - 1, k])
                cp = remote(
                    src, place_of(s, 1, piece, part), f_send.at[s - 1, k], f_recv.at[s - 1, k], sib
                )
                cp.start()
                now.append(cp)
        moved.extend(now)
        return now

    def y_copy(d, q):
        r = cols(q, fc)
        return remote(
            gt.at[r, pl.ds(0, 512)],
            gt.at[r, pl.ds((4 - d) * 512, 512)],
            y_send.at[d // 2, q],
            y_recv.at[3 - d, q],
            group[d],
        )

    def y_relay(d, q):
        half = d // 2
        r = pl.ds(pl.multiple_of(q * fc + half * (fc // 2), fc // 2), fc // 2)
        return remote(
            gt.at[r, pl.ds((4 - d) * 512, 512)],
            gt.at[r, pl.ds(1024, 512)],
            y_send.at[2 + half, q],
            y_recv.at[1 if half == 0 else 3, q],
            group[d],
        )

    def y_start(q):
        for d in (1, 3):
            y_copy(d, q).start()

    def y_pass(q):
        for d in (1, 3):
            landed(gt.at[cols(q, fc), pl.ds((4 - d) * 512, 512)], y_recv.at[3 - d, q])
            y_relay(d, q).start()

    def arrived(s, halves=(0, 1)):
        for half in halves:
            landed(half_rows(s, half), n_recv.at[slot(*s) * 2 + half])

    def block(pieces, last=False):
        for piece in pieces:
            arrived((1, *piece))
        at = [rows(cc, *piece) for cc in (0, 1) for piece in pieces]

        @pl.loop(0, 4)
        def _(j):
            t = cols(j, 256)
            x = jnp.concatenate([n[r, :] for r in at], axis=0)
            pre = jnp.dot(x, w[:, t], preferred_element_type=F32) + bias[:, t].astype(F32)
            up = jnp.concatenate([g[r, t] for r in at], axis=0).astype(F32)
            sq = pre * pre
            th = jnp.tanh(GELU_A * pre * (1.0 + GELU_B * sq))
            slope = 0.5 * (1.0 + th) + 0.5 * GELU_A * pre * (1.0 - th * th) * (1.0 + 3.0 * GELU_B * sq)
            grad = (up * slope).astype(BF16)
            for k, r in enumerate(at):
                g[r, t] = grad[k * 32 : k * 32 + 32]
            if last:
                gt[t, 0:512] = g[:, t].T

                @pl.when(j == 0)
                def _():
                    y_start(0)
                    y_start(1)

    own, near_pair = (0, 0, 0), (0, 0, 1)
    send(own, (0, 3, 0), ring[1], (0,))
    send(own, (0, 1, 0), ring[3], (1,))
    send(own, (0, 0, 1), pair)
    send(own, (0, 3, 0), ring[1], (1,))
    send(own, (0, 1, 0), ring[3], (0,))
    send(own, (1, 0, 0), sib)
    exchange((0, 0), "whole")

    def ring_piece(ll, part):
        arrived((0, 3, ll), (0,))
        send((0, 3, ll), (0, 2, ll), ring[1], (0,))
        arrived((0, 1, ll), (1,))
        send((0, 1, ll), (0, 2, ll), ring[3], (1,))
        if ll == 0:
            arrived(near_pair, (1,))
            send(near_pair, (0, 1, 1), ring[3], (1,))
            send(near_pair, (0, 3, 1), ring[1], (1,))
            send(near_pair, (1, 0, 1), sib)
            exchange((0, 1), "whole")
        arrived((0, 3, ll), (1,))
        arrived((0, 1, ll), (0,))
        for zz in (3, 1):
            send((0, zz, ll), (1, zz, ll), sib)
            exchange((zz, ll), part)

    def opposite_piece(ll):
        arrived((0, 2, ll))
        send((0, 2, ll), (1, 2, ll), sib)
        exchange((2, ll), "first")

    arrived(near_pair, (0,))
    send(near_pair, (0, 3, 1), ring[1], (0,))
    send(near_pair, (0, 1, 1), ring[3], (0,))
    ring_piece(0, "whole")
    for cp in loads[3:]:
        cp.wait()
    block(((0, 0), (0, 1)))
    block(((3, 0), (1, 0)))
    ring_piece(1, "first")
    opposite_piece(0)
    block(((3, 1), (1, 1)))
    opposite_piece(1)
    pass_on(SOON, "whole")
    block(((2, 0), (2, 1)), last=True)
    own_columns = pltpu.make_async_copy(n.at[:, cols(y, 2048)], cb.at[pl.ds(0, 512)], own_sem)
    own_columns.start()

    def s_copy(j):
        k = lax.rem(j, 2)
        return remote(sb.at[k], share.at[pl.ds(2 * j, 2)], s_send.at[k], s_recv.at[j], sib)

    def z_copy(d, j):
        return remote(
            zs.at[pl.ds(d * 64, 64), cols(j, dc)],
            zr.at[3 - d, :, cols(j, dc)],
            z_send.at[d - 1, j],
            z_recv.at[3 - d, j],
            ring[d],
        )

    def core_sum(j):
        t = cols(j, dc)
        landed(share.at[pl.ds(2 * j, 2)], s_recv.at[j])
        theirs = share[pl.ds(2 * j, 2)].reshape(256, dc).astype(F32)
        zs[:, t] = (zs[:, t].astype(F32) + theirs).astype(BF16)
        for d in (2, 1, 3):
            z_copy(d, j).start()

    def normed_part(j):
        k = lax.rem(j, 2)

        @pl.when(j >= 2)
        def _():
            s_copy(j).wait_send()

        @pl.loop(0, dc // 512)
        def _(i):
            t = pl.ds(pl.multiple_of(j * dc + i * 512, 512), 512)
            p = lax.dot_general(g[...], w[t, :], (((1,), (1,)), ((), ())), preferred_element_type=F32)
            p = p.astype(BF16)
            zs[:, t] = p[0:256]
            sb[k, 0, :, cols(i, 512)] = p[256:384]
            sb[k, 1, :, cols(i, 512)] = p[384:512]

        s_copy(j).start()

        @pl.when(j >= 1)
        def _():
            core_sum(j - 1)

    def x_copy(q):
        return remote(pw.at[q], xw.at[q], x_send.at[q], x_recv.at[q], cross)

    def l_copy(j):
        return remote(xs.at[:, cols(j, dc)], xr.at[:, cols(j, dc)], l_send.at[j], l_recv.at[j], pair)

    def weight_tile(q, column):
        t = pl.ds(pl.multiple_of(column, 512), 512)
        return jnp.dot(gt[cols(q, fc), :], cb[:, t], preferred_element_type=F32).astype(BF16)

    def weight_first(q):
        for half in (0, 1):
            r = pl.ds(pl.multiple_of(q * fc + half * (fc // 2), fc // 2), fc // 2)
            landed(gt.at[r, pl.ds(1024, 512)], y_recv.at[1 + 2 * half, q])

        @pl.loop(0, 2)
        def _(i):
            pw[q, :, cols(i, 512)] = weight_tile(q, (1 - h) * 1024 + i * 512)

        x_copy(q).start()

    def weight_second(q):
        @pl.loop(0, 2)
        def _(i):
            share[q, :, cols(i, 512)] = weight_tile(q, h * 1024 + i * 512)

        nt = (((1,), (1,)), ((), ()))
        bsum[:, cols(q, fc)] = lax.dot_general(
            jnp.ones((8, 2048), BF16), gt[cols(q, fc), :], nt, preferred_element_type=F32
        )

    def out_copy(q):
        k = lax.rem(q, 2)
        return pltpu.make_async_copy(weight_grad.at[k], weight_hbm.at[:, cols(q, fc)], wo_sem.at[k])

    def weight_sum(q):
        landed(xw.at[q], x_recv.at[q])

        @pl.when(q >= 2)
        def _():
            out_copy(q - 2).wait()

        weight_grad[lax.rem(q, 2)] = (share[q].astype(F32) + xw[q].astype(F32)).T.astype(BF16)
        out_copy(q).start()

    def z_sum(j):
        t = cols(j, dc)
        for s in range(3):
            landed(zr.at[s, :, t], z_recv.at[s, j])
        total = zs[0:64, t].astype(F32)
        for s in range(3):
            total += zr[s, :, t].astype(F32)
        keep[:, t] = total[0:32]
        xs[:, t] = total[32:64].astype(BF16)
        l_copy(j).start()

    def row_sum(j):
        t = cols(j, dc)
        landed(xr.at[:, t], l_recv.at[j])
        total = keep[:, t] + xr[:, t].astype(F32)
        keep[:, t] = total
        term[0, 0:1, t] = jnp.sum(total, axis=0, keepdims=True)
        hat = xhat(t)
        term[0, 1:2, t] = jnp.sum(total * hat, axis=0, keepdims=True)
        scaled = total * (1.0 + of_image(scale, t))
        stats[2] += wide(jnp.sum(scaled, axis=-1, keepdims=True))
        stats[3] += wide(jnp.sum(scaled * hat, axis=-1, keepdims=True))

    normed_part(0)
    y_pass(0)
    pass_on(LATE, "first")
    pl.loop(1, AHEAD)(normed_part)
    own_columns.wait()
    for cp in moved:
        cp.wait()

    def step(q):
        weight_first(q)

        @pl.when(q + 1 < NF)
        def _():
            y_pass(q + 1)

        @pl.when(q + 2 < NF)
        def _():
            y_start(q + 2)

        j = AHEAD + 2 * q

        @pl.when(j < ND)
        def _():
            normed_part(j)

        @pl.when(j + 1 < ND)
        def _():
            normed_part(j + 1)

        @pl.when(q == (ND - AHEAD + 1) // 2)
        def _():
            core_sum(ND - 1)

    step(0)
    for piece in LATE:
        exchange(piece, "second")
    z_sum(0)
    step(1)
    z_sum(1)
    row_sum(0)
    for cp in pass_on(LATE, "second"):
        cp.wait()

    @pl.loop(2, NF)
    def _(q):
        step(q)
        weight_second(q - 2)
        z_sum(q)
        row_sum(q - 1)

        @pl.when(q >= 4)
        def _():
            weight_sum(q - 4)

    row_sum(ND - 1)

    near = (peer()[0], z + 1 - 2 * lax.rem(z, 2), peer()[2])
    hops = [
        remote(term.at[k], trec.at[k], t_send.at[k], t_recv.at[k], to)
        for k, to in enumerate((sib, pair, near, ring[2]))
    ]
    hops[0].start()
    weight_second(NF - 2)
    weight_second(NF - 1)
    b_copy = remote(bsum, brec, b_send.at[0], b_recv.at[0], cross)
    b_copy.start()
    hops[0].wait_recv()
    term[1] = term[0] + trec[0]
    hops[1].start()

    @pl.loop(0, ND)
    def _(j):
        t = cols(j, dc)
        mean_one, mean_two = stats[2, :, 0:1] * (1.0 / 8192), stats[3, :, 0:1] * (1.0 / 8192)
        scaled = keep[:, t] * (1.0 + of_image(scale, t))
        token_grad[:, t] = (stats[1, :, 0:1] * (scaled - mean_one - xhat(t) * mean_two)).astype(BF16)

    outs = [
        pltpu.make_async_copy(src, dst, out_sem.at[k])
        for k, (src, dst) in enumerate(
            ((token_grad, token_hbm), (brec, sums_hbm), (shift_grad, shift_out), (scale_grad, scale_out))
        )
    ]
    outs[0].start()

    for k in (1, 2):
        hops[k].wait_recv()
        term[k + 1] = term[k] + trec[k]
        hops[k + 1].start()
        weight_sum(NF - 5 + k)
    b_copy.wait()
    brec[...] = bsum[...] + brec[...]
    outs[1].start()
    hops[3].wait_recv()
    first = (z < 2).astype(F32) > 0.5
    near_sum, far_sum = term[3], trec[3]
    shift_grad[0:1, :] = jnp.where(first, near_sum[0:1], far_sum[0:1])
    shift_grad[1:2, :] = jnp.where(first, far_sum[0:1], near_sum[0:1])
    scale_grad[0:1, :] = jnp.where(first, near_sum[1:2], far_sum[1:2])
    scale_grad[1:2, :] = jnp.where(first, far_sum[1:2], near_sum[1:2])
    outs[2].start()
    outs[3].start()
    weight_sum(NF - 2)
    weight_sum(NF - 1)

    for k in range(4):
        hops[k].wait_send()
    for cp in pending + sent:
        cp.wait_send()
    s_copy(0).wait_send()
    s_copy(1).wait_send()

    @pl.loop(0, NF)
    def _(q):
        for d in (1, 3):
            y_copy(d, q).wait_send()
            y_relay(d, q).wait_send()
        for d in (1, 2, 3):
            z_copy(d, q).wait_send()
        l_copy(q).wait_send()
        x_copy(q).wait_send()

    out_copy(NF - 2).wait()
    out_copy(NF - 1).wait()
    for cp in outs:
        cp.wait()


def result_kernel(a, b, c, d, e, ao, bo, co, do, eo, av, bv, cv, dv, ev, sem):
    held = (av, bv, cv, dv, ev)
    takes = [pltpu.make_async_copy(src, v, sem.at[k]) for k, (src, v) in enumerate(zip((a, b, c, d, e), held))]
    gives = [
        pltpu.make_async_copy(v, dst, sem.at[5 + k])
        for k, (v, dst) in enumerate(zip((av, bv, cv.at[0:1], dv, ev), (ao, bo, co, do, eo)))
    ]
    for cp in takes:
        cp.start()
    for cp, give in zip(takes, gives):
        cp.wait()
        give.start()
    for give in gives:
        give.wait()


def local(tokens, mod_shift, mod_scale, up_weight, up_bias, act_grad):
    vmem = pl.BlockSpec(memory_space=pltpu.VMEM)
    hbm = pl.BlockSpec(memory_space=pltpu.HBM)
    dma = pltpu.SemaphoreType.DMA
    results = (
        jax.ShapeDtypeStruct((32, 8192), BF16),
        jax.ShapeDtypeStruct((1024, 1024), BF16),
        jax.ShapeDtypeStruct((8, 1024), F32),
        jax.ShapeDtypeStruct((2, 8192), F32),
        jax.ShapeDtypeStruct((2, 8192), F32),
    )
    parts = pl.pallas_call(
        block_kernel,
        out_shape=results,
        in_specs=[hbm] * 6,
        out_specs=(hbm,) * 5,
        scratch_shapes=[
            pltpu.VMEM((32, 8192), BF16),
            pltpu.VMEM((2, 8192), BF16),
            pltpu.VMEM((2, 8192), BF16),
            pltpu.VMEM((1, 1024), BF16),
            pltpu.VMEM((512, 8192), BF16),
            pltpu.VMEM((2048, 2048), BF16),
            pltpu.VMEM((8192, 1024), BF16),
            pltpu.VMEM((512, 1024), BF16),
            pltpu.VMEM((1024, 2048), BF16),
            pltpu.VMEM((2, 2, 128, 1024), BF16),
            pltpu.VMEM((16, 128, 1024), BF16),
            pltpu.VMEM((NF, 128, 1024), BF16),
            pltpu.VMEM((256, 8192), BF16),
            pltpu.VMEM((3, 64, 8192), BF16),
            pltpu.VMEM((32, 8192), BF16),
            pltpu.VMEM((32, 8192), BF16),
            pltpu.VMEM((32, 8192), F32),
            pltpu.VMEM((4, 32, 128), F32),
            pltpu.VMEM((NF, 128, 1024), BF16),
            pltpu.VMEM((8, 1024), F32),
            pltpu.VMEM((8, 1024), F32),
            pltpu.VMEM((4, 2, 8192), F32),
            pltpu.VMEM((4, 2, 8192), F32),
            pltpu.VMEM((32, 8192), BF16),
            pltpu.VMEM((2, 1024, 128), BF16),
            pltpu.VMEM((2, 8192), F32),
            pltpu.VMEM((2, 8192), F32),
            dma((21,)),
            dma((4,)),
            dma((2,)),
            dma(()),
            dma((32,)),
            dma((32,)),
            dma((3, 12)),
            dma((3, 12)),
            dma((3, 12)),
            dma((3, 12)),
            dma((4, NF)),
            dma((4, NF)),
            dma((2,)),
            dma((ND,)),
            dma((3, ND)),
            dma((3, ND)),
            dma((ND,)),
            dma((ND,)),
            dma((NF,)),
            dma((NF,)),
            dma((1,)),
            dma((1,)),
            dma((4,)),
            dma((4,)),
        ],
        compiler_params=pltpu.CompilerParams(
            collective_id=0, has_side_effects=True, vmem_limit_bytes=61 * MIB
        ),
        name="block",
    )(tokens, mod_shift, mod_scale, up_weight, up_bias[None, :], act_grad)
    final = list(results)
    final[2] = jax.ShapeDtypeStruct((1, 1024), F32)
    token_grad, weight_grad, bias_grad, shift_grad, scale_grad = pl.pallas_call(
        result_kernel,
        out_shape=tuple(final),
        in_specs=[hbm] * 5,
        out_specs=(hbm,) * 5,
        scratch_shapes=[pltpu.VMEM(r.shape, r.dtype) for r in results] + [dma((10,))],
        compiler_params=pltpu.CompilerParams(vmem_limit_bytes=61 * MIB),
        name="results",
    )(*parts)
    return token_grad, weight_grad, bias_grad.reshape(1024), shift_grad, scale_grad


def solution(mesh):
    return jax.shard_map(
        local,
        mesh=mesh,
        in_specs=(
            P(("dp", "tx", "ty"), None),
            P("dp", None),
            P("dp", None),
            P(None, ("tx", "ty")),
            P(("tx", "ty")),
            P("dp", ("tx", "ty")),
        ),
        out_specs=(
            P(("dp", "tx", "ty"), None),
            P("dp", ("tx", "ty")),
            P(("tx", "ty")),
            P("dp", None),
            P("dp", None),
        ),
        check_vma=False,
    )
```

```python
import jax
import jax.numpy as jnp
from jax import lax
from jax.experimental import pallas as pl
from jax.experimental.pallas import tpu as pltpu
from jax.sharding import PartitionSpec as P

MESH = pl.DeviceIdType.MESH
MIB = 1 << 20
F32 = jnp.float32
BF16 = jnp.bfloat16
GELU_A = 0.7978845608028654
GELU_B = 0.044715


def place():
    dp, tx, ty = (lax.axis_index(a) for a in ("dp", "tx", "ty"))
    return dp // 2, dp % 2, tx, ty // 2, ty % 2


def peer(dy=0, dh=0, dz=0, dl=0, dc=0):
    y, h, z, l, c = place()
    return (
        lax.rem(y + dy, 4) * 2 + lax.rem(h + dh, 2),
        lax.rem(z + dz, 4),
        lax.rem(l + dl, 2) * 2 + lax.rem(c + dc, 2),
    )


def remote(src, dst, send, recv, to):
    return pltpu.make_async_remote_copy(
        src_ref=src, dst_ref=dst, send_sem=send, recv_sem=recv, device_id=to, device_id_type=MESH
    )


def landed(ref, sem):
    pltpu.make_async_copy(ref, ref, sem).wait()


def cols(i, n):
    return pl.ds(pl.multiple_of(i * n, n), n)


def lane_sums(x):
    parts = [x[:, k : k + 128] for k in range(0, x.shape[1], 128)]
    while len(parts) > 1:
        parts = [a + b for a, b in zip(parts[::2], parts[1::2])]
    return parts[0]


def wide(x):
    return jnp.broadcast_to(x, (32, 128))


def slot(c, z, l):
    return c * 8 + z * 2 + l


def rows(c, z, l):
    return pl.ds(slot(c, z, l) * 32, 32)


SOON = ((0, 0), (0, 1), (3, 0), (1, 0))
LATE = ((3, 1), (1, 1), (2, 0), (2, 1))
NF = 8
ND = 8
AHEAD = 4


def block_kernel(
    tok_hbm, shift_hbm, scale_hbm, w_hbm, bias_hbm, act_hbm,
    token_hbm, weight_hbm, sums_hbm, shift_out, scale_out,
    tok, shift, scale, bias, n, cb, w, g, gt, sb, share, zs, zr, xr, keep, stats,
    xw, bsum, brec, term, trec, weight_grad, shift_grad, scale_grad,
    in_sem, out_sem, wo_sem, own_sem, n_send, n_recv, c_send, c_recv, f_send, f_recv,
    y_send, y_recv, s_send, s_recv, z_send, z_recv, l_send, l_recv, x_send, x_recv,
    b_send, b_recv, t_send, t_recv,
):
    y, h, z, l, c = place()
    sib = peer(dc=1)
    pair = peer(dl=1)
    ring = {d: peer(dz=d) for d in (1, 2, 3)}
    group = {d: peer(dy=d) for d in (1, 2, 3)}
    cross = peer(dh=1)
    fc, dc = 1024 // NF, 8192 // ND

    loads = [
        pltpu.make_async_copy(src, dst, in_sem.at[k])
        for k, (src, dst) in enumerate(
            ((tok_hbm, tok), (shift_hbm, shift), (scale_hbm, scale), (bias_hbm, bias), (w_hbm, w))
        )
    ]
    for cc in (0, 1):
        for zz in range(4):
            for ll in (0, 1):
                r = (lax.rem(z + zz, 4) * 4 + lax.rem(l + ll, 2) * 2 + lax.rem(c + cc, 2)) * 32
                src = act_hbm.at[pl.ds(pl.multiple_of(r, 32), 32)]
                loads.append(pltpu.make_async_copy(src, g.at[rows(cc, zz, ll)], in_sem.at[len(loads)]))
    for cp in loads:
        cp.start()
    peers = [sib, pair, *ring.values(), *group.values(), cross]
    barrier = pltpu.get_barrier_semaphore()
    for p in peers:
        pl.semaphore_signal(barrier, inc=1, device_id=p, device_id_type=MESH)
    for cp in loads[:3]:
        cp.wait()

    def of_image(ref, t):
        m = ref[:, t].astype(F32)
        return jnp.where((z < 2).astype(F32) > 0.5, m[0:1], m[1:2])

    def row_total(f):
        def body(j, acc):
            return acc + lane_sums(f(tok[:, cols(j, dc)].astype(F32)))

        acc = lax.fori_loop(0, ND, body, jnp.zeros((32, 128), F32))
        return jnp.sum(acc, axis=-1, keepdims=True) * (1.0 / 8192)

    average = row_total(lambda v: v)
    inverse = lax.rsqrt(row_total(lambda v: (v - average) * (v - average)) + 1e-06)
    stats[0] = wide(average)
    stats[1] = wide(inverse)
    stats[2] = jnp.zeros((32, 128), F32)
    stats[3] = jnp.zeros((32, 128), F32)

    def xhat(t):
        return (tok[:, t].astype(F32) - stats[0, :, 0:1]) * stats[1, :, 0:1]

    @pl.loop(0, ND)
    def _(j):
        t = cols(j, dc)
        n[rows(0, 0, 0), t] = (xhat(t) * (1.0 + of_image(scale, t)) + of_image(shift, t)).astype(BF16)

    pl.semaphore_wait(barrier, len(peers))

    pending = []

    def half_rows(s, half):
        return n.at[pl.ds(slot(*s) * 32 + half * 16, 16)]

    def send(src, dst, to, halves=(0, 1)):
        for half in halves:
            sem = n_recv.at[slot(*dst) * 2 + half]
            cp = remote(half_rows(src, half), half_rows(dst, half), n_send.at[len(pending)], sem, to)
            cp.start()
            pending.append(cp)

    def span(piece, part):
        k = piece[0] * 2 + piece[1]
        if part == "whole":
            return 0, 2048, k
        if part == "first":
            return (1 - h) * 1024, 1024, k
        return h * 1024, 1024, 8 + LATE.index(piece)

    def place_of(s, cc, piece, part):
        start, width, _ = span(piece, part)
        r = pl.ds(s * 512 + slot(cc, *piece) * 32, 32)
        return cb.at[r, pl.ds(pl.multiple_of(start, 1024), width)]

    def columns_copy(d, piece, part):
        start, width, k = span(piece, part)
        start = lax.rem(y + d, 4) * 2048 + start
        src = n.at[rows(0, *piece), pl.ds(pl.multiple_of(start, 1024), width)]
        dst = place_of(4 - d, 0, piece, part)
        return remote(src, dst, c_send.at[d - 1, k], c_recv.at[3 - d, k], group[d])

    sent = []

    def exchange(piece, part):
        for d in (2, 1, 3):
            cp = columns_copy(d, piece, part)
            cp.start()
            if part != "second":
                sent.append(cp)

    moved = []

    def pass_on(pieces, part):
        now = []
        for piece in pieces:
            k = span(piece, part)[2]
            for s in (1, 2, 3):
                src = place_of(s, 0, piece, part)
                landed(src, c_recv.at[s - 1, k])
                cp = remote(
                    src, place_of(s, 1, piece, part), f_send.at[s - 1, k], f_recv.at[s - 1, k], sib
                )
                cp.start()
                now.append(cp)
        moved.extend(now)
        return now

    def y_copy(d, q):
        r = cols(q, fc)
        return remote(
            gt.at[r, pl.ds(0, 512)],
            gt.at[r, pl.ds((4 - d) * 512, 512)],
            y_send.at[d // 2, q],
            y_recv.at[3 - d, q],
            group[d],
        )

    def y_relay(d, q):
        half = d // 2
        r = pl.ds(pl.multiple_of(q * fc + half * (fc // 2), fc // 2), fc // 2)
        return remote(
            gt.at[r, pl.ds((4 - d) * 512, 512)],
            gt.at[r, pl.ds(1024, 512)],
            y_send.at[2 + half, q],
            y_recv.at[1 if half == 0 else 3, q],
            group[d],
        )

    def y_start(q):
        for d in (1, 3):
            y_copy(d, q).start()

    def y_pass(q):
        for d in (1, 3):
            landed(gt.at[cols(q, fc), pl.ds((4 - d) * 512, 512)], y_recv.at[3 - d, q])
            y_relay(d, q).start()

    def arrived(s, halves=(0, 1)):
        for half in halves:
            landed(half_rows(s, half), n_recv.at[slot(*s) * 2 + half])

    def block(pieces, last=False):
        for piece in pieces:
            arrived((1, *piece))
        at = [rows(cc, *piece) for cc in (0, 1) for piece in pieces]

        @pl.loop(0, 2)
        def _(j):
            t = cols(j, 512)
            x = jnp.concatenate([n[r, :] for r in at], axis=0)
            pre = jnp.dot(x, w[:, t], preferred_element_type=F32) + bias[:, t].astype(F32)
            up = jnp.concatenate([g[r, t] for r in at], axis=0).astype(F32)
            sq = pre * pre
            th = jnp.tanh(GELU_A * pre * (1.0 + GELU_B * sq))
            slope = 0.5 * (1.0 + th) + 0.5 * GELU_A * pre * (1.0 - th * th) * (1.0 + 3.0 * GELU_B * sq)
            grad = (up * slope).astype(BF16)
            for k, r in enumerate(at):
                g[r, t] = grad[k * 32 : k * 32 + 32]
            if last:
                gt[t, 0:512] = g[:, t].T

                @pl.when(j == 0)
                def _():
                    y_start(0)
                    y_start(1)
                    y_start(2)

    own, near_pair = (0, 0, 0), (0, 0, 1)
    send(own, (0, 3, 0), ring[1], (0,))
    send(own, (0, 1, 0), ring[3], (1,))
    send(own, (0, 0, 1), pair)
    send(own, (0, 3, 0), ring[1], (1,))
    send(own, (0, 1, 0), ring[3], (0,))
    send(own, (1, 0, 0), sib)
    exchange((0, 0), "whole")

    def ring_piece(ll, part):
        arrived((0, 3, ll), (0,))
        send((0, 3, ll), (0, 2, ll), ring[1], (0,))
        arrived((0, 1, ll), (1,))
        send((0, 1, ll), (0, 2, ll), ring[3], (1,))
        if ll == 0:
            arrived(near_pair, (1,))
            send(near_pair, (0, 1, 1), ring[3], (1,))
            send(near_pair, (0, 3, 1), ring[1], (1,))
            send(near_pair, (1, 0, 1), sib)
            exchange((0, 1), "whole")
        arrived((0, 3, ll), (1,))
        arrived((0, 1, ll), (0,))
        for zz in (3, 1):
            send((0, zz, ll), (1, zz, ll), sib)
            exchange((zz, ll), part)

    def opposite_piece(ll):
        arrived((0, 2, ll))
        send((0, 2, ll), (1, 2, ll), sib)
        exchange((2, ll), "first")

    arrived(near_pair, (0,))
    send(near_pair, (0, 3, 1), ring[1], (0,))
    send(near_pair, (0, 1, 1), ring[3], (0,))
    ring_piece(0, "whole")
    for cp in loads[3:]:
        cp.wait()
    block(((0, 0), (0, 1)))
    block(((3, 0), (1, 0)))
    ring_piece(1, "first")
    opposite_piece(0)
    block(((3, 1), (1, 1)))
    opposite_piece(1)
    pass_on(SOON, "whole")
    block(((2, 0), (2, 1)), last=True)
    own_columns = pltpu.make_async_copy(n.at[:, cols(y, 2048)], cb.at[pl.ds(0, 512)], own_sem)
    own_columns.start()

    def s_copy(j):
        k = lax.rem(j, 2)
        return remote(sb.at[k], share.at[pl.ds(2 * j, 2)], s_send.at[k], s_recv.at[j], sib)

    def z_copy(d, j):
        return remote(
            zs.at[pl.ds(d * 64, 64), cols(j, dc)],
            zr.at[3 - d, :, cols(j, dc)],
            z_send.at[d - 1, j],
            z_recv.at[3 - d, j],
            ring[d],
        )

    def core_sum(j):
        t = cols(j, dc)
        landed(share.at[pl.ds(2 * j, 2)], s_recv.at[j])
        theirs = share[pl.ds(2 * j, 2)].reshape(256, dc).astype(F32)
        zs[:, t] = (zs[:, t].astype(F32) + theirs).astype(BF16)
        for d in (2, 1, 3):
            z_copy(d, j).start()

    def normed_part(j):
        k = lax.rem(j, 2)

        @pl.when(j >= 2)
        def _():
            s_copy(j).wait_send()

        @pl.loop(0, dc // 512)
        def _(i):
            t = pl.ds(pl.multiple_of(j * dc + i * 512, 512), 512)
            p = lax.dot_general(g[...], w[t, :], (((1,), (1,)), ((), ())), preferred_element_type=F32)
            p = p.astype(BF16)
            zs[:, t] = p[0:256]
            sb[k, 0, :, cols(i, 512)] = p[256:384]
            sb[k, 1, :, cols(i, 512)] = p[384:512]

        s_copy(j).start()

        @pl.when(j >= 1)
        def _():
            core_sum(j - 1)

    def part(q):
        return (16 + q) % 19

    def x_copy(q):
        return remote(share.at[part(q)], xw.at[q], x_send.at[q], x_recv.at[q], cross)

    def l_copy(j):
        return remote(zs.at[pl.ds(32, 32), cols(j, dc)], xr.at[:, cols(j, dc)], l_send.at[j], l_recv.at[j], pair)

    def weight_tile(q, column):
        t = pl.ds(pl.multiple_of(column, 1024), 1024)
        return jnp.dot(gt[cols(q, fc), :], cb[:, t], preferred_element_type=F32).astype(BF16)

    def weight_first(q):
        for half in (0, 1):
            r = pl.ds(pl.multiple_of(q * fc + half * (fc // 2), fc // 2), fc // 2)
            landed(gt.at[r, pl.ds(1024, 512)], y_recv.at[1 + 2 * half, q])

        share[part(q)] = weight_tile(q, (1 - h) * 1024)
        x_copy(q).start()

    def weight_second(q):
        share[NF + q] = weight_tile(q, h * 1024)

    def out_copy(q):
        k = lax.rem(q, 2)
        return pltpu.make_async_copy(weight_grad.at[k], weight_hbm.at[:, cols(q, fc)], wo_sem.at[k])

    def weight_sum(q):
        landed(xw.at[q], x_recv.at[q])

        @pl.when(q >= 2)
        def _():
            out_copy(q - 2).wait()

        weight_grad[lax.rem(q, 2)] = (share[NF + q].astype(F32) + xw[q].astype(F32)).T.astype(BF16)
        out_copy(q).start()

    def z_sum(j):
        t = cols(j, dc)
        for s in range(3):
            landed(zr.at[s, :, t], z_recv.at[s, j])
        total = zs[0:64, t].astype(F32)
        for s in range(3):
            total += zr[s, :, t].astype(F32)
        keep[:, t] = total[0:32]
        zs[32:64, t] = total[32:64].astype(BF16)
        l_copy(j).start()

    def row_sum(j):
        t = cols(j, dc)
        landed(xr.at[:, t], l_recv.at[j])
        total = keep[:, t] + xr[:, t].astype(F32)
        keep[:, t] = total
        term[0, 0:1, t] = jnp.sum(total, axis=0, keepdims=True)
        hat = xhat(t)
        term[0, 1:2, t] = jnp.sum(total * hat, axis=0, keepdims=True)
        scaled = total * (1.0 + of_image(scale, t))
        stats[2] += lane_sums(scaled)
        stats[3] += lane_sums(scaled * hat)

    pl.loop(0, AHEAD - 1)(normed_part)
    y_pass(0)
    pass_on(LATE, "first")
    y_pass(1)
    normed_part(AHEAD - 1)
    own_columns.wait()
    for cp in moved:
        cp.wait()

    def step(q):
        weight_first(q)

        @pl.when(q + 2 < NF)
        def _():
            y_pass(q + 2)

        @pl.when(q + 3 < NF)
        def _():
            y_start(q + 3)

        j = AHEAD + 2 * q

        @pl.when(j < ND)
        def _():
            normed_part(j)

        @pl.when(j + 1 < ND)
        def _():
            normed_part(j + 1)

        @pl.when(q == (ND - AHEAD + 1) // 2)
        def _():
            core_sum(ND - 1)

    def rows_step(q):
        @pl.when(q >= 1)
        def _():
            z_sum(q - 1)

        @pl.when(q >= 2)
        def _():
            row_sum(q - 2)

    @pl.loop(0, 5)
    def _(q):
        step(q)
        for k, piece in enumerate(LATE):

            @pl.when(q == 1 + k)
            def _():
                exchange(piece, "second")

        rows_step(q)

    second = pass_on(LATE, "second")

    @pl.loop(5, NF)
    def _(q):
        step(q)

        @pl.when(q == 5)
        def _():
            for cp in second:
                cp.wait()

        for k in range(3):
            p = 3 * (q - 5) + k

            @pl.when(p < NF)
            def _():
                weight_second(p)

        rows_step(q)
        weight_sum(q - 5)

    z_sum(ND - 1)
    row_sum(ND - 2)
    row_sum(ND - 1)

    near = (peer()[0], z + 1 - 2 * lax.rem(z, 2), peer()[2])
    hops = [
        remote(term.at[k], trec.at[k], t_send.at[k], t_recv.at[k], to)
        for k, to in enumerate((sib, pair, near, ring[2]))
    ]
    hops[0].start()
    nt = (((1,), (1,)), ((), ()))
    bsum[...] = lax.dot_general(jnp.ones((8, 2048), BF16), gt[...], nt, preferred_element_type=F32)
    b_copy = remote(bsum, brec, b_send.at[0], b_recv.at[0], cross)
    b_copy.start()
    hops[0].wait_recv()
    term[1] = term[0] + trec[0]
    hops[1].start()

    stats[2] = wide(jnp.sum(stats[2], axis=-1, keepdims=True) * (1.0 / 8192))
    stats[3] = wide(jnp.sum(stats[3], axis=-1, keepdims=True) * (1.0 / 8192))

    @pl.loop(0, ND)
    def _(j):
        t = cols(j, dc)
        mean_one, mean_two = stats[2, :, 0:1], stats[3, :, 0:1]
        scaled = keep[:, t] * (1.0 + of_image(scale, t))
        xr[:, t] = (stats[1, :, 0:1] * (scaled - mean_one - xhat(t) * mean_two)).astype(BF16)

    outs = [
        pltpu.make_async_copy(src, dst, out_sem.at[k])
        for k, (src, dst) in enumerate(
            ((xr, token_hbm), (brec, sums_hbm), (shift_grad, shift_out), (scale_grad, scale_out))
        )
    ]
    outs[0].start()

    for k in (1, 2):
        hops[k].wait_recv()
        term[k + 1] = term[k] + trec[k]
        hops[k + 1].start()
        weight_sum(2 + k)
    b_copy.wait()
    brec[...] = bsum[...] + brec[...]
    outs[1].start()
    hops[3].wait_recv()
    first = (z < 2).astype(F32) > 0.5
    near_sum, far_sum = term[3], trec[3]
    shift_grad[0:1, :] = jnp.where(first, near_sum[0:1], far_sum[0:1])
    shift_grad[1:2, :] = jnp.where(first, far_sum[0:1], near_sum[0:1])
    scale_grad[0:1, :] = jnp.where(first, near_sum[1:2], far_sum[1:2])
    scale_grad[1:2, :] = jnp.where(first, far_sum[1:2], near_sum[1:2])
    outs[2].start()
    outs[3].start()
    for q in (5, 6, 7):
        weight_sum(q)

    for k in range(4):
        hops[k].wait_send()
    for cp in pending + sent + [columns_copy(d, piece, "second") for piece in LATE for d in (1, 2, 3)]:
        cp.wait_send()
    s_copy(0).wait_send()
    s_copy(1).wait_send()

    @pl.loop(0, NF)
    def _(q):
        for d in (1, 3):
            y_copy(d, q).wait_send()
            y_relay(d, q).wait_send()
        for d in (1, 2, 3):
            z_copy(d, q).wait_send()
        l_copy(q).wait_send()
        x_copy(q).wait_send()

    out_copy(NF - 2).wait()
    out_copy(NF - 1).wait()
    for cp in outs:
        cp.wait()


def result_kernel(a, b, c, d, e, ao, bo, co, do, eo, av, bv, cv, dv, ev, sem):
    held = (av, bv, cv, dv, ev)
    takes = [pltpu.make_async_copy(src, v, sem.at[k]) for k, (src, v) in enumerate(zip((a, b, c, d, e), held))]
    gives = [
        pltpu.make_async_copy(v, dst, sem.at[5 + k])
        for k, (v, dst) in enumerate(zip((av, bv, cv.at[0:1], dv, ev), (ao, bo, co, do, eo)))
    ]
    for cp in takes:
        cp.start()
    for cp, give in zip(takes, gives):
        cp.wait()
        give.start()
    for give in gives:
        give.wait()


def local(tokens, mod_shift, mod_scale, up_weight, up_bias, act_grad):
    vmem = pl.BlockSpec(memory_space=pltpu.VMEM)
    hbm = pl.BlockSpec(memory_space=pltpu.HBM)
    dma = pltpu.SemaphoreType.DMA
    results = (
        jax.ShapeDtypeStruct((32, 8192), BF16),
        jax.ShapeDtypeStruct((1024, 1024), BF16),
        jax.ShapeDtypeStruct((8, 1024), F32),
        jax.ShapeDtypeStruct((2, 8192), F32),
        jax.ShapeDtypeStruct((2, 8192), F32),
    )
    parts = pl.pallas_call(
        block_kernel,
        out_shape=results,
        in_specs=[hbm] * 6,
        out_specs=(hbm,) * 5,
        scratch_shapes=[
            pltpu.VMEM((32, 8192), BF16),
            pltpu.VMEM((2, 8192), BF16),
            pltpu.VMEM((2, 8192), BF16),
            pltpu.VMEM((1, 1024), BF16),
            pltpu.VMEM((512, 8192), BF16),
            pltpu.VMEM((2048, 2048), BF16),
            pltpu.VMEM((8192, 1024), BF16),
            pltpu.VMEM((512, 1024), BF16),
            pltpu.VMEM((1024, 2048), BF16),
            pltpu.VMEM((2, 2, 128, 1024), BF16),
            pltpu.VMEM((19, 128, 1024), BF16),
            pltpu.VMEM((256, 8192), BF16),
            pltpu.VMEM((3, 64, 8192), BF16),
            pltpu.VMEM((32, 8192), BF16),
            pltpu.VMEM((32, 8192), F32),
            pltpu.VMEM((4, 32, 128), F32),
            pltpu.VMEM((NF, 128, 1024), BF16),
            pltpu.VMEM((8, 1024), F32),
            pltpu.VMEM((8, 1024), F32),
            pltpu.VMEM((4, 2, 8192), F32),
            pltpu.VMEM((4, 2, 8192), F32),
            pltpu.VMEM((2, 1024, 128), BF16),
            pltpu.VMEM((2, 8192), F32),
            pltpu.VMEM((2, 8192), F32),
            dma((21,)),
            dma((4,)),
            dma((2,)),
            dma(()),
            dma((32,)),
            dma((32,)),
            dma((3, 12)),
            dma((3, 12)),
            dma((3, 12)),
            dma((3, 12)),
            dma((4, NF)),
            dma((4, NF)),
            dma((2,)),
            dma((ND,)),
            dma((3, ND)),
            dma((3, ND)),
            dma((ND,)),
            dma((ND,)),
            dma((NF,)),
            dma((NF,)),
            dma((1,)),
            dma((1,)),
            dma((4,)),
            dma((4,)),
        ],
        compiler_params=pltpu.CompilerParams(
            collective_id=0, has_side_effects=True, vmem_limit_bytes=61 * MIB
        ),
        name="block",
    )(tokens, mod_shift, mod_scale, up_weight, up_bias[None, :], act_grad)
    final = list(results)
    final[2] = jax.ShapeDtypeStruct((1, 1024), F32)
    token_grad, weight_grad, bias_grad, shift_grad, scale_grad = pl.pallas_call(
        result_kernel,
        out_shape=tuple(final),
        in_specs=[hbm] * 5,
        out_specs=(hbm,) * 5,
        scratch_shapes=[pltpu.VMEM(r.shape, r.dtype) for r in results] + [dma((10,))],
        compiler_params=pltpu.CompilerParams(vmem_limit_bytes=61 * MIB),
        name="results",
    )(*parts)
    return token_grad, weight_grad, bias_grad.reshape(1024), shift_grad, scale_grad


def solution(mesh):
    return jax.shard_map(
        local,
        mesh=mesh,
        in_specs=(
            P(("dp", "tx", "ty"), None),
            P("dp", None),
            P("dp", None),
            P(None, ("tx", "ty")),
            P(("tx", "ty")),
            P("dp", ("tx", "ty")),
        ),
        out_specs=(
            P(("dp", "tx", "ty"), None),
            P("dp", ("tx", "ty")),
            P(("tx", "ty")),
            P("dp", None),
            P("dp", None),
        ),
        check_vma=False,
    )
```

```python
import jax
import jax.numpy as jnp
from jax import lax
from jax.experimental import pallas as pl
from jax.experimental.pallas import tpu as pltpu
from jax.sharding import PartitionSpec as P

MESH = pl.DeviceIdType.MESH
MIB = 1 << 20
F32 = jnp.float32
BF16 = jnp.bfloat16
GELU_A = 0.7978845608028654
GELU_B = 0.044715


def place():
    dp, tx, ty = (lax.axis_index(a) for a in ("dp", "tx", "ty"))
    return dp // 2, dp % 2, tx, ty // 2, ty % 2


def peer(dy=0, dh=0, dz=0, dl=0, dc=0):
    y, h, z, l, c = place()
    return (
        lax.rem(y + dy, 4) * 2 + lax.rem(h + dh, 2),
        lax.rem(z + dz, 4),
        lax.rem(l + dl, 2) * 2 + lax.rem(c + dc, 2),
    )


def remote(src, dst, send, recv, to):
    return pltpu.make_async_remote_copy(
        src_ref=src, dst_ref=dst, send_sem=send, recv_sem=recv, device_id=to, device_id_type=MESH
    )


def landed(ref, sem):
    pltpu.make_async_copy(ref, ref, sem).wait()


def cols(i, n):
    return pl.ds(pl.multiple_of(i * n, n), n)


def lane_sums(x):
    parts = [x[:, k : k + 128] for k in range(0, x.shape[1], 128)]
    while len(parts) > 1:
        parts = [a + b for a, b in zip(parts[::2], parts[1::2])]
    return parts[0]


def wide(x):
    return jnp.broadcast_to(x, (32, 128))


def slot(c, z, l):
    return c * 8 + z * 2 + l


def rows(c, z, l):
    return pl.ds(slot(c, z, l) * 32, 32)


SOON = ((0, 0), (0, 1), (3, 0), (1, 0))
LATE = ((3, 1), (1, 1), (2, 0), (2, 1))
NF = 8
ND = 8
BLOCKS = (((0, 0), (0, 1)), ((3, 0), (1, 0)), ((3, 1), (1, 1)), ((2, 0), (2, 1)))


def block_kernel(
    tok_hbm, shift_hbm, scale_hbm, w_hbm, bias_hbm, act_hbm,
    token_hbm, weight_hbm, sums_hbm, shift_out, scale_out,
    tok, shift, scale, bias, n, cb, w, g, gt, sb, share, zs, zr, xr, keep, stats,
    xw, bsum, brec, term, trec, weight_grad, shift_grad, scale_grad,
    in_sem, out_sem, wo_sem, own_sem, n_send, n_recv, c_send, c_recv, f_send, f_recv,
    y_send, y_recv, s_send, s_recv, zw_send, zw_recv, z_send, z_recv, l_send, l_recv, x_send, x_recv,
    b_send, b_recv, t_send, t_recv,
):
    y, h, z, l, c = place()
    sib = peer(dc=1)
    pair = peer(dl=1)
    ring = {d: peer(dz=d) for d in (1, 2, 3)}
    group = {d: peer(dy=d) for d in (1, 2, 3)}
    cross = peer(dh=1)
    fc, dc = 1024 // NF, 8192 // ND

    loads = [
        pltpu.make_async_copy(src, dst, in_sem.at[k])
        for k, (src, dst) in enumerate(
            ((tok_hbm, tok), (shift_hbm, shift), (scale_hbm, scale), (bias_hbm, bias), (w_hbm, w))
        )
    ]
    for cc in (0, 1):
        for zz in range(4):
            for ll in (0, 1):
                r = (lax.rem(z + zz, 4) * 4 + lax.rem(l + ll, 2) * 2 + lax.rem(c + cc, 2)) * 32
                src = act_hbm.at[pl.ds(pl.multiple_of(r, 32), 32)]
                loads.append(pltpu.make_async_copy(src, g.at[rows(cc, zz, ll)], in_sem.at[len(loads)]))
    for cp in loads:
        cp.start()
    peers = [sib, pair, *ring.values(), *group.values(), cross]
    barrier = pltpu.get_barrier_semaphore()
    for p in peers:
        pl.semaphore_signal(barrier, inc=1, device_id=p, device_id_type=MESH)
    for cp in loads[:3]:
        cp.wait()

    def of_image(ref, t):
        m = ref[:, t].astype(F32)
        return jnp.where((z < 2).astype(F32) > 0.5, m[0:1], m[1:2])

    def row_total(f):
        def body(j, acc):
            return acc + lane_sums(f(tok[:, cols(j, dc)].astype(F32)))

        acc = lax.fori_loop(0, ND, body, jnp.zeros((32, 128), F32))
        return jnp.sum(acc, axis=-1, keepdims=True) * (1.0 / 8192)

    average = row_total(lambda v: v)
    inverse = lax.rsqrt(row_total(lambda v: (v - average) * (v - average)) + 1e-06)
    stats[0] = wide(average)
    stats[1] = wide(inverse)
    stats[2] = jnp.zeros((32, 128), F32)
    stats[3] = jnp.zeros((32, 128), F32)

    def xhat(t):
        return (tok[:, t].astype(F32) - stats[0, :, 0:1]) * stats[1, :, 0:1]

    @pl.loop(0, ND)
    def _(j):
        t = cols(j, dc)
        n[rows(0, 0, 0), t] = (xhat(t) * (1.0 + of_image(scale, t)) + of_image(shift, t)).astype(BF16)

    pl.semaphore_wait(barrier, len(peers))

    pending = []

    def half_rows(s, half):
        return n.at[pl.ds(slot(*s) * 32 + half * 16, 16)]

    def send(src, dst, to, halves=(0, 1)):
        for half in halves:
            sem = n_recv.at[slot(*dst) * 2 + half]
            cp = remote(half_rows(src, half), half_rows(dst, half), n_send.at[len(pending)], sem, to)
            cp.start()
            pending.append(cp)

    def span(piece, part):
        k = piece[0] * 2 + piece[1]
        if part == "whole":
            return 0, 2048, k
        if part == "first":
            return (1 - h) * 1024, 1024, k
        return h * 1024, 1024, 8 + LATE.index(piece)

    def place_of(s, cc, piece, part):
        start, width, _ = span(piece, part)
        r = pl.ds(s * 512 + slot(cc, *piece) * 32, 32)
        return cb.at[r, pl.ds(pl.multiple_of(start, 1024), width)]

    def columns_copy(d, piece, part):
        start, width, k = span(piece, part)
        start = lax.rem(y + d, 4) * 2048 + start
        src = n.at[rows(0, *piece), pl.ds(pl.multiple_of(start, 1024), width)]
        dst = place_of(4 - d, 0, piece, part)
        return remote(src, dst, c_send.at[d - 1, k], c_recv.at[3 - d, k], group[d])

    sent = []

    def exchange(piece, part):
        for d in (2, 1, 3):
            cp = columns_copy(d, piece, part)
            cp.start()
            if part != "second":
                sent.append(cp)

    moved = []

    def pass_on(pieces, part):
        now = []
        for piece in pieces:
            k = span(piece, part)[2]
            for s in (1, 2, 3):
                src = place_of(s, 0, piece, part)
                landed(src, c_recv.at[s - 1, k])
                cp = remote(
                    src, place_of(s, 1, piece, part), f_send.at[s - 1, k], f_recv.at[s - 1, k], sib
                )
                cp.start()
                now.append(cp)
        moved.extend(now)
        return now

    def y_copy(d, q):
        r = cols(q, fc)
        return remote(
            gt.at[r, pl.ds(0, 512)],
            gt.at[r, pl.ds((4 - d) * 512, 512)],
            y_send.at[d // 2, q],
            y_recv.at[3 - d, q],
            group[d],
        )

    def y_relay(d, q):
        half = d // 2
        r = pl.ds(pl.multiple_of(q * fc + half * (fc // 2), fc // 2), fc // 2)
        return remote(
            gt.at[r, pl.ds((4 - d) * 512, 512)],
            gt.at[r, pl.ds(1024, 512)],
            y_send.at[2 + half, q],
            y_recv.at[1 if half == 0 else 3, q],
            group[d],
        )

    def y_start(q):
        for d in (1, 3):
            y_copy(d, q).start()

    def y_pass(q):
        for d in (1, 3):
            landed(gt.at[cols(q, fc), pl.ds((4 - d) * 512, 512)], y_recv.at[3 - d, q])
            y_relay(d, q).start()

    def arrived(s, halves=(0, 1)):
        for half in halves:
            landed(half_rows(s, half), n_recv.at[slot(*s) * 2 + half])

    def block(pieces, last=False):
        for piece in pieces:
            arrived((1, *piece))
        at = [rows(cc, *piece) for cc in (0, 1) for piece in pieces]

        @pl.loop(0, 2)
        def _(j):
            t = cols(j, 512)
            x = jnp.concatenate([n[r, :] for r in at], axis=0)
            pre = jnp.dot(x, w[:, t], preferred_element_type=F32) + bias[:, t].astype(F32)
            up = jnp.concatenate([g[r, t] for r in at], axis=0).astype(F32)
            sq = pre * pre
            th = jnp.tanh(GELU_A * pre * (1.0 + GELU_B * sq))
            slope = 0.5 * (1.0 + th) + 0.5 * GELU_A * pre * (1.0 - th * th) * (1.0 + 3.0 * GELU_B * sq)
            grad = (up * slope).astype(BF16)
            for k, r in enumerate(at):
                g[r, t] = grad[k * 32 : k * 32 + 32]
            if last:
                gt[t, 0:512] = g[:, t].T

                @pl.when(j == 0)
                def _():
                    y_start(0)
                    y_start(1)
                    y_start(2)

    def s_copy(b, j):
        there = share.at[2 * j + b // 2, pl.ds((b % 2) * 64, 64)]
        return remote(sb.at[j], there, s_send.at[j], s_recv.at[b, j], sib)

    def z_whole(zz, ll):
        k = (zz // 2) * 2 + ll
        there = zr.at[3 - zz, pl.ds(ll * 32, 32)]
        return remote(zs.at[rows(0, zz, ll)], there, zw_send.at[k], zw_recv.at[k], ring[zz])

    def z_far(j):
        t = cols(j, dc)
        return remote(zs.at[pl.ds(128, 64), t], zr.at[1, :, t], z_send.at[j], z_recv.at[j], ring[2])

    def core_sum(b, j):
        t = cols(j, dc)
        unit, first_row = 2 * j + b // 2, (b % 2) * 64
        landed(share.at[unit, pl.ds(first_row, 64)], s_recv.at[b, j])
        for k, piece in enumerate(BLOCKS[b]):
            theirs = share[unit, first_row + k * 32 : first_row + k * 32 + 32].astype(F32)
            zs[rows(0, *piece), t] = (zs[rows(0, *piece), t].astype(F32) + theirs).astype(BF16)
        if b == 3:
            z_far(j).start()

    def normed(b):
        at = [rows(cc, *piece) for cc in (0, 1) for piece in BLOCKS[b]]

        @pl.loop(0, ND)
        def _(j):
            if b > 0:
                s_copy(b - 1, j).wait_send()

            @pl.loop(0, dc // 512)
            def _(i):
                t = pl.ds(pl.multiple_of(j * dc + i * 512, 512), 512)
                x = jnp.concatenate([g[r, :] for r in at], axis=0)
                p = lax.dot_general(x, w[t, :], (((1,), (1,)), ((), ())), preferred_element_type=F32)
                p = p.astype(BF16)
                for k, piece in enumerate(BLOCKS[b]):
                    zs[rows(0, *piece), t] = p[k * 32 : k * 32 + 32]
                sb[j, :, cols(i, 512)] = p[64:128]

            s_copy(b, j).start()

            @pl.when(j >= 1)
            def _():
                core_sum(b, j - 1)

        core_sum(b, ND - 1)

    own, near_pair = (0, 0, 0), (0, 0, 1)
    send(own, (0, 3, 0), ring[1], (0,))
    send(own, (0, 1, 0), ring[3], (1,))
    send(own, (0, 0, 1), pair)
    send(own, (0, 3, 0), ring[1], (1,))
    send(own, (0, 1, 0), ring[3], (0,))
    send(own, (1, 0, 0), sib)
    exchange((0, 0), "whole")

    def ring_piece(ll):
        arrived((0, 3, ll), (0,))
        send((0, 3, ll), (0, 2, ll), ring[1], (0,))
        arrived((0, 1, ll), (1,))
        send((0, 1, ll), (0, 2, ll), ring[3], (1,))

    def ring_rest(ll, part):
        if ll == 0:
            arrived(near_pair, (1,))
            send(near_pair, (0, 1, 1), ring[3], (1,))
            send(near_pair, (0, 3, 1), ring[1], (1,))
            send(near_pair, (1, 0, 1), sib)
            exchange((0, 1), "whole")
        arrived((0, 3, ll), (1,))
        arrived((0, 1, ll), (0,))
        for zz in (3, 1):
            send((0, zz, ll), (1, zz, ll), sib)
            exchange((zz, ll), part)

    def opposite_piece(ll):
        arrived((0, 2, ll))
        send((0, 2, ll), (1, 2, ll), sib)
        exchange((2, ll), "first")

    arrived(near_pair, (0,))
    send(near_pair, (0, 3, 1), ring[1], (0,))
    send(near_pair, (0, 1, 1), ring[3], (0,))
    ring_piece(0)
    ring_rest(0, "whole")
    for cp in loads[3:]:
        cp.wait()
    block(BLOCKS[0])
    block(BLOCKS[1])
    ring_piece(1)
    normed(0)
    normed(1)
    ring_rest(1, "first")
    opposite_piece(0)
    block(BLOCKS[2])
    opposite_piece(1)
    z_whole(3, 0).start()
    z_whole(1, 0).start()
    pass_on(SOON, "whole")
    block(BLOCKS[3], last=True)
    own_columns = pltpu.make_async_copy(n.at[:, cols(y, 2048)], cb.at[pl.ds(0, 512)], own_sem)
    own_columns.start()

    def part(q):
        return (16 + q) % 19

    def x_copy(q):
        return remote(share.at[part(q)], xw.at[q], x_send.at[q], x_recv.at[q], cross)

    def l_copy(j):
        return remote(zs.at[pl.ds(32, 32), cols(j, dc)], xr.at[:, cols(j, dc)], l_send.at[j], l_recv.at[j], pair)

    def weight_tile(q, column):
        t = pl.ds(pl.multiple_of(column, 1024), 1024)
        return jnp.dot(gt[cols(q, fc), :], cb[:, t], preferred_element_type=F32).astype(BF16)

    def weight_first(q):
        for half in (0, 1):
            r = pl.ds(pl.multiple_of(q * fc + half * (fc // 2), fc // 2), fc // 2)
            landed(gt.at[r, pl.ds(1024, 512)], y_recv.at[1 + 2 * half, q])

        share[part(q)] = weight_tile(q, (1 - h) * 1024)
        x_copy(q).start()

    def weight_second(q):
        share[NF + q] = weight_tile(q, h * 1024)

    def out_copy(q):
        k = lax.rem(q, 2)
        return pltpu.make_async_copy(weight_grad.at[k], weight_hbm.at[:, cols(q, fc)], wo_sem.at[k])

    def weight_sum(q):
        landed(xw.at[q], x_recv.at[q])

        @pl.when(q >= 2)
        def _():
            out_copy(q - 2).wait()

        weight_grad[lax.rem(q, 2)] = (share[NF + q].astype(F32) + xw[q].astype(F32)).T.astype(BF16)
        out_copy(q).start()

    def z_sum(j):
        t = cols(j, dc)
        landed(zr.at[1, :, t], z_recv.at[j])
        total = zs[0:64, t].astype(F32)
        for s in range(3):
            total += zr[s, :, t].astype(F32)
        keep[:, t] = total[0:32]
        zs[32:64, t] = total[32:64].astype(BF16)
        l_copy(j).start()

    def row_sum(j):
        t = cols(j, dc)
        landed(xr.at[:, t], l_recv.at[j])
        total = keep[:, t] + xr[:, t].astype(F32)
        keep[:, t] = total
        term[0, 0:1, t] = jnp.sum(total, axis=0, keepdims=True)
        hat = xhat(t)
        term[0, 1:2, t] = jnp.sum(total * hat, axis=0, keepdims=True)
        scaled = total * (1.0 + of_image(scale, t))
        stats[2] += lane_sums(scaled)
        stats[3] += lane_sums(scaled * hat)

    normed(2)
    z_whole(3, 1).start()
    z_whole(1, 1).start()
    y_pass(0)
    pass_on(LATE, "first")
    normed(3)
    y_pass(1)
    own_columns.wait()
    for cp in moved:
        cp.wait()

    def step(q):
        weight_first(q)

        @pl.when(q + 2 < NF)
        def _():
            y_pass(q + 2)

        @pl.when(q + 3 < NF)
        def _():
            y_start(q + 3)

    def rows_step(q):
        @pl.when(q == 3)
        def _():
            for zz in (1, 3):
                for ll in (0, 1):
                    landed(zr.at[3 - zz, pl.ds(ll * 32, 32)], zw_recv.at[(zz // 2) * 2 + ll])

        @pl.when((q >= 3) & (q <= 6))
        def _():
            z_sum(2 * q - 6)
            z_sum(2 * q - 5)

        @pl.when(q >= 4)
        def _():
            row_sum(2 * q - 8)
            row_sum(2 * q - 7)

    @pl.loop(0, 5)
    def _(q):
        step(q)
        for k, piece in enumerate(LATE):

            @pl.when(q == 1 + k)
            def _():
                exchange(piece, "second")

        rows_step(q)

    second = pass_on(LATE, "second")

    @pl.loop(5, NF)
    def _(q):
        step(q)

        @pl.when(q == 5)
        def _():
            for cp in second:
                cp.wait()

        for k in range(3):
            p = 3 * (q - 5) + k

            @pl.when(p < NF)
            def _():
                weight_second(p)

        rows_step(q)
        weight_sum(q - 5)


    near = (peer()[0], z + 1 - 2 * lax.rem(z, 2), peer()[2])
    hops = [
        remote(term.at[k], trec.at[k], t_send.at[k], t_recv.at[k], to)
        for k, to in enumerate((sib, pair, near, ring[2]))
    ]
    hops[0].start()
    nt = (((1,), (1,)), ((), ()))
    bsum[...] = lax.dot_general(jnp.ones((8, 2048), BF16), gt[...], nt, preferred_element_type=F32)
    b_copy = remote(bsum, brec, b_send.at[0], b_recv.at[0], cross)
    b_copy.start()
    hops[0].wait_recv()
    term[1] = term[0] + trec[0]
    hops[1].start()

    stats[2] = wide(jnp.sum(stats[2], axis=-1, keepdims=True) * (1.0 / 8192))
    stats[3] = wide(jnp.sum(stats[3], axis=-1, keepdims=True) * (1.0 / 8192))

    @pl.loop(0, ND)
    def _(j):
        t = cols(j, dc)
        mean_one, mean_two = stats[2, :, 0:1], stats[3, :, 0:1]
        scaled = keep[:, t] * (1.0 + of_image(scale, t))
        xr[:, t] = (stats[1, :, 0:1] * (scaled - mean_one - xhat(t) * mean_two)).astype(BF16)

    outs = [
        pltpu.make_async_copy(src, dst, out_sem.at[k])
        for k, (src, dst) in enumerate(
            ((xr, token_hbm), (brec, sums_hbm), (shift_grad, shift_out), (scale_grad, scale_out))
        )
    ]
    outs[0].start()

    for k in (1, 2):
        hops[k].wait_recv()
        term[k + 1] = term[k] + trec[k]
        hops[k + 1].start()
        weight_sum(2 + k)
    b_copy.wait()
    brec[...] = bsum[...] + brec[...]
    outs[1].start()
    hops[3].wait_recv()
    first = (z < 2).astype(F32) > 0.5
    near_sum, far_sum = term[3], trec[3]
    shift_grad[0:1, :] = jnp.where(first, near_sum[0:1], far_sum[0:1])
    shift_grad[1:2, :] = jnp.where(first, far_sum[0:1], near_sum[0:1])
    scale_grad[0:1, :] = jnp.where(first, near_sum[1:2], far_sum[1:2])
    scale_grad[1:2, :] = jnp.where(first, far_sum[1:2], near_sum[1:2])
    outs[2].start()
    outs[3].start()
    for q in (5, 6, 7):
        weight_sum(q)

    for k in range(4):
        hops[k].wait_send()
    for cp in pending + sent + [columns_copy(d, piece, "second") for piece in LATE for d in (1, 2, 3)]:
        cp.wait_send()
    for zz in (1, 3):
        for ll in (0, 1):
            z_whole(zz, ll).wait_send()

    @pl.loop(0, NF)
    def _(q):
        for d in (1, 3):
            y_copy(d, q).wait_send()
            y_relay(d, q).wait_send()
        z_far(q).wait_send()
        s_copy(3, q).wait_send()
        l_copy(q).wait_send()
        x_copy(q).wait_send()

    out_copy(NF - 2).wait()
    out_copy(NF - 1).wait()
    for cp in outs:
        cp.wait()


def result_kernel(a, b, c, d, e, ao, bo, co, do, eo, av, bv, cv, dv, ev, sem):
    held = (av, bv, cv, dv, ev)
    takes = [pltpu.make_async_copy(src, v, sem.at[k]) for k, (src, v) in enumerate(zip((a, b, c, d, e), held))]
    gives = [
        pltpu.make_async_copy(v, dst, sem.at[5 + k])
        for k, (v, dst) in enumerate(zip((av, bv, cv.at[0:1], dv, ev), (ao, bo, co, do, eo)))
    ]
    for cp in takes:
        cp.start()
    for cp, give in zip(takes, gives):
        cp.wait()
        give.start()
    for give in gives:
        give.wait()


def local(tokens, mod_shift, mod_scale, up_weight, up_bias, act_grad):
    vmem = pl.BlockSpec(memory_space=pltpu.VMEM)
    hbm = pl.BlockSpec(memory_space=pltpu.HBM)
    dma = pltpu.SemaphoreType.DMA
    results = (
        jax.ShapeDtypeStruct((32, 8192), BF16),
        jax.ShapeDtypeStruct((1024, 1024), BF16),
        jax.ShapeDtypeStruct((8, 1024), F32),
        jax.ShapeDtypeStruct((2, 8192), F32),
        jax.ShapeDtypeStruct((2, 8192), F32),
    )
    parts = pl.pallas_call(
        block_kernel,
        out_shape=results,
        in_specs=[hbm] * 6,
        out_specs=(hbm,) * 5,
        scratch_shapes=[
            pltpu.VMEM((32, 8192), BF16),
            pltpu.VMEM((2, 8192), BF16),
            pltpu.VMEM((2, 8192), BF16),
            pltpu.VMEM((1, 1024), BF16),
            pltpu.VMEM((512, 8192), BF16),
            pltpu.VMEM((2048, 2048), BF16),
            pltpu.VMEM((8192, 1024), BF16),
            pltpu.VMEM((512, 1024), BF16),
            pltpu.VMEM((1024, 2048), BF16),
            pltpu.VMEM((ND, 64, 1024), BF16),
            pltpu.VMEM((19, 128, 1024), BF16),
            pltpu.VMEM((256, 8192), BF16),
            pltpu.VMEM((3, 64, 8192), BF16),
            pltpu.VMEM((32, 8192), BF16),
            pltpu.VMEM((32, 8192), F32),
            pltpu.VMEM((4, 32, 128), F32),
            pltpu.VMEM((NF, 128, 1024), BF16),
            pltpu.VMEM((8, 1024), F32),
            pltpu.VMEM((8, 1024), F32),
            pltpu.VMEM((4, 2, 8192), F32),
            pltpu.VMEM((4, 2, 8192), F32),
            pltpu.VMEM((2, 1024, 128), BF16),
            pltpu.VMEM((2, 8192), F32),
            pltpu.VMEM((2, 8192), F32),
            dma((21,)),
            dma((4,)),
            dma((2,)),
            dma(()),
            dma((32,)),
            dma((32,)),
            dma((3, 12)),
            dma((3, 12)),
            dma((3, 12)),
            dma((3, 12)),
            dma((4, NF)),
            dma((4, NF)),
            dma((ND,)),
            dma((4, ND)),
            dma((4,)),
            dma((4,)),
            dma((ND,)),
            dma((ND,)),
            dma((ND,)),
            dma((ND,)),
            dma((NF,)),
            dma((NF,)),
            dma((1,)),
            dma((1,)),
            dma((4,)),
            dma((4,)),
        ],
        compiler_params=pltpu.CompilerParams(
            collective_id=0, has_side_effects=True, vmem_limit_bytes=61 * MIB
        ),
        name="block",
    )(tokens, mod_shift, mod_scale, up_weight, up_bias[None, :], act_grad)
    final = list(results)
    final[2] = jax.ShapeDtypeStruct((1, 1024), F32)
    token_grad, weight_grad, bias_grad, shift_grad, scale_grad = pl.pallas_call(
        result_kernel,
        out_shape=tuple(final),
        in_specs=[hbm] * 5,
        out_specs=(hbm,) * 5,
        scratch_shapes=[pltpu.VMEM(r.shape, r.dtype) for r in results] + [dma((10,))],
        compiler_params=pltpu.CompilerParams(vmem_limit_bytes=61 * MIB),
        name="results",
    )(*parts)
    return token_grad, weight_grad, bias_grad.reshape(1024), shift_grad, scale_grad


def solution(mesh):
    return jax.shard_map(
        local,
        mesh=mesh,
        in_specs=(
            P(("dp", "tx", "ty"), None),
            P("dp", None),
            P("dp", None),
            P(None, ("tx", "ty")),
            P(("tx", "ty")),
            P("dp", ("tx", "ty")),
        ),
        out_specs=(
            P(("dp", "tx", "ty"), None),
            P("dp", ("tx", "ty")),
            P(("tx", "ty")),
            P("dp", None),
            P("dp", None),
        ),
        check_vma=False,
    )
```

```python
import jax
import jax.numpy as jnp
from jax import lax
from jax.experimental import pallas as pl
from jax.experimental.pallas import tpu as pltpu
from jax.sharding import PartitionSpec as P

MESH = pl.DeviceIdType.MESH
MIB = 1 << 20
F32 = jnp.float32
BF16 = jnp.bfloat16
GELU_A = 0.7978845608028654
GELU_B = 0.044715


def place():
    dp, tx, ty = (lax.axis_index(a) for a in ("dp", "tx", "ty"))
    return dp // 2, dp % 2, tx, ty // 2, ty % 2


def peer(dy=0, dh=0, dz=0, dl=0, dc=0):
    y, h, z, l, c = place()
    return (
        lax.rem(y + dy, 4) * 2 + lax.rem(h + dh, 2),
        lax.rem(z + dz, 4),
        lax.rem(l + dl, 2) * 2 + lax.rem(c + dc, 2),
    )


def remote(src, dst, send, recv, to):
    return pltpu.make_async_remote_copy(
        src_ref=src, dst_ref=dst, send_sem=send, recv_sem=recv, device_id=to, device_id_type=MESH
    )


def landed(ref, sem):
    pltpu.make_async_copy(ref, ref, sem).wait()


def cols(i, n):
    return pl.ds(pl.multiple_of(i * n, n), n)


def lane_sums(x):
    parts = [x[:, k : k + 128] for k in range(0, x.shape[1], 128)]
    while len(parts) > 1:
        parts = [a + b for a, b in zip(parts[::2], parts[1::2])]
    return parts[0]


def wide(x):
    return jnp.broadcast_to(x, (32, 128))


def slot(c, z, l):
    return c * 8 + z * 2 + l


def rows(c, z, l):
    return pl.ds(slot(c, z, l) * 32, 32)


SOON = ((0, 0), (0, 1), (3, 0), (1, 0))
LATE = ((3, 1), (1, 1), (2, 0), (2, 1))
BLOCKS = (((0, 0), (0, 1)), ((3, 0), (1, 0)), ((3, 1), (1, 1)), ((2, 0), (2, 1)))
HALVES = (BLOCKS[0] + BLOCKS[1], BLOCKS[2] + BLOCKS[3])
NF = 8
ND = 8


def block_kernel(
    tok_hbm, shift_hbm, scale_hbm, w_hbm, bias_hbm, act_hbm,
    token_hbm, weight_hbm, sums_hbm, shift_out, scale_out,
    tok, shift, scale, bias, n, cb, w, g, gt, sb, share, zs, zr, xr, keep, stats,
    xw, bsum, brec, term, trec, weight_grad, shift_grad, scale_grad,
    in_sem, out_sem, wo_sem, own_sem, n_send, n_recv, c_send, c_recv, f_send, f_recv,
    y_send, y_recv, s_send, s_recv, zw_send, zw_recv, z_send, z_recv, l_send, l_recv, x_send, x_recv,
    b_send, b_recv, t_send, t_recv,
):
    y, h, z, l, c = place()
    sib = peer(dc=1)
    pair = peer(dl=1)
    ring = {d: peer(dz=d) for d in (1, 2, 3)}
    group = {d: peer(dy=d) for d in (1, 2, 3)}
    cross = peer(dh=1)
    fc, dc = 1024 // NF, 8192 // ND

    loads = [
        pltpu.make_async_copy(src, dst, in_sem.at[k])
        for k, (src, dst) in enumerate(
            ((tok_hbm, tok), (shift_hbm, shift), (scale_hbm, scale), (bias_hbm, bias), (w_hbm, w))
        )
    ]
    for cc in (0, 1):
        for zz in range(4):
            for ll in (0, 1):
                r = (lax.rem(z + zz, 4) * 4 + lax.rem(l + ll, 2) * 2 + lax.rem(c + cc, 2)) * 32
                src = act_hbm.at[pl.ds(pl.multiple_of(r, 32), 32)]
                loads.append(pltpu.make_async_copy(src, g.at[rows(cc, zz, ll)], in_sem.at[len(loads)]))
    for cp in loads:
        cp.start()
    peers = [sib, pair, *ring.values(), *group.values(), cross]
    barrier = pltpu.get_barrier_semaphore()
    for p in peers:
        pl.semaphore_signal(barrier, inc=1, device_id=p, device_id_type=MESH)
    for cp in loads[:3]:
        cp.wait()

    def of_image(ref, t):
        m = ref[:, t].astype(F32)
        return jnp.where((z < 2).astype(F32) > 0.5, m[0:1], m[1:2])

    def row_total(f):
        def body(j, acc):
            return acc + lane_sums(f(tok[:, cols(j, dc)].astype(F32)))

        acc = lax.fori_loop(0, ND, body, jnp.zeros((32, 128), F32))
        return jnp.sum(acc, axis=-1, keepdims=True) * (1.0 / 8192)

    average = row_total(lambda v: v)
    inverse = lax.rsqrt(row_total(lambda v: (v - average) * (v - average)) + 1e-06)
    stats[0] = wide(average)
    stats[1] = wide(inverse)
    stats[2] = jnp.zeros((32, 128), F32)
    stats[3] = jnp.zeros((32, 128), F32)

    def xhat(t):
        return (tok[:, t].astype(F32) - stats[0, :, 0:1]) * stats[1, :, 0:1]

    @pl.loop(0, ND)
    def _(j):
        t = cols(j, dc)
        n[rows(0, 0, 0), t] = (xhat(t) * (1.0 + of_image(scale, t)) + of_image(shift, t)).astype(BF16)

    pl.semaphore_wait(barrier, len(peers))

    pending = []

    def half_rows(s, half):
        return n.at[pl.ds(slot(*s) * 32 + half * 16, 16)]

    def send(src, dst, to, halves=(0, 1)):
        for half in halves:
            sem = n_recv.at[slot(*dst) * 2 + half]
            cp = remote(half_rows(src, half), half_rows(dst, half), n_send.at[len(pending)], sem, to)
            cp.start()
            pending.append(cp)

    def span(piece, part):
        k = piece[0] * 2 + piece[1]
        if part == "whole":
            return 0, 2048, k
        if part == "first":
            return (1 - h) * 1024, 1024, k
        return h * 1024, 1024, 8 + LATE.index(piece)

    def place_of(s, cc, piece, part):
        start, width, _ = span(piece, part)
        r = pl.ds(s * 512 + slot(cc, *piece) * 32, 32)
        return cb.at[r, pl.ds(pl.multiple_of(start, 1024), width)]

    def columns_copy(d, piece, part):
        start, width, k = span(piece, part)
        start = lax.rem(y + d, 4) * 2048 + start
        src = n.at[rows(0, *piece), pl.ds(pl.multiple_of(start, 1024), width)]
        dst = place_of(4 - d, 0, piece, part)
        return remote(src, dst, c_send.at[d - 1, k], c_recv.at[3 - d, k], group[d])

    sent = []

    def exchange(piece, part):
        for d in (2, 1, 3):
            cp = columns_copy(d, piece, part)
            cp.start()
            if part != "second":
                sent.append(cp)

    moved = []

    def pass_on(pieces, part):
        now = []
        for piece in pieces:
            k = span(piece, part)[2]
            for s in (1, 2, 3):
                src = place_of(s, 0, piece, part)
                landed(src, c_recv.at[s - 1, k])
                cp = remote(
                    src, place_of(s, 1, piece, part), f_send.at[s - 1, k], f_recv.at[s - 1, k], sib
                )
                cp.start()
                now.append(cp)
        moved.extend(now)
        return now

    def y_copy(d, q):
        r = cols(q, fc)
        return remote(
            gt.at[r, pl.ds(0, 512)],
            gt.at[r, pl.ds((4 - d) * 512, 512)],
            y_send.at[d // 2, q],
            y_recv.at[3 - d, q],
            group[d],
        )

    def y_relay(d, q):
        half = d // 2
        r = pl.ds(pl.multiple_of(q * fc + half * (fc // 2), fc // 2), fc // 2)
        return remote(
            gt.at[r, pl.ds((4 - d) * 512, 512)],
            gt.at[r, pl.ds(1024, 512)],
            y_send.at[2 + half, q],
            y_recv.at[1 if half == 0 else 3, q],
            group[d],
        )

    def y_start(q):
        for d in (1, 3):
            y_copy(d, q).start()

    def y_pass(q):
        for d in (1, 3):
            landed(gt.at[cols(q, fc), pl.ds((4 - d) * 512, 512)], y_recv.at[3 - d, q])
            y_relay(d, q).start()

    def arrived(s, halves=(0, 1)):
        for half in halves:
            landed(half_rows(s, half), n_recv.at[slot(*s) * 2 + half])

    def block(pieces, last=False):
        for piece in pieces:
            arrived((1, *piece))
        at = [rows(cc, *piece) for cc in (0, 1) for piece in pieces]

        @pl.loop(0, 2)
        def _(j):
            t = cols(j, 512)
            x = jnp.concatenate([n[r, :] for r in at], axis=0)
            pre = jnp.dot(x, w[:, t], preferred_element_type=F32) + bias[:, t].astype(F32)
            up = jnp.concatenate([g[r, t] for r in at], axis=0).astype(F32)
            sq = pre * pre
            th = jnp.tanh(GELU_A * pre * (1.0 + GELU_B * sq))
            slope = 0.5 * (1.0 + th) + 0.5 * GELU_A * pre * (1.0 - th * th) * (1.0 + 3.0 * GELU_B * sq)
            grad = (up * slope).astype(BF16)
            for k, r in enumerate(at):
                g[r, t] = grad[k * 32 : k * 32 + 32]
            if last:
                gt[t, 0:512] = g[:, t].T

                @pl.when(j == 0)
                def _():
                    y_start(0)
                    y_start(1)
                    y_start(2)

    def s_copy(b, j):
        k = j % 4
        return remote(sb.at[k], share.at[2 * j + b], s_send.at[k], s_recv.at[b, j], sib)

    def z_whole(zz):
        k = zz // 2
        there = zr.at[3 - zz, pl.ds(0, 32)]
        return remote(zs.at[rows(0, zz, 0)], there, zw_send.at[k], zw_recv.at[k], ring[zz])

    def z_near(zz, j):
        k, t = zz // 2, cols(j, dc)
        there = zr.at[3 - zz, pl.ds(32, 32), t]
        return remote(zs.at[rows(0, zz, 1), t], there, z_send.at[k, j], z_recv.at[k, j], ring[zz])

    def z_far(j):
        t = cols(j, dc)
        return remote(zs.at[pl.ds(128, 64), t], zr.at[1, :, t], z_send.at[2, j], z_recv.at[2, j], ring[2])

    def core_sum(b, j):
        t = cols(j, dc)
        landed(share.at[2 * j + b], s_recv.at[b, j])
        for k, piece in enumerate(HALVES[b]):
            theirs = share[2 * j + b, k * 32 : k * 32 + 32].astype(F32)
            zs[rows(0, *piece), t] = (zs[rows(0, *piece), t].astype(F32) + theirs).astype(BF16)
        if b == 1:
            z_near(3, j).start()
            z_near(1, j).start()
            z_far(j).start()

    def normed(b, low, high):
        at = [rows(cc, *piece) for cc in (0, 1) for piece in HALVES[b]]

        @pl.loop(low, high)
        def _(j):
            @pl.when(4 * b + j >= 4)
            def _():
                s_copy(b, j).wait_send()

            t = cols(j, dc)
            x = jnp.concatenate([g[r, :] for r in at], axis=0)
            p = lax.dot_general(x, w[t, :], (((1,), (1,)), ((), ())), preferred_element_type=F32)
            p = p.astype(BF16)
            for k, piece in enumerate(HALVES[b]):
                zs[rows(0, *piece), t] = p[k * 32 : k * 32 + 32]
            sb[j % 4] = p[128:256]
            s_copy(b, j).start()

            @pl.when(j >= 1)
            def _():
                core_sum(b, j - 1)

        if high == ND:
            core_sum(b, ND - 1)

    own, near_pair = (0, 0, 0), (0, 0, 1)
    send(own, (0, 3, 0), ring[1], (0,))
    send(own, (0, 1, 0), ring[3], (1,))
    send(own, (0, 0, 1), pair)
    send(own, (0, 3, 0), ring[1], (1,))
    send(own, (0, 1, 0), ring[3], (0,))
    send(own, (1, 0, 0), sib)
    exchange((0, 0), "whole")

    def ring_piece(ll):
        arrived((0, 3, ll), (0,))
        send((0, 3, ll), (0, 2, ll), ring[1], (0,))
        arrived((0, 1, ll), (1,))
        send((0, 1, ll), (0, 2, ll), ring[3], (1,))

    def ring_rest(ll, part):
        if ll == 0:
            arrived(near_pair, (1,))
            send(near_pair, (0, 1, 1), ring[3], (1,))
            send(near_pair, (0, 3, 1), ring[1], (1,))
            send(near_pair, (1, 0, 1), sib)
            exchange((0, 1), "whole")
        arrived((0, 3, ll), (1,))
        arrived((0, 1, ll), (0,))
        for zz in (3, 1):
            send((0, zz, ll), (1, zz, ll), sib)
            exchange((zz, ll), part)

    def opposite_piece(ll):
        arrived((0, 2, ll))
        send((0, 2, ll), (1, 2, ll), sib)
        exchange((2, ll), "first")

    arrived(near_pair, (0,))
    send(near_pair, (0, 3, 1), ring[1], (0,))
    send(near_pair, (0, 1, 1), ring[3], (0,))
    ring_piece(0)
    ring_rest(0, "whole")
    for cp in loads[3:]:
        cp.wait()
    block(BLOCKS[0])
    block(BLOCKS[1])
    ring_piece(1)
    normed(0, 0, ND)
    ring_rest(1, "first")
    opposite_piece(0)
    block(BLOCKS[2])
    opposite_piece(1)
    z_whole(3).start()
    z_whole(1).start()
    pass_on(SOON, "whole")
    block(BLOCKS[3], last=True)
    own_columns = pltpu.make_async_copy(n.at[:, cols(y, 2048)], cb.at[pl.ds(0, 512)], own_sem)
    own_columns.start()

    def part(q):
        return (16 + q) % 19

    def x_copy(q):
        return remote(share.at[part(q)], xw.at[q], x_send.at[q], x_recv.at[q], cross)

    def l_copy(j):
        return remote(zs.at[pl.ds(32, 32), cols(j, dc)], xr.at[:, cols(j, dc)], l_send.at[j], l_recv.at[j], pair)

    def weight_tile(q, column):
        t = pl.ds(pl.multiple_of(column, 1024), 1024)
        return jnp.dot(gt[cols(q, fc), :], cb[:, t], preferred_element_type=F32).astype(BF16)

    def weight_first(q):
        for half in (0, 1):
            r = pl.ds(pl.multiple_of(q * fc + half * (fc // 2), fc // 2), fc // 2)
            landed(gt.at[r, pl.ds(1024, 512)], y_recv.at[1 + 2 * half, q])

        share[part(q)] = weight_tile(q, (1 - h) * 1024)
        x_copy(q).start()

    def weight_second(q):
        share[NF + q] = weight_tile(q, h * 1024)

    def out_copy(q):
        k = lax.rem(q, 2)
        return pltpu.make_async_copy(weight_grad.at[k], weight_hbm.at[:, cols(q, fc)], wo_sem.at[k])

    def weight_sum(q):
        landed(xw.at[q], x_recv.at[q])

        @pl.when(q >= 2)
        def _():
            out_copy(q - 2).wait()

        weight_grad[lax.rem(q, 2)] = (share[NF + q].astype(F32) + xw[q].astype(F32)).T.astype(BF16)
        out_copy(q).start()

    def z_sum(j):
        t = cols(j, dc)
        landed(zr.at[1, :, t], z_recv.at[2, j])
        for zz in (1, 3):
            landed(zr.at[3 - zz, pl.ds(32, 32), t], z_recv.at[zz // 2, j])
        total = zs[0:64, t].astype(F32)
        for s in range(3):
            total += zr[s, :, t].astype(F32)
        keep[:, t] = total[0:32]
        zs[32:64, t] = total[32:64].astype(BF16)
        l_copy(j).start()

    def row_sum(j):
        t = cols(j, dc)
        landed(xr.at[:, t], l_recv.at[j])
        total = keep[:, t] + xr[:, t].astype(F32)
        keep[:, t] = total
        term[0, 0:1, t] = jnp.sum(total, axis=0, keepdims=True)
        hat = xhat(t)
        term[0, 1:2, t] = jnp.sum(total * hat, axis=0, keepdims=True)
        scaled = total * (1.0 + of_image(scale, t))
        stats[2] += lane_sums(scaled)
        stats[3] += lane_sums(scaled * hat)

    normed(1, 0, 4)
    y_pass(0)
    pass_on(LATE, "first")
    normed(1, 4, ND)
    y_pass(1)
    own_columns.wait()
    for cp in moved:
        cp.wait()

    def step(q):
        weight_first(q)

        @pl.when(q + 2 < NF)
        def _():
            y_pass(q + 2)

        @pl.when(q + 3 < NF)
        def _():
            y_start(q + 3)

    def rows_step(q):
        @pl.when(q == 3)
        def _():
            for zz in (1, 3):
                landed(zr.at[3 - zz, pl.ds(0, 32)], zw_recv.at[zz // 2])

        @pl.when((q >= 3) & (q <= 6))
        def _():
            z_sum(2 * q - 6)
            z_sum(2 * q - 5)

        @pl.when(q >= 4)
        def _():
            row_sum(2 * q - 8)
            row_sum(2 * q - 7)

    @pl.loop(0, 5)
    def _(q):
        step(q)
        for k, piece in enumerate(LATE):

            @pl.when(q == 1 + k)
            def _():
                exchange(piece, "second")

        rows_step(q)

    second = pass_on(LATE, "second")

    @pl.loop(5, NF)
    def _(q):
        step(q)

        @pl.when(q == 5)
        def _():
            for cp in second:
                cp.wait()

        for k in range(3):
            p = 3 * (q - 5) + k

            @pl.when(p < NF)
            def _():
                weight_second(p)

        rows_step(q)
        weight_sum(q - 5)


    near = (peer()[0], z + 1 - 2 * lax.rem(z, 2), peer()[2])
    hops = [
        remote(term.at[k], trec.at[k], t_send.at[k], t_recv.at[k], to)
        for k, to in enumerate((sib, pair, near, ring[2]))
    ]
    hops[0].start()
    nt = (((1,), (1,)), ((), ()))
    bsum[...] = lax.dot_general(jnp.ones((8, 2048), BF16), gt[...], nt, preferred_element_type=F32)
    b_copy = remote(bsum, brec, b_send.at[0], b_recv.at[0], cross)
    b_copy.start()
    hops[0].wait_recv()
    term[1] = term[0] + trec[0]
    hops[1].start()

    stats[2] = wide(jnp.sum(stats[2], axis=-1, keepdims=True) * (1.0 / 8192))
    stats[3] = wide(jnp.sum(stats[3], axis=-1, keepdims=True) * (1.0 / 8192))

    @pl.loop(0, ND)
    def _(j):
        t = cols(j, dc)
        mean_one, mean_two = stats[2, :, 0:1], stats[3, :, 0:1]
        scaled = keep[:, t] * (1.0 + of_image(scale, t))
        xr[:, t] = (stats[1, :, 0:1] * (scaled - mean_one - xhat(t) * mean_two)).astype(BF16)

    outs = [
        pltpu.make_async_copy(src, dst, out_sem.at[k])
        for k, (src, dst) in enumerate(
            ((xr, token_hbm), (brec, sums_hbm), (shift_grad, shift_out), (scale_grad, scale_out))
        )
    ]
    outs[0].start()

    for k in (1, 2):
        hops[k].wait_recv()
        term[k + 1] = term[k] + trec[k]
        hops[k + 1].start()
        weight_sum(2 + k)
    b_copy.wait()
    brec[...] = bsum[...] + brec[...]
    outs[1].start()
    hops[3].wait_recv()
    first = (z < 2).astype(F32) > 0.5
    near_sum, far_sum = term[3], trec[3]
    shift_grad[0:1, :] = jnp.where(first, near_sum[0:1], far_sum[0:1])
    shift_grad[1:2, :] = jnp.where(first, far_sum[0:1], near_sum[0:1])
    scale_grad[0:1, :] = jnp.where(first, near_sum[1:2], far_sum[1:2])
    scale_grad[1:2, :] = jnp.where(first, far_sum[1:2], near_sum[1:2])
    outs[2].start()
    outs[3].start()
    for q in (5, 6, 7):
        weight_sum(q)

    for k in range(4):
        hops[k].wait_send()
    for cp in pending + sent + [columns_copy(d, piece, "second") for piece in LATE for d in (1, 2, 3)]:
        cp.wait_send()
    for zz in (1, 3):
        z_whole(zz).wait_send()
    for j in range(4):
        s_copy(1, j).wait_send()

    @pl.loop(0, NF)
    def _(q):
        for d in (1, 3):
            y_copy(d, q).wait_send()
            y_relay(d, q).wait_send()
        z_far(q).wait_send()
        z_near(1, q).wait_send()
        z_near(3, q).wait_send()
        l_copy(q).wait_send()
        x_copy(q).wait_send()

    out_copy(NF - 2).wait()
    out_copy(NF - 1).wait()
    for cp in outs:
        cp.wait()


def result_kernel(a, b, c, d, e, ao, bo, co, do, eo, av, bv, cv, dv, ev, sem):
    held = (av, bv, cv, dv, ev)
    takes = [pltpu.make_async_copy(src, v, sem.at[k]) for k, (src, v) in enumerate(zip((a, b, c, d, e), held))]
    gives = [
        pltpu.make_async_copy(v, dst, sem.at[5 + k])
        for k, (v, dst) in enumerate(zip((av, bv, cv.at[0:1], dv, ev), (ao, bo, co, do, eo)))
    ]
    for cp in takes:
        cp.start()
    for cp, give in zip(takes, gives):
        cp.wait()
        give.start()
    for give in gives:
        give.wait()


def local(tokens, mod_shift, mod_scale, up_weight, up_bias, act_grad):
    vmem = pl.BlockSpec(memory_space=pltpu.VMEM)
    hbm = pl.BlockSpec(memory_space=pltpu.HBM)
    dma = pltpu.SemaphoreType.DMA
    results = (
        jax.ShapeDtypeStruct((32, 8192), BF16),
        jax.ShapeDtypeStruct((1024, 1024), BF16),
        jax.ShapeDtypeStruct((8, 1024), F32),
        jax.ShapeDtypeStruct((2, 8192), F32),
        jax.ShapeDtypeStruct((2, 8192), F32),
    )
    parts = pl.pallas_call(
        block_kernel,
        out_shape=results,
        in_specs=[hbm] * 6,
        out_specs=(hbm,) * 5,
        scratch_shapes=[
            pltpu.VMEM((32, 8192), BF16),
            pltpu.VMEM((2, 8192), BF16),
            pltpu.VMEM((2, 8192), BF16),
            pltpu.VMEM((1, 1024), BF16),
            pltpu.VMEM((512, 8192), BF16),
            pltpu.VMEM((2048, 2048), BF16),
            pltpu.VMEM((8192, 1024), BF16),
            pltpu.VMEM((512, 1024), BF16),
            pltpu.VMEM((1024, 2048), BF16),
            pltpu.VMEM((4, 128, 1024), BF16),
            pltpu.VMEM((19, 128, 1024), BF16),
            pltpu.VMEM((256, 8192), BF16),
            pltpu.VMEM((3, 64, 8192), BF16),
            pltpu.VMEM((32, 8192), BF16),
            pltpu.VMEM((32, 8192), F32),
            pltpu.VMEM((4, 32, 128), F32),
            pltpu.VMEM((NF, 128, 1024), BF16),
            pltpu.VMEM((8, 1024), F32),
            pltpu.VMEM((8, 1024), F32),
            pltpu.VMEM((4, 2, 8192), F32),
            pltpu.VMEM((4, 2, 8192), F32),
            pltpu.VMEM((2, 1024, 128), BF16),
            pltpu.VMEM((2, 8192), F32),
            pltpu.VMEM((2, 8192), F32),
            dma((21,)),
            dma((4,)),
            dma((2,)),
            dma(()),
            dma((32,)),
            dma((32,)),
            dma((3, 12)),
            dma((3, 12)),
            dma((3, 12)),
            dma((3, 12)),
            dma((4, NF)),
            dma((4, NF)),
            dma((4,)),
            dma((2, ND)),
            dma((2,)),
            dma((2,)),
            dma((3, ND)),
            dma((3, ND)),
            dma((ND,)),
            dma((ND,)),
            dma((NF,)),
            dma((NF,)),
            dma((1,)),
            dma((1,)),
            dma((4,)),
            dma((4,)),
        ],
        compiler_params=pltpu.CompilerParams(
            collective_id=0, has_side_effects=True, vmem_limit_bytes=61 * MIB
        ),
        name="block",
    )(tokens, mod_shift, mod_scale, up_weight, up_bias[None, :], act_grad)
    final = list(results)
    final[2] = jax.ShapeDtypeStruct((1, 1024), F32)
    token_grad, weight_grad, bias_grad, shift_grad, scale_grad = pl.pallas_call(
        result_kernel,
        out_shape=tuple(final),
        in_specs=[hbm] * 5,
        out_specs=(hbm,) * 5,
        scratch_shapes=[pltpu.VMEM(r.shape, r.dtype) for r in results] + [dma((10,))],
        compiler_params=pltpu.CompilerParams(vmem_limit_bytes=61 * MIB),
        name="results",
    )(*parts)
    return token_grad, weight_grad, bias_grad.reshape(1024), shift_grad, scale_grad


def solution(mesh):
    return jax.shard_map(
        local,
        mesh=mesh,
        in_specs=(
            P(("dp", "tx", "ty"), None),
            P("dp", None),
            P("dp", None),
            P(None, ("tx", "ty")),
            P(("tx", "ty")),
            P("dp", ("tx", "ty")),
        ),
        out_specs=(
            P(("dp", "tx", "ty"), None),
            P("dp", ("tx", "ty")),
            P(("tx", "ty")),
            P("dp", None),
            P("dp", None),
        ),
        check_vma=False,
    )
```

```python
import jax
import jax.numpy as jnp
from jax import lax
from jax.experimental import pallas as pl
from jax.experimental.pallas import tpu as pltpu
from jax.sharding import PartitionSpec as P

MESH = pl.DeviceIdType.MESH
MIB = 1 << 20
F32 = jnp.float32
BF16 = jnp.bfloat16
GELU_A = 0.7978845608028654
GELU_B = 0.044715


def place():
    dp, tx, ty = (lax.axis_index(a) for a in ("dp", "tx", "ty"))
    return dp // 2, dp % 2, tx, ty // 2, ty % 2


def peer(dy=0, dh=0, dz=0, dl=0, dc=0):
    y, h, z, l, c = place()
    return (
        lax.rem(y + dy, 4) * 2 + lax.rem(h + dh, 2),
        lax.rem(z + dz, 4),
        lax.rem(l + dl, 2) * 2 + lax.rem(c + dc, 2),
    )


def remote(src, dst, send, recv, to):
    return pltpu.make_async_remote_copy(
        src_ref=src, dst_ref=dst, send_sem=send, recv_sem=recv, device_id=to, device_id_type=MESH
    )


def landed(ref, sem):
    pltpu.make_async_copy(ref, ref, sem).wait()


def cols(i, n):
    return pl.ds(pl.multiple_of(i * n, n), n)


def lane_sums(x):
    parts = [x[:, k : k + 128] for k in range(0, x.shape[1], 128)]
    while len(parts) > 1:
        parts = [a + b for a, b in zip(parts[::2], parts[1::2])]
    return parts[0]


def wide(x):
    return jnp.broadcast_to(x, (32, 128))


def slot(c, z, l):
    return c * 8 + z * 2 + l


def rows(c, z, l):
    return pl.ds(slot(c, z, l) * 32, 32)


SOON = ((0, 0), (0, 1), (3, 0), (1, 0))
LATE = ((3, 1), (1, 1), (2, 0), (2, 1))
BLOCKS = (((0, 0), (0, 1)), ((3, 0), (1, 0)), ((3, 1), (1, 1)), ((2, 0), (2, 1)))
HALVES = (BLOCKS[0] + BLOCKS[1], BLOCKS[2] + BLOCKS[3])
NF = 8
ND = 8


def block_kernel(
    tok_hbm, shift_hbm, scale_hbm, w_hbm, bias_hbm, act_hbm,
    token_hbm, weight_hbm, sums_hbm, shift_out, scale_out,
    tok, shift, scale, bias, n, cb, w, g, gt, sb, share, zs, zr, xr, keep, stats,
    xw, bsum, brec, term, trec, weight_grad, shift_grad, scale_grad,
    in_sem, out_sem, wo_sem, own_sem, n_send, n_recv, c_send, c_recv, f_send, f_recv,
    y_send, y_recv, s_send, s_recv, zw_send, zw_recv, z_send, z_recv, l_send, l_recv, x_send, x_recv,
    b_send, b_recv, t_send, t_recv,
):
    y, h, z, l, c = place()
    sib = peer(dc=1)
    pair = peer(dl=1)
    ring = {d: peer(dz=d) for d in (1, 2, 3)}
    group = {d: peer(dy=d) for d in (1, 2, 3)}
    cross = peer(dh=1)
    fc, dc = 1024 // NF, 8192 // ND

    loads = [
        pltpu.make_async_copy(src, dst, in_sem.at[k])
        for k, (src, dst) in enumerate(
            ((tok_hbm, tok), (shift_hbm, shift), (scale_hbm, scale), (bias_hbm, bias), (w_hbm, w))
        )
    ]
    for cc in (0, 1):
        for zz in range(4):
            for ll in (0, 1):
                r = (lax.rem(z + zz, 4) * 4 + lax.rem(l + ll, 2) * 2 + lax.rem(c + cc, 2)) * 32
                src = act_hbm.at[pl.ds(pl.multiple_of(r, 32), 32)]
                loads.append(pltpu.make_async_copy(src, g.at[rows(cc, zz, ll)], in_sem.at[len(loads)]))
    for cp in loads:
        cp.start()
    peers = [sib, pair, *ring.values(), *group.values(), cross]
    barrier = pltpu.get_barrier_semaphore()
    for p in peers:
        pl.semaphore_signal(barrier, inc=1, device_id=p, device_id_type=MESH)
    for cp in loads[:3]:
        cp.wait()

    def of_image(ref, t):
        m = ref[:, t].astype(F32)
        return jnp.where((z < 2).astype(F32) > 0.5, m[0:1], m[1:2])

    def row_total(f):
        def body(j, acc):
            return acc + lane_sums(f(tok[:, cols(j, dc)].astype(F32)))

        acc = lax.fori_loop(0, ND, body, jnp.zeros((32, 128), F32))
        return jnp.sum(acc, axis=-1, keepdims=True) * (1.0 / 8192)

    average = row_total(lambda v: v)
    inverse = lax.rsqrt(row_total(lambda v: (v - average) * (v - average)) + 1e-06)
    stats[0] = wide(average)
    stats[1] = wide(inverse)
    stats[2] = jnp.zeros((32, 128), F32)
    stats[3] = jnp.zeros((32, 128), F32)

    def xhat(t):
        return (tok[:, t].astype(F32) - stats[0, :, 0:1]) * stats[1, :, 0:1]

    @pl.loop(0, ND)
    def _(j):
        t = cols(j, dc)
        n[rows(0, 0, 0), t] = (xhat(t) * (1.0 + of_image(scale, t)) + of_image(shift, t)).astype(BF16)

    pl.semaphore_wait(barrier, len(peers))

    pending = []

    def half_rows(s, half):
        return n.at[pl.ds(slot(*s) * 32 + half * 16, 16)]

    def send(src, dst, to, halves=(0, 1)):
        for half in halves:
            sem = n_recv.at[slot(*dst) * 2 + half]
            cp = remote(half_rows(src, half), half_rows(dst, half), n_send.at[len(pending)], sem, to)
            cp.start()
            pending.append(cp)

    def span(piece, part):
        k = piece[0] * 2 + piece[1]
        if part == "whole":
            return 0, 2048, k
        if part == "first":
            return (1 - h) * 1024, 1024, k
        return h * 1024, 1024, 8 + LATE.index(piece)

    def place_of(s, cc, piece, part):
        start, width, _ = span(piece, part)
        r = pl.ds(s * 512 + slot(cc, *piece) * 32, 32)
        return cb.at[r, pl.ds(pl.multiple_of(start, 1024), width)]

    def columns_copy(d, piece, part):
        start, width, k = span(piece, part)
        start = lax.rem(y + d, 4) * 2048 + start
        src = n.at[rows(0, *piece), pl.ds(pl.multiple_of(start, 1024), width)]
        dst = place_of(4 - d, 0, piece, part)
        return remote(src, dst, c_send.at[d - 1, k], c_recv.at[3 - d, k], group[d])

    sent = []

    def exchange(piece, part):
        for d in (2, 1, 3):
            cp = columns_copy(d, piece, part)
            cp.start()
            if part != "second":
                sent.append(cp)

    moved = []

    def pass_on(pieces, part):
        now = []
        for piece in pieces:
            k = span(piece, part)[2]
            for s in (1, 2, 3):
                src = place_of(s, 0, piece, part)
                landed(src, c_recv.at[s - 1, k])
                cp = remote(
                    src, place_of(s, 1, piece, part), f_send.at[s - 1, k], f_recv.at[s - 1, k], sib
                )
                cp.start()
                now.append(cp)
        moved.extend(now)
        return now

    def y_copy(d, q):
        r = cols(q, fc)
        return remote(
            gt.at[r, pl.ds(0, 512)],
            gt.at[r, pl.ds((4 - d) * 512, 512)],
            y_send.at[d // 2, q],
            y_recv.at[3 - d, q],
            group[d],
        )

    def y_relay(d, q):
        half = d // 2
        r = pl.ds(pl.multiple_of(q * fc + half * (fc // 2), fc // 2), fc // 2)
        return remote(
            gt.at[r, pl.ds((4 - d) * 512, 512)],
            gt.at[r, pl.ds(1024, 512)],
            y_send.at[2 + half, q],
            y_recv.at[1 if half == 0 else 3, q],
            group[d],
        )

    def y_start(q):
        for d in (1, 3):
            y_copy(d, q).start()

    def y_pass(q):
        for d in (1, 3):
            landed(gt.at[cols(q, fc), pl.ds((4 - d) * 512, 512)], y_recv.at[3 - d, q])
            y_relay(d, q).start()

    def arrived(s, halves=(0, 1)):
        for half in halves:
            landed(half_rows(s, half), n_recv.at[slot(*s) * 2 + half])

    def block(pieces, last=False):
        for piece in pieces:
            arrived((1, *piece))
        at = [rows(cc, *piece) for cc in (0, 1) for piece in pieces]

        @pl.loop(0, 2)
        def _(j):
            t = cols(j, 512)
            x = jnp.concatenate([n[r, :] for r in at], axis=0)
            pre = jnp.dot(x, w[:, t], preferred_element_type=F32) + bias[:, t].astype(F32)
            up = jnp.concatenate([g[r, t] for r in at], axis=0).astype(F32)
            sq = pre * pre
            th = jnp.tanh(GELU_A * pre * (1.0 + GELU_B * sq))
            slope = 0.5 * (1.0 + th) + 0.5 * GELU_A * pre * (1.0 - th * th) * (1.0 + 3.0 * GELU_B * sq)
            grad = (up * slope).astype(BF16)
            for k, r in enumerate(at):
                g[r, t] = grad[k * 32 : k * 32 + 32]
            if last:
                gt[t, 0:512] = g[:, t].T

                @pl.when(j == 0)
                def _():
                    y_start(0)
                    y_start(1)
                    y_start(2)

    def s_copy(b, j):
        k = j % 4
        return remote(sb.at[k], share.at[2 * j + b], s_send.at[k], s_recv.at[b, j], sib)

    def z_whole(zz):
        k = zz // 2
        there = zr.at[3 - zz, pl.ds(0, 32)]
        return remote(zs.at[rows(0, zz, 0)], there, zw_send.at[k], zw_recv.at[k], ring[zz])

    def z_near(zz, j):
        k, t = zz // 2, cols(j, dc)
        there = zr.at[3 - zz, pl.ds(32, 32), t]
        return remote(zs.at[rows(0, zz, 1), t], there, z_send.at[k, j], z_recv.at[k, j], ring[zz])

    def z_far(j):
        t = cols(j, dc)
        return remote(zs.at[pl.ds(128, 64), t], zr.at[1, :, t], z_send.at[2, j], z_recv.at[2, j], ring[2])

    def core_sum(b, j):
        t = cols(j, dc)
        landed(share.at[2 * j + b], s_recv.at[b, j])
        for k, piece in enumerate(HALVES[b]):
            theirs = share[2 * j + b, k * 32 : k * 32 + 32].astype(F32)
            zs[rows(0, *piece), t] = (zs[rows(0, *piece), t].astype(F32) + theirs).astype(BF16)
        if b == 1:
            z_near(3, j).start()
            z_near(1, j).start()
            z_far(j).start()

    def normed(b, low, high):
        at = [rows(cc, *piece) for cc in (0, 1) for piece in HALVES[b]]

        @pl.loop(low, high)
        def _(j):
            @pl.when(4 * b + j >= 4)
            def _():
                s_copy(b, j).wait_send()

            t = cols(j, dc)
            x = jnp.concatenate([g[r, :] for r in at], axis=0)
            p = lax.dot_general(x, w[t, :], (((1,), (1,)), ((), ())), preferred_element_type=F32)
            p = p.astype(BF16)
            for k, piece in enumerate(HALVES[b]):
                zs[rows(0, *piece), t] = p[k * 32 : k * 32 + 32]
            sb[j % 4] = p[128:256]
            s_copy(b, j).start()

            @pl.when(j >= 1)
            def _():
                core_sum(b, j - 1)

        if high == ND:
            core_sum(b, ND - 1)

    own, near_pair = (0, 0, 0), (0, 0, 1)
    send(own, (0, 3, 0), ring[1], (0,))
    send(own, (0, 1, 0), ring[3], (1,))
    send(own, (0, 0, 1), pair)
    send(own, (0, 3, 0), ring[1], (1,))
    send(own, (0, 1, 0), ring[3], (0,))
    send(own, (1, 0, 0), sib)
    exchange((0, 0), "whole")

    def ring_piece(ll):
        arrived((0, 3, ll), (0,))
        send((0, 3, ll), (0, 2, ll), ring[1], (0,))
        arrived((0, 1, ll), (1,))
        send((0, 1, ll), (0, 2, ll), ring[3], (1,))

    def ring_rest(ll, part):
        if ll == 0:
            arrived(near_pair, (1,))
            send(near_pair, (0, 1, 1), ring[3], (1,))
            send(near_pair, (0, 3, 1), ring[1], (1,))
            send(near_pair, (1, 0, 1), sib)
            exchange((0, 1), "whole")
        arrived((0, 3, ll), (1,))
        arrived((0, 1, ll), (0,))
        for zz in (3, 1):
            send((0, zz, ll), (1, zz, ll), sib)
            exchange((zz, ll), part)

    def opposite_piece(ll):
        arrived((0, 2, ll))
        send((0, 2, ll), (1, 2, ll), sib)
        exchange((2, ll), "first")

    arrived(near_pair, (0,))
    send(near_pair, (0, 3, 1), ring[1], (0,))
    send(near_pair, (0, 1, 1), ring[3], (0,))
    ring_piece(0)
    ring_rest(0, "whole")
    for cp in loads[3:]:
        cp.wait()
    block(BLOCKS[0])
    block(BLOCKS[1])
    ring_piece(1)
    normed(0, 0, ND)
    ring_rest(1, "first")
    opposite_piece(0)
    block(BLOCKS[2])
    opposite_piece(1)
    z_whole(3).start()
    z_whole(1).start()
    pass_on(SOON, "whole")
    block(BLOCKS[3], last=True)
    own_columns = pltpu.make_async_copy(n.at[:, cols(y, 2048)], cb.at[pl.ds(0, 512)], own_sem)
    own_columns.start()

    def part(q):
        return (16 + q) % 19

    def x_copy(q):
        return remote(share.at[part(q)], xw.at[q], x_send.at[q], x_recv.at[q], cross)

    def l_copy(j):
        return remote(zs.at[pl.ds(32, 32), cols(j, dc)], xr.at[:, cols(j, dc)], l_send.at[j], l_recv.at[j], pair)

    def weight_tile(q, column):
        t = pl.ds(pl.multiple_of(column, 1024), 1024)
        return jnp.dot(gt[cols(q, fc), :], cb[:, t], preferred_element_type=F32).astype(BF16)

    def weight_first(q):
        for half in (0, 1):
            r = pl.ds(pl.multiple_of(q * fc + half * (fc // 2), fc // 2), fc // 2)
            landed(gt.at[r, pl.ds(1024, 512)], y_recv.at[1 + 2 * half, q])

        share[part(q)] = weight_tile(q, (1 - h) * 1024)
        x_copy(q).start()

    def weight_second(q):
        share[NF + q] = weight_tile(q, h * 1024)

    def out_copy(q):
        k = lax.rem(q, 2)
        return pltpu.make_async_copy(weight_grad.at[k], weight_hbm.at[:, cols(q, fc)], wo_sem.at[k])

    def weight_sum(q):
        landed(xw.at[q], x_recv.at[q])

        @pl.when(q >= 2)
        def _():
            out_copy(q - 2).wait()

        weight_grad[lax.rem(q, 2)] = (share[NF + q].astype(F32) + xw[q].astype(F32)).T.astype(BF16)
        out_copy(q).start()

    def z_sum(j):
        t = cols(j, dc)
        landed(zr.at[1, :, t], z_recv.at[2, j])
        for zz in (1, 3):
            landed(zr.at[3 - zz, pl.ds(32, 32), t], z_recv.at[zz // 2, j])
        total = zs[0:64, t].astype(F32)
        for s in range(3):
            total += zr[s, :, t].astype(F32)
        keep[:, t] = total[0:32]
        zs[32:64, t] = total[32:64].astype(BF16)
        l_copy(j).start()

    def row_sum(j):
        t = cols(j, dc)
        landed(xr.at[:, t], l_recv.at[j])
        total = keep[:, t] + xr[:, t].astype(F32)
        keep[:, t] = total
        term[0, 0:1, t] = jnp.sum(total, axis=0, keepdims=True)
        hat = xhat(t)
        term[0, 1:2, t] = jnp.sum(total * hat, axis=0, keepdims=True)
        scaled = total * (1.0 + of_image(scale, t))
        stats[2] += lane_sums(scaled)
        stats[3] += lane_sums(scaled * hat)

    normed(1, 0, 5)
    y_pass(0)
    pass_on(LATE, "first")
    y_pass(1)
    own_columns.wait()
    for cp in moved:
        cp.wait()

    def step(q):
        weight_first(q)

        @pl.when(q + 2 < NF)
        def _():
            y_pass(q + 2)

        @pl.when(q + 3 < NF)
        def _():
            y_start(q + 3)

    def rows_step(q):
        @pl.when(q == 0)
        def _():
            normed(1, 5, ND)

        @pl.when(q == 5)
        def _():
            for zz in (1, 3):
                landed(zr.at[3 - zz, pl.ds(0, 32)], zw_recv.at[zz // 2])

        for k in range(3):
            j = 3 * (q - 5) + k

            @pl.when((j >= 0) & (j < ND))
            def _():
                z_sum(j)

        for k in range(3):
            j = 3 * (q - 6) + k

            @pl.when(j >= 0)
            def _():
                row_sum(j)

    @pl.loop(0, 5)
    def _(q):
        step(q)
        for k, piece in enumerate(LATE):

            @pl.when(q == 1 + k)
            def _():
                exchange(piece, "second")

        rows_step(q)

    second = pass_on(LATE, "second")

    @pl.loop(5, NF)
    def _(q):
        step(q)

        @pl.when(q == 5)
        def _():
            for cp in second:
                cp.wait()

        for k in range(3):
            p = 3 * (q - 5) + k

            @pl.when(p < NF)
            def _():
                weight_second(p)

        rows_step(q)
        weight_sum(q - 5)


    row_sum(ND - 2)
    row_sum(ND - 1)
    near = (peer()[0], z + 1 - 2 * lax.rem(z, 2), peer()[2])
    hops = [
        remote(term.at[k], trec.at[k], t_send.at[k], t_recv.at[k], to)
        for k, to in enumerate((sib, pair, near, ring[2]))
    ]
    hops[0].start()
    nt = (((1,), (1,)), ((), ()))
    bsum[...] = lax.dot_general(jnp.ones((8, 2048), BF16), gt[...], nt, preferred_element_type=F32)
    b_copy = remote(bsum, brec, b_send.at[0], b_recv.at[0], cross)
    b_copy.start()
    hops[0].wait_recv()
    term[1] = term[0] + trec[0]
    hops[1].start()

    stats[2] = wide(jnp.sum(stats[2], axis=-1, keepdims=True) * (1.0 / 8192))
    stats[3] = wide(jnp.sum(stats[3], axis=-1, keepdims=True) * (1.0 / 8192))

    @pl.loop(0, ND)
    def _(j):
        t = cols(j, dc)
        mean_one, mean_two = stats[2, :, 0:1], stats[3, :, 0:1]
        scaled = keep[:, t] * (1.0 + of_image(scale, t))
        xr[:, t] = (stats[1, :, 0:1] * (scaled - mean_one - xhat(t) * mean_two)).astype(BF16)

    outs = [
        pltpu.make_async_copy(src, dst, out_sem.at[k])
        for k, (src, dst) in enumerate(
            ((xr, token_hbm), (brec, sums_hbm), (shift_grad, shift_out), (scale_grad, scale_out))
        )
    ]
    outs[0].start()

    for k in (1, 2):
        hops[k].wait_recv()
        term[k + 1] = term[k] + trec[k]
        hops[k + 1].start()
        weight_sum(2 + k)
    b_copy.wait()
    brec[...] = bsum[...] + brec[...]
    outs[1].start()
    hops[3].wait_recv()
    first = (z < 2).astype(F32) > 0.5
    near_sum, far_sum = term[3], trec[3]
    shift_grad[0:1, :] = jnp.where(first, near_sum[0:1], far_sum[0:1])
    shift_grad[1:2, :] = jnp.where(first, far_sum[0:1], near_sum[0:1])
    scale_grad[0:1, :] = jnp.where(first, near_sum[1:2], far_sum[1:2])
    scale_grad[1:2, :] = jnp.where(first, far_sum[1:2], near_sum[1:2])
    outs[2].start()
    outs[3].start()
    for q in (5, 6, 7):
        weight_sum(q)

    for k in range(4):
        hops[k].wait_send()
    for cp in pending + sent + [columns_copy(d, piece, "second") for piece in LATE for d in (1, 2, 3)]:
        cp.wait_send()
    for zz in (1, 3):
        z_whole(zz).wait_send()
    for j in range(4):
        s_copy(1, j).wait_send()

    @pl.loop(0, NF)
    def _(q):
        for d in (1, 3):
            y_copy(d, q).wait_send()
            y_relay(d, q).wait_send()
        z_far(q).wait_send()
        z_near(1, q).wait_send()
        z_near(3, q).wait_send()
        l_copy(q).wait_send()
        x_copy(q).wait_send()

    out_copy(NF - 2).wait()
    out_copy(NF - 1).wait()
    for cp in outs:
        cp.wait()


def result_kernel(a, b, c, d, e, ao, bo, co, do, eo, av, bv, cv, dv, ev, sem):
    held = (av, bv, cv, dv, ev)
    takes = [pltpu.make_async_copy(src, v, sem.at[k]) for k, (src, v) in enumerate(zip((a, b, c, d, e), held))]
    gives = [
        pltpu.make_async_copy(v, dst, sem.at[5 + k])
        for k, (v, dst) in enumerate(zip((av, bv, cv.at[0:1], dv, ev), (ao, bo, co, do, eo)))
    ]
    for cp in takes:
        cp.start()
    for cp, give in zip(takes, gives):
        cp.wait()
        give.start()
    for give in gives:
        give.wait()


def local(tokens, mod_shift, mod_scale, up_weight, up_bias, act_grad):
    vmem = pl.BlockSpec(memory_space=pltpu.VMEM)
    hbm = pl.BlockSpec(memory_space=pltpu.HBM)
    dma = pltpu.SemaphoreType.DMA
    results = (
        jax.ShapeDtypeStruct((32, 8192), BF16),
        jax.ShapeDtypeStruct((1024, 1024), BF16),
        jax.ShapeDtypeStruct((8, 1024), F32),
        jax.ShapeDtypeStruct((2, 8192), F32),
        jax.ShapeDtypeStruct((2, 8192), F32),
    )
    parts = pl.pallas_call(
        block_kernel,
        out_shape=results,
        in_specs=[hbm] * 6,
        out_specs=(hbm,) * 5,
        scratch_shapes=[
            pltpu.VMEM((32, 8192), BF16),
            pltpu.VMEM((2, 8192), BF16),
            pltpu.VMEM((2, 8192), BF16),
            pltpu.VMEM((1, 1024), BF16),
            pltpu.VMEM((512, 8192), BF16),
            pltpu.VMEM((2048, 2048), BF16),
            pltpu.VMEM((8192, 1024), BF16),
            pltpu.VMEM((512, 1024), BF16),
            pltpu.VMEM((1024, 2048), BF16),
            pltpu.VMEM((4, 128, 1024), BF16),
            pltpu.VMEM((19, 128, 1024), BF16),
            pltpu.VMEM((256, 8192), BF16),
            pltpu.VMEM((3, 64, 8192), BF16),
            pltpu.VMEM((32, 8192), BF16),
            pltpu.VMEM((32, 8192), F32),
            pltpu.VMEM((4, 32, 128), F32),
            pltpu.VMEM((NF, 128, 1024), BF16),
            pltpu.VMEM((8, 1024), F32),
            pltpu.VMEM((8, 1024), F32),
            pltpu.VMEM((4, 2, 8192), F32),
            pltpu.VMEM((4, 2, 8192), F32),
            pltpu.VMEM((2, 1024, 128), BF16),
            pltpu.VMEM((2, 8192), F32),
            pltpu.VMEM((2, 8192), F32),
            dma((21,)),
            dma((4,)),
            dma((2,)),
            dma(()),
            dma((32,)),
            dma((32,)),
            dma((3, 12)),
            dma((3, 12)),
            dma((3, 12)),
            dma((3, 12)),
            dma((4, NF)),
            dma((4, NF)),
            dma((4,)),
            dma((2, ND)),
            dma((2,)),
            dma((2,)),
            dma((3, ND)),
            dma((3, ND)),
            dma((ND,)),
            dma((ND,)),
            dma((NF,)),
            dma((NF,)),
            dma((1,)),
            dma((1,)),
            dma((4,)),
            dma((4,)),
        ],
        compiler_params=pltpu.CompilerParams(
            collective_id=0, has_side_effects=True, vmem_limit_bytes=61 * MIB
        ),
        name="block",
    )(tokens, mod_shift, mod_scale, up_weight, up_bias[None, :], act_grad)
    final = list(results)
    final[2] = jax.ShapeDtypeStruct((1, 1024), F32)
    token_grad, weight_grad, bias_grad, shift_grad, scale_grad = pl.pallas_call(
        result_kernel,
        out_shape=tuple(final),
        in_specs=[hbm] * 5,
        out_specs=(hbm,) * 5,
        scratch_shapes=[pltpu.VMEM(r.shape, r.dtype) for r in results] + [dma((10,))],
        compiler_params=pltpu.CompilerParams(vmem_limit_bytes=61 * MIB),
        name="results",
    )(*parts)
    return token_grad, weight_grad, bias_grad.reshape(1024), shift_grad, scale_grad


def solution(mesh):
    return jax.shard_map(
        local,
        mesh=mesh,
        in_specs=(
            P(("dp", "tx", "ty"), None),
            P("dp", None),
            P("dp", None),
            P(None, ("tx", "ty")),
            P(("tx", "ty")),
            P("dp", ("tx", "ty")),
        ),
        out_specs=(
            P(("dp", "tx", "ty"), None),
            P("dp", ("tx", "ty")),
            P(("tx", "ty")),
            P("dp", None),
            P("dp", None),
        ),
        check_vma=False,
    )
```

```python
import jax
import jax.numpy as jnp
from jax import lax
from jax.experimental import pallas as pl
from jax.experimental.pallas import tpu as pltpu
from jax.sharding import PartitionSpec as P

MESH = pl.DeviceIdType.MESH
MIB = 1 << 20
F32 = jnp.float32
BF16 = jnp.bfloat16
GELU_A = 0.7978845608028654
GELU_B = 0.044715


def place():
    dp, tx, ty = (lax.axis_index(a) for a in ("dp", "tx", "ty"))
    return dp // 2, dp % 2, tx, ty // 2, ty % 2


def peer(dy=0, dh=0, dz=0, dl=0, dc=0):
    y, h, z, l, c = place()
    return (
        lax.rem(y + dy, 4) * 2 + lax.rem(h + dh, 2),
        lax.rem(z + dz, 4),
        lax.rem(l + dl, 2) * 2 + lax.rem(c + dc, 2),
    )


def remote(src, dst, send, recv, to):
    return pltpu.make_async_remote_copy(
        src_ref=src, dst_ref=dst, send_sem=send, recv_sem=recv, device_id=to, device_id_type=MESH
    )


def landed(ref, sem):
    pltpu.make_async_copy(ref, ref, sem).wait()


def cols(i, n):
    return pl.ds(pl.multiple_of(i * n, n), n)


def lane_sums(x):
    parts = [x[:, k : k + 128] for k in range(0, x.shape[1], 128)]
    while len(parts) > 1:
        parts = [a + b for a, b in zip(parts[::2], parts[1::2])]
    return parts[0]


def wide(x):
    return jnp.broadcast_to(x, (32, 128))


def slot(c, z, l):
    return c * 8 + z * 2 + l


def rows(c, z, l):
    return pl.ds(slot(c, z, l) * 32, 32)


SOON = ((0, 0), (0, 1), (3, 0), (1, 0))
LATE = ((3, 1), (1, 1), (2, 0), (2, 1))
NF = 8
ND = 8
AHEAD = 4


def block_kernel(
    tok_hbm, shift_hbm, scale_hbm, w_hbm, bias_hbm, act_hbm,
    token_hbm, weight_hbm, sums_hbm, shift_out, scale_out,
    tok, shift, scale, bias, n, cb, w, g, gt, sb, share, zs, zr, xr, keep, stats,
    xw, bsum, brec, term, trec, weight_grad, shift_grad, scale_grad,
    in_sem, out_sem, wo_sem, own_sem, n_send, n_recv, c_send, c_recv, f_send, f_recv,
    y_send, y_recv, s_send, s_recv, z_send, z_recv, l_send, l_recv, x_send, x_recv,
    b_send, b_recv, t_send, t_recv,
):
    y, h, z, l, c = place()
    sib = peer(dc=1)
    pair = peer(dl=1)
    ring = {d: peer(dz=d) for d in (1, 2, 3)}
    group = {d: peer(dy=d) for d in (1, 2, 3)}
    cross = peer(dh=1)
    fc, dc = 1024 // NF, 8192 // ND

    loads = [
        pltpu.make_async_copy(src, dst, in_sem.at[k])
        for k, (src, dst) in enumerate(
            ((tok_hbm, tok), (shift_hbm, shift), (scale_hbm, scale), (bias_hbm, bias), (w_hbm, w))
        )
    ]
    for cc in (0, 1):
        for zz in range(4):
            for ll in (0, 1):
                r = (lax.rem(z + zz, 4) * 4 + lax.rem(l + ll, 2) * 2 + lax.rem(c + cc, 2)) * 32
                src = act_hbm.at[pl.ds(pl.multiple_of(r, 32), 32)]
                loads.append(pltpu.make_async_copy(src, g.at[rows(cc, zz, ll)], in_sem.at[len(loads)]))
    for cp in loads:
        cp.start()
    peers = [sib, pair, *ring.values(), *group.values(), cross]
    barrier = pltpu.get_barrier_semaphore()
    for p in peers:
        pl.semaphore_signal(barrier, inc=1, device_id=p, device_id_type=MESH)
    for cp in loads[:3]:
        cp.wait()

    def of_image(ref, t):
        m = ref[:, t].astype(F32)
        return jnp.where((z < 2).astype(F32) > 0.5, m[0:1], m[1:2])

    def row_total(f):
        def body(j, acc):
            return acc + lane_sums(f(tok[:, cols(j, dc)].astype(F32)))

        acc = lax.fori_loop(0, ND, body, jnp.zeros((32, 128), F32))
        return jnp.sum(acc, axis=-1, keepdims=True) * (1.0 / 8192)

    average = row_total(lambda v: v)
    inverse = lax.rsqrt(row_total(lambda v: (v - average) * (v - average)) + 1e-06)
    stats[0] = wide(average)
    stats[1] = wide(inverse)
    stats[2] = jnp.zeros((32, 128), F32)
    stats[3] = jnp.zeros((32, 128), F32)

    def xhat(t):
        return (tok[:, t].astype(F32) - stats[0, :, 0:1]) * stats[1, :, 0:1]

    @pl.loop(0, ND)
    def _(j):
        t = cols(j, dc)
        n[rows(0, 0, 0), t] = (xhat(t) * (1.0 + of_image(scale, t)) + of_image(shift, t)).astype(BF16)

    pl.semaphore_wait(barrier, len(peers))

    pending = []

    def half_rows(s, half):
        return n.at[pl.ds(slot(*s) * 32 + half * 16, 16)]

    def send(src, dst, to, halves=(0, 1)):
        for half in halves:
            sem = n_recv.at[slot(*dst) * 2 + half]
            cp = remote(half_rows(src, half), half_rows(dst, half), n_send.at[len(pending)], sem, to)
            cp.start()
            pending.append(cp)

    def span(piece, part):
        k = piece[0] * 2 + piece[1]
        if part == "whole":
            return 0, 2048, k
        if part == "first":
            return (1 - h) * 1024, 1024, k
        return h * 1024, 1024, 8 + LATE.index(piece)

    def place_of(s, cc, piece, part):
        start, width, _ = span(piece, part)
        r = pl.ds(s * 512 + slot(cc, *piece) * 32, 32)
        return cb.at[r, pl.ds(pl.multiple_of(start, 1024), width)]

    def columns_copy(d, piece, part):
        start, width, k = span(piece, part)
        start = lax.rem(y + d, 4) * 2048 + start
        src = n.at[rows(0, *piece), pl.ds(pl.multiple_of(start, 1024), width)]
        dst = place_of(4 - d, 0, piece, part)
        return remote(src, dst, c_send.at[d - 1, k], c_recv.at[3 - d, k], group[d])

    sent = []

    def exchange(piece, part):
        for d in (2, 1, 3):
            cp = columns_copy(d, piece, part)
            cp.start()
            if part != "second":
                sent.append(cp)

    moved = []

    def pass_on(pieces, part):
        now = []
        for piece in pieces:
            k = span(piece, part)[2]
            for s in (1, 2, 3):
                src = place_of(s, 0, piece, part)
                landed(src, c_recv.at[s - 1, k])
                cp = remote(
                    src, place_of(s, 1, piece, part), f_send.at[s - 1, k], f_recv.at[s - 1, k], sib
                )
                cp.start()
                now.append(cp)
        moved.extend(now)
        return now

    def y_copy(d, q):
        r = cols(q, fc)
        return remote(
            gt.at[r, pl.ds(0, 512)],
            gt.at[r, pl.ds((4 - d) * 512, 512)],
            y_send.at[d // 2, q],
            y_recv.at[3 - d, q],
            group[d],
        )

    def y_relay(d, q):
        half = d // 2
        r = pl.ds(pl.multiple_of(q * fc + half * (fc // 2), fc // 2), fc // 2)
        return remote(
            gt.at[r, pl.ds((4 - d) * 512, 512)],
            gt.at[r, pl.ds(1024, 512)],
            y_send.at[2 + half, q],
            y_recv.at[1 if half == 0 else 3, q],
            group[d],
        )

    def y_start(q):
        for d in (1, 3):
            y_copy(d, q).start()

    def y_pass(q):
        for d in (1, 3):
            landed(gt.at[cols(q, fc), pl.ds((4 - d) * 512, 512)], y_recv.at[3 - d, q])
            y_relay(d, q).start()

    def arrived(s, halves=(0, 1)):
        for half in halves:
            landed(half_rows(s, half), n_recv.at[slot(*s) * 2 + half])

    def block(pieces, last=False):
        for piece in pieces:
            arrived((1, *piece))
        at = [rows(cc, *piece) for cc in (0, 1) for piece in pieces]

        @pl.loop(0, 2)
        def _(j):
            t = cols(j, 512)
            x = jnp.concatenate([n[r, :] for r in at], axis=0)
            pre = jnp.dot(x, w[:, t], preferred_element_type=F32) + bias[:, t].astype(F32)
            up = jnp.concatenate([g[r, t] for r in at], axis=0).astype(F32)
            sq = pre * pre
            th = jnp.tanh(GELU_A * pre * (1.0 + GELU_B * sq))
            slope = 0.5 * (1.0 + th) + 0.5 * GELU_A * pre * (1.0 - th * th) * (1.0 + 3.0 * GELU_B * sq)
            grad = (up * slope).astype(BF16)
            for k, r in enumerate(at):
                g[r, t] = grad[k * 32 : k * 32 + 32]
            if last:
                gt[t, 0:512] = g[:, t].T

                @pl.when(j == 0)
                def _():
                    y_start(0)
                    y_start(1)
                    y_start(2)

    own, near_pair = (0, 0, 0), (0, 0, 1)
    send(own, (0, 3, 0), ring[1], (0,))
    send(own, (0, 1, 0), ring[3], (1,))
    send(own, (0, 0, 1), pair)
    send(own, (0, 3, 0), ring[1], (1,))
    send(own, (0, 1, 0), ring[3], (0,))
    send(own, (1, 0, 0), sib)
    exchange((0, 0), "whole")

    def ring_piece(ll, part):
        arrived((0, 3, ll), (0,))
        send((0, 3, ll), (0, 2, ll), ring[1], (0,))
        arrived((0, 1, ll), (1,))
        send((0, 1, ll), (0, 2, ll), ring[3], (1,))
        if ll == 0:
            arrived(near_pair, (1,))
            send(near_pair, (0, 1, 1), ring[3], (1,))
            send(near_pair, (0, 3, 1), ring[1], (1,))
            send(near_pair, (1, 0, 1), sib)
            exchange((0, 1), "whole")
        arrived((0, 3, ll), (1,))
        arrived((0, 1, ll), (0,))
        for zz in (3, 1):
            send((0, zz, ll), (1, zz, ll), sib)
            exchange((zz, ll), part)

    def opposite_piece(ll):
        arrived((0, 2, ll))
        send((0, 2, ll), (1, 2, ll), sib)
        exchange((2, ll), "first")

    arrived(near_pair, (0,))
    send(near_pair, (0, 3, 1), ring[1], (0,))
    send(near_pair, (0, 1, 1), ring[3], (0,))
    ring_piece(0, "whole")
    for cp in loads[3:]:
        cp.wait()
    block(((0, 0), (0, 1)))
    block(((3, 0), (1, 0)))
    ring_piece(1, "first")
    opposite_piece(0)
    block(((3, 1), (1, 1)))
    opposite_piece(1)
    pass_on(SOON, "whole")
    block(((2, 0), (2, 1)), last=True)
    own_columns = pltpu.make_async_copy(n.at[:, cols(y, 2048)], cb.at[pl.ds(0, 512)], own_sem)
    own_columns.start()

    def s_copy(j):
        k = lax.rem(j, 2)
        return remote(sb.at[k], share.at[pl.ds(2 * j, 2)], s_send.at[k], s_recv.at[j], sib)

    def z_copy(d, j):
        return remote(
            zs.at[pl.ds(d * 64, 64), cols(j, dc)],
            zr.at[3 - d, :, cols(j, dc)],
            z_send.at[d - 1, j],
            z_recv.at[3 - d, j],
            ring[d],
        )

    def core_sum(j):
        t = cols(j, dc)
        landed(share.at[pl.ds(2 * j, 2)], s_recv.at[j])
        theirs = share[pl.ds(2 * j, 2)].reshape(256, dc).astype(F32)
        zs[:, t] = (zs[:, t].astype(F32) + theirs).astype(BF16)
        for d in (2, 1, 3):
            z_copy(d, j).start()

    def normed_part(j):
        k = lax.rem(j, 2)

        @pl.when(j >= 2)
        def _():
            s_copy(j).wait_send()

        @pl.loop(0, dc // 512)
        def _(i):
            t = pl.ds(pl.multiple_of(j * dc + i * 512, 512), 512)
            p = lax.dot_general(g[...], w[t, :], (((1,), (1,)), ((), ())), preferred_element_type=F32)
            p = p.astype(BF16)
            zs[:, t] = p[0:256]
            sb[k, 0, :, cols(i, 512)] = p[256:384]
            sb[k, 1, :, cols(i, 512)] = p[384:512]

        s_copy(j).start()

        @pl.when(j >= 1)
        def _():
            core_sum(j - 1)

    def part(q):
        return (16 + q) % 19

    def x_copy(q):
        return remote(share.at[part(q)], xw.at[q], x_send.at[q], x_recv.at[q], cross)

    def l_copy(j):
        return remote(zs.at[pl.ds(32, 32), cols(j, dc)], xr.at[:, cols(j, dc)], l_send.at[j], l_recv.at[j], pair)

    def weight_tile(q, column):
        t = pl.ds(pl.multiple_of(column, 1024), 1024)
        return jnp.dot(gt[cols(q, fc), :], cb[:, t], preferred_element_type=F32).astype(BF16)

    def weight_first(q):
        for half in (0, 1):
            r = pl.ds(pl.multiple_of(q * fc + half * (fc // 2), fc // 2), fc // 2)
            landed(gt.at[r, pl.ds(1024, 512)], y_recv.at[1 + 2 * half, q])

        share[part(q)] = weight_tile(q, (1 - h) * 1024)
        @pl.when(q < NF - 1)
        def _():
            x_copy(q).start()

    def weight_second(q):
        share[NF + q] = weight_tile(q, h * 1024)

    def out_copy(q):
        k = lax.rem(q, 2)
        return pltpu.make_async_copy(weight_grad.at[k], weight_hbm.at[:, cols(q, fc)], wo_sem.at[k])

    def weight_sum(q):
        landed(xw.at[q], x_recv.at[q])

        @pl.when(q >= 2)
        def _():
            out_copy(q - 2).wait()

        weight_grad[lax.rem(q, 2)] = (share[NF + q].astype(F32) + xw[q].astype(F32)).T.astype(BF16)
        out_copy(q).start()

    def z_sum(j):
        t = cols(j, dc)
        for s in range(3):
            landed(zr.at[s, :, t], z_recv.at[s, j])
        total = zs[0:64, t].astype(F32)
        for s in range(3):
            total += zr[s, :, t].astype(F32)
        keep[:, t] = total[0:32]
        zs[32:64, t] = total[32:64].astype(BF16)
        l_copy(j).start()

    def row_sum(j):
        t = cols(j, dc)
        landed(xr.at[:, t], l_recv.at[j])
        total = keep[:, t] + xr[:, t].astype(F32)
        keep[:, t] = total
        term[0, 0:1, t] = jnp.sum(total, axis=0, keepdims=True)
        hat = xhat(t)
        term[0, 1:2, t] = jnp.sum(total * hat, axis=0, keepdims=True)
        scaled = total * (1.0 + of_image(scale, t))
        stats[2] += lane_sums(scaled)
        stats[3] += lane_sums(scaled * hat)

    pl.loop(0, AHEAD - 1)(normed_part)
    y_pass(0)
    pass_on(LATE, "first")
    y_pass(1)
    normed_part(AHEAD - 1)
    own_columns.wait()
    for cp in moved:
        cp.wait()

    def step(q):
        weight_first(q)

        @pl.when(q + 2 < NF)
        def _():
            y_pass(q + 2)

        @pl.when(q + 3 < NF)
        def _():
            y_start(q + 3)

        j = AHEAD + 2 * q

        @pl.when(j < ND)
        def _():
            normed_part(j)

        @pl.when(j + 1 < ND)
        def _():
            normed_part(j + 1)

        @pl.when(q == (ND - AHEAD + 1) // 2)
        def _():
            core_sum(ND - 1)

    def rows_step(q):
        @pl.when(q >= 1)
        def _():
            z_sum(q - 1)

        @pl.when(q >= 2)
        def _():
            row_sum(q - 2)

    @pl.loop(0, 5)
    def _(q):
        step(q)
        for k, piece in enumerate(LATE):

            @pl.when(q == 1 + k)
            def _():
                exchange(piece, "second")

        rows_step(q)

    second = pass_on(LATE, "second")

    @pl.loop(5, NF)
    def _(q):
        step(q)

        @pl.when(q == 5)
        def _():
            for cp in second:
                cp.wait()

        for k in range(3):
            p = 3 * (q - 5) + k

            @pl.when(p < NF)
            def _():
                weight_second(p)

        rows_step(q)
        weight_sum(q - 5)

    z_sum(ND - 1)
    x_copy(NF - 1).start()
    row_sum(ND - 2)
    row_sum(ND - 1)

    near = (peer()[0], z + 1 - 2 * lax.rem(z, 2), peer()[2])
    hops = [
        remote(term.at[k], trec.at[k], t_send.at[k], t_recv.at[k], to)
        for k, to in enumerate((sib, near, ring[2]))
    ]
    both = [
        remote(src, dst, t_send.at[k], t_recv.at[k], pair)
        for src, dst, k in ((term.at[2], trec.at[3], 3), (trec.at[2], term.at[3], 4))
    ]
    hops[0].start()
    nt = (((1,), (1,)), ((), ()))
    bsum[...] = lax.dot_general(jnp.ones((8, 2048), BF16), gt[...], nt, preferred_element_type=F32)
    b_copy = remote(bsum, brec, b_send.at[0], b_recv.at[0], cross)
    b_copy.start()
    hops[0].wait_recv()
    term[1] = term[0] + trec[0]
    hops[1].start()

    stats[2] = wide(jnp.sum(stats[2], axis=-1, keepdims=True) * (1.0 / 8192))
    stats[3] = wide(jnp.sum(stats[3], axis=-1, keepdims=True) * (1.0 / 8192))

    @pl.loop(0, ND)
    def _(j):
        t = cols(j, dc)
        mean_one, mean_two = stats[2, :, 0:1], stats[3, :, 0:1]
        scaled = keep[:, t] * (1.0 + of_image(scale, t))
        xr[:, t] = (stats[1, :, 0:1] * (scaled - mean_one - xhat(t) * mean_two)).astype(BF16)

    outs = [
        pltpu.make_async_copy(src, dst, out_sem.at[k])
        for k, (src, dst) in enumerate(
            ((xr, token_hbm), (brec, sums_hbm), (shift_grad, shift_out), (scale_grad, scale_out))
        )
    ]
    outs[0].start()

    hops[1].wait_recv()
    term[2] = term[1] + trec[1]
    hops[2].start()
    both[0].start()
    weight_sum(3)
    hops[2].wait_recv()
    both[1].start()
    weight_sum(4)
    b_copy.wait()
    brec[...] = bsum[...] + brec[...]
    outs[1].start()
    for cp in both:
        cp.wait_recv()
    first = (z < 2).astype(F32) > 0.5
    near_sum, far_sum = term[2] + trec[3], trec[2] + term[3]
    shift_grad[0:1, :] = jnp.where(first, near_sum[0:1], far_sum[0:1])
    shift_grad[1:2, :] = jnp.where(first, far_sum[0:1], near_sum[0:1])
    scale_grad[0:1, :] = jnp.where(first, near_sum[1:2], far_sum[1:2])
    scale_grad[1:2, :] = jnp.where(first, far_sum[1:2], near_sum[1:2])
    outs[2].start()
    outs[3].start()
    for q in (5, 6, 7):
        weight_sum(q)

    for cp in hops + both:
        cp.wait_send()
    for cp in pending + sent + [columns_copy(d, piece, "second") for piece in LATE for d in (1, 2, 3)]:
        cp.wait_send()
    s_copy(0).wait_send()
    s_copy(1).wait_send()

    @pl.loop(0, NF)
    def _(q):
        for d in (1, 3):
            y_copy(d, q).wait_send()
            y_relay(d, q).wait_send()
        for d in (1, 2, 3):
            z_copy(d, q).wait_send()
        l_copy(q).wait_send()
        x_copy(q).wait_send()

    out_copy(NF - 2).wait()
    out_copy(NF - 1).wait()
    for cp in outs:
        cp.wait()


def result_kernel(a, b, c, d, e, ao, bo, co, do, eo, av, bv, cv, dv, ev, sem):
    held = (av, bv, cv, dv, ev)
    takes = [pltpu.make_async_copy(src, v, sem.at[k]) for k, (src, v) in enumerate(zip((a, b, c, d, e), held))]
    gives = [
        pltpu.make_async_copy(v, dst, sem.at[5 + k])
        for k, (v, dst) in enumerate(zip((av, bv, cv.at[0:1], dv, ev), (ao, bo, co, do, eo)))
    ]
    for cp in takes:
        cp.start()
    for cp, give in zip(takes, gives):
        cp.wait()
        give.start()
    for give in gives:
        give.wait()


def local(tokens, mod_shift, mod_scale, up_weight, up_bias, act_grad):
    vmem = pl.BlockSpec(memory_space=pltpu.VMEM)
    hbm = pl.BlockSpec(memory_space=pltpu.HBM)
    dma = pltpu.SemaphoreType.DMA
    results = (
        jax.ShapeDtypeStruct((32, 8192), BF16),
        jax.ShapeDtypeStruct((1024, 1024), BF16),
        jax.ShapeDtypeStruct((8, 1024), F32),
        jax.ShapeDtypeStruct((2, 8192), F32),
        jax.ShapeDtypeStruct((2, 8192), F32),
    )
    parts = pl.pallas_call(
        block_kernel,
        out_shape=results,
        in_specs=[hbm] * 6,
        out_specs=(hbm,) * 5,
        scratch_shapes=[
            pltpu.VMEM((32, 8192), BF16),
            pltpu.VMEM((2, 8192), BF16),
            pltpu.VMEM((2, 8192), BF16),
            pltpu.VMEM((1, 1024), BF16),
            pltpu.VMEM((512, 8192), BF16),
            pltpu.VMEM((2048, 2048), BF16),
            pltpu.VMEM((8192, 1024), BF16),
            pltpu.VMEM((512, 1024), BF16),
            pltpu.VMEM((1024, 2048), BF16),
            pltpu.VMEM((2, 2, 128, 1024), BF16),
            pltpu.VMEM((19, 128, 1024), BF16),
            pltpu.VMEM((256, 8192), BF16),
            pltpu.VMEM((3, 64, 8192), BF16),
            pltpu.VMEM((32, 8192), BF16),
            pltpu.VMEM((32, 8192), F32),
            pltpu.VMEM((4, 32, 128), F32),
            pltpu.VMEM((NF, 128, 1024), BF16),
            pltpu.VMEM((8, 1024), F32),
            pltpu.VMEM((8, 1024), F32),
            pltpu.VMEM((4, 2, 8192), F32),
            pltpu.VMEM((4, 2, 8192), F32),
            pltpu.VMEM((2, 1024, 128), BF16),
            pltpu.VMEM((2, 8192), F32),
            pltpu.VMEM((2, 8192), F32),
            dma((21,)),
            dma((4,)),
            dma((2,)),
            dma(()),
            dma((32,)),
            dma((32,)),
            dma((3, 12)),
            dma((3, 12)),
            dma((3, 12)),
            dma((3, 12)),
            dma((4, NF)),
            dma((4, NF)),
            dma((2,)),
            dma((ND,)),
            dma((3, ND)),
            dma((3, ND)),
            dma((ND,)),
            dma((ND,)),
            dma((NF,)),
            dma((NF,)),
            dma((1,)),
            dma((1,)),
            dma((5,)),
            dma((5,)),
        ],
        compiler_params=pltpu.CompilerParams(
            collective_id=0, has_side_effects=True, vmem_limit_bytes=61 * MIB
        ),
        name="block",
    )(tokens, mod_shift, mod_scale, up_weight, up_bias[None, :], act_grad)
    final = list(results)
    final[2] = jax.ShapeDtypeStruct((1, 1024), F32)
    token_grad, weight_grad, bias_grad, shift_grad, scale_grad = pl.pallas_call(
        result_kernel,
        out_shape=tuple(final),
        in_specs=[hbm] * 5,
        out_specs=(hbm,) * 5,
        scratch_shapes=[pltpu.VMEM(r.shape, r.dtype) for r in results] + [dma((10,))],
        compiler_params=pltpu.CompilerParams(vmem_limit_bytes=61 * MIB),
        name="results",
    )(*parts)
    return token_grad, weight_grad, bias_grad.reshape(1024), shift_grad, scale_grad


def solution(mesh):
    return jax.shard_map(
        local,
        mesh=mesh,
        in_specs=(
            P(("dp", "tx", "ty"), None),
            P("dp", None),
            P("dp", None),
            P(None, ("tx", "ty")),
            P(("tx", "ty")),
            P("dp", ("tx", "ty")),
        ),
        out_specs=(
            P(("dp", "tx", "ty"), None),
            P("dp", ("tx", "ty")),
            P(("tx", "ty")),
            P("dp", None),
            P("dp", None),
        ),
        check_vma=False,
    )
```
